128 devices in a mesh: samp: 4 (over y_hi, core), row: 32 (over y_lo, x, z).
Axes of the slice: x: 4, y: 4 (y_hi: 2, y_lo: 2; y = y_hi * 2 + y_lo), z: 4, core: 2. Of those that a mesh axis runs over, the one named last changes fastest.
Arguments:
- queries: bfloat16 [8, 2048, 768], P('samp', 'row'), may hold values from -6 to 6
- keys: bfloat16 [8, 2048, 768], P('samp', 'row'), may hold values from -6 to 6
- values: bfloat16 [8, 2048, 768], P('samp', 'row'), may hold values from -6 to 6
- out_grad: bfloat16 [8, 2048, 768], P('samp', 'row'), may hold values from -6 to 6
- pair_repr: bfloat16 [2048, 2048, 128], P('row', 'samp'), may hold values from -6 to 6
- norm_gain: float32 [128], replicated, may hold values from 0.25 to 1.75
- bias_weight: bfloat16 [128, 16], replicated, may hold values from -0.5 to 0.5
- token_mask: int32 [2048], replicated, may hold values 0 or 1
Outputs:
- grad_queries: bfloat16 [8, 2048, 768], P('samp', 'row')
- grad_keys: bfloat16 [8, 2048, 768], P('samp', 'row')
- grad_values: bfloat16 [8, 2048, 768], P('samp', 'row')
- grad_pair: bfloat16 [2048, 2048, 128], P('row', 'samp')
- grad_weight: float32 [128, 16], replicated
- grad_gain: float32 [128], replicated
The draws below stay inside these ranges and needn't reach their ends.
All inputs are finite; a program needn't handle non-finite values.
Results may differ from the reference program's by a relative error of at most 0.03.
Values may be sent and summed in bfloat16 or wider, within the bound.
A program may use at most 320 MiB of HBM per device.

```python
import math
import jax
import jax.numpy as jnp
from jax import lax

D = 768
HEADS = 16
PAIR_CH = 128
ROWS_DEV = 64
SAMP_DEV = 2
HEAD_DIM = 48
TOKENS = 2048
SAMPLES = 8
N_SAMP = 4
N_ROW = 32


def query_key_base(key):
    first_key, second_key = jax.random.split(key)
    shape = (SAMPLES, TOKENS, D)
    return (jax.random.normal(first_key, shape, jnp.float32), jax.random.normal(second_key, shape, jnp.float32))


def draw_queries(key, part):
    query_draw, key_draw = query_key_base(key)
    return jnp.clip(query_draw, -6.0, 6.0).astype(jnp.bfloat16)


def draw_keys(key, part):
    query_draw, key_draw = query_key_base(key)
    return jnp.clip(key_draw, -6.0, 6.0).astype(jnp.bfloat16)


def touch_ends(result, stream_key, smallest, top_value):
    longest = result.shape.index(max(result.shape))
    spots = []
    for shift in (0, 1):
        where = [jax.random.randint(jax.random.fold_in(stream_key, axis), (), 0, length) for axis, length in enumerate(result.shape)]
        where[longest] = (where[longest] + shift) % result.shape[longest]
        spots.append(tuple(where))
    return result.at[spots[0]].set(smallest).at[spots[1]].set(top_value)


def block_levels(stream_key, extent, cuts, smallest, high):
    gain, own = 1.0, jax.random.fold_in(stream_key, 6)
    for dim, shards_of in cuts:
        heights = jnp.exp(jax.random.uniform(jax.random.fold_in(own, dim), (shards_of,), jnp.float32, smallest / len(cuts), high / len(cuts)))
        gain = gain * jnp.repeat(heights, extent[dim] // shards_of).reshape([-1 if axis == dim else 1 for axis in range(len(extent))])
    return gain


def scatter_about(stream_key, extent, width, bound, cuts=(), kind=jnp.bfloat16):
    loudness = block_levels(stream_key, extent, cuts, -0.22, 0.18) if cuts else 1.0
    drawn = jax.random.normal(stream_key, extent, jnp.float32) * width * loudness
    return jnp.minimum(jnp.maximum(drawn, -bound), bound).astype(kind)


def setup_inputs(seed: int = 0) -> dict:
    key_of = jax.random.split(jax.random.key(seed), 9)
    queries = draw_queries(jax.random.fold_in(key_of[8], 71), 0)
    keys = draw_keys(jax.random.fold_in(key_of[8], 71), 0)
    values = scatter_about(key_of[2], (SAMPLES, TOKENS, D), 1.0, 6.0, ((0, 4), (1, 32)))
    out_grad = scatter_about(key_of[3], (SAMPLES, TOKENS, D), 1.0, 6.0, ((0, 4), (1, 32)))
    pair_repr = scatter_about(key_of[4], (TOKENS, TOKENS, PAIR_CH), 1.0, 6.0, ((0, 32), (1, 4)))
    norm_gain = jnp.clip(1.0 + 0.15 * jax.random.normal(key_of[5], (PAIR_CH,), jnp.float32), 0.25, 1.75)
    bias_weight = scatter_about(key_of[6], (PAIR_CH, HEADS), PAIR_CH ** -0.5, 0.5)
    token_mask = touch_ends((jax.random.randint(key_of[7], (TOKENS,), 0, 8) < 7).astype(jnp.int32), jax.random.fold_in(key_of[7], 1), 0, 1)
    return {"queries": queries, "keys": keys, "values": values, "out_grad": out_grad, "pair_repr": pair_repr, "norm_gain": norm_gain, "bias_weight": bias_weight, "token_mask": token_mask}


def layer_stats(pair_rows, norm_gain):
    entries = pair_rows.astype(jnp.float32)
    average = lax.optimization_barrier(jnp.mean(entries, -1, keepdims=True))
    centred = entries - average
    variance = lax.optimization_barrier(jnp.mean(centred * centred, -1, keepdims=True))
    inverse = lax.rsqrt(variance + 1e-05)
    standard = centred * inverse
    normed = (standard * norm_gain).astype(jnp.bfloat16)
    return (standard, inverse, normed)

def pair_back(standard, inverse, normed, grad_bias, norm_gain, weight_wide):
    bias_wide = grad_bias.astype(jnp.float32)
    grad_normed = jnp.einsum('hrj,ch->rjc', bias_wide, weight_wide)
    grad_weight = jnp.einsum('rjc,hrj->ch', normed.astype(jnp.float32), bias_wide)
    grad_gain = lax.optimization_barrier(jnp.sum(grad_normed * standard, (0, 1)))
    scaled = grad_normed * norm_gain
    grad_pair = inverse * (scaled - lax.optimization_barrier(jnp.mean(scaled, -1, keepdims=True)) - standard * lax.optimization_barrier(jnp.mean(scaled * standard, -1, keepdims=True)))
    return (grad_pair.astype(jnp.bfloat16), grad_weight, grad_gain)

def reference(queries, keys, values, out_grad, pair_repr, norm_gain, bias_weight, token_mask):
    inv_root = 1.0 / math.sqrt(HEAD_DIM)
    key_keep = token_mask > 0
    key_heads = keys.astype(jnp.float32).reshape(SAMPLES, TOKENS, HEADS, HEAD_DIM)
    value_heads = values.astype(jnp.float32).reshape(SAMPLES, TOKENS, HEADS, HEAD_DIM)
    weight_wide = bias_weight.astype(jnp.float32)

    def tile_step(carry, begin_row):
        key_total, value_total, weight_total, gain_total = carry
        query_tile = lax.dynamic_slice_in_dim(queries, begin_row, ROWS_DEV, 1).astype(jnp.float32)
        query_tile = query_tile.reshape(SAMPLES, ROWS_DEV, HEADS, HEAD_DIM)
        grad_tile = lax.dynamic_slice_in_dim(out_grad, begin_row, ROWS_DEV, 1).astype(jnp.float32)
        grad_tile = grad_tile.reshape(SAMPLES, ROWS_DEV, HEADS, HEAD_DIM)
        pair_tile = lax.dynamic_slice_in_dim(pair_repr, begin_row, ROWS_DEV, 0)
        standard, inverse, normed = layer_stats(pair_tile, norm_gain)
        pair_bias = jnp.einsum('rjc,ch->hrj', normed.astype(jnp.float32), weight_wide).astype(jnp.bfloat16)
        scores = jnp.einsum('srhe,sjhe->shrj', query_tile, key_heads) * inv_root
        scores = scores + pair_bias.astype(jnp.float32)[None]
        scores = jnp.where(key_keep[None, None, None, :], scores, -1000000000.0)
        row_top = lax.optimization_barrier(jnp.max(scores, -1, keepdims=True))
        raised = jnp.exp(scores - row_top)
        probs = raised / lax.optimization_barrier(jnp.sum(raised, -1, keepdims=True))
        probs_low = probs.astype(jnp.bfloat16)
        grad_prob = jnp.einsum('srhe,sjhe->shrj', grad_tile, value_heads)
        row_along = lax.optimization_barrier(jnp.sum(probs * grad_prob, -1, keepdims=True))
        grad_score = probs * (grad_prob - row_along)
        score_low = grad_score.astype(jnp.bfloat16)
        grad_query = jnp.einsum('shrj,sjhe->srhe', score_low.astype(jnp.float32), key_heads) * inv_root
        grad_query = grad_query.astype(jnp.bfloat16).reshape(SAMPLES, ROWS_DEV, D)
        key_part = (jnp.einsum('shrj,srhe->sjhe', score_low.astype(jnp.float32), query_tile) * inv_root).astype(jnp.bfloat16)
        key_part = lax.optimization_barrier(key_part)
        value_part = jnp.einsum('shrj,srhe->sjhe', probs_low.astype(jnp.float32), grad_tile).astype(jnp.bfloat16)
        value_part = lax.optimization_barrier(value_part)
        grouped = grad_score.reshape(N_SAMP, SAMP_DEV, HEADS, ROWS_DEV, TOKENS)
        group_low = lax.optimization_barrier(jnp.sum(grouped, 1)).astype(jnp.bfloat16)
        group_low = lax.optimization_barrier(group_low)
        grad_bias = lax.optimization_barrier(jnp.sum(group_low.astype(jnp.float32), 0)).astype(jnp.bfloat16)
        grad_pair, grad_weight, grad_gain = pair_back(standard, inverse, normed, grad_bias, norm_gain, weight_wide)
        key_total = key_total + key_part.astype(jnp.float32).reshape(SAMPLES, TOKENS, D)
        value_total = value_total + value_part.astype(jnp.float32).reshape(SAMPLES, TOKENS, D)
        carry = (key_total, value_total, weight_total + grad_weight, gain_total + grad_gain)
        return (carry, (grad_query, grad_pair))
    initial = (jnp.zeros((SAMPLES, TOKENS, D), jnp.float32), jnp.zeros((SAMPLES, TOKENS, D), jnp.float32), jnp.zeros((PAIR_CH, HEADS), jnp.float32), jnp.zeros((PAIR_CH,), jnp.float32))
    starts = jnp.arange(N_ROW, dtype=jnp.int32) * ROWS_DEV
    carry, (query_blocks, pair_blocks) = lax.scan(tile_step, initial, starts)
    key_total, value_total, weight_total, gain_total = carry
    grad_queries = query_blocks.transpose(1, 0, 2, 3).reshape(SAMPLES, TOKENS, D)
    grad_pair = pair_blocks.reshape(TOKENS, TOKENS, PAIR_CH)
    return (grad_queries, key_total.astype(jnp.bfloat16), value_total.astype(jnp.bfloat16), grad_pair, weight_total, gain_total)
```

```python
import functools
import math

import jax
import jax.numpy as jnp
from jax import lax
from jax.experimental import pallas as pl
from jax.experimental.pallas import tpu as pltpu
from jax.sharding import PartitionSpec as P

MESH = pl.DeviceIdType.MESH
F32 = jnp.float32
BF16 = jnp.bfloat16
LOG2E = math.log2(math.e)
MASKED = -1e9 * LOG2E
HEADS = 16
SIZE = 48
ANY = pl.BlockSpec(memory_space=pl.ANY)
WHOLE = pl.BlockSpec(memory_space=pltpu.VMEM)
MIB = 1024 * 1024


def shape(dims, dtype=BF16):
    return jax.ShapeDtypeStruct(dims, dtype)


def place():
    samp, row = lax.axis_index("samp"), lax.axis_index("row")
    return samp, row // HEADS, lax.rem(row, HEADS)


def remote(src, dst, send, recv, samp, half, head):
    return pltpu.make_async_remote_copy(
        src_ref=src,
        dst_ref=dst,
        send_sem=send,
        recv_sem=recv,
        device_id=(samp, half * HEADS + head),
        device_id_type=MESH,
    )


def greet(samp, half, head, plane, group):
    barrier = pltpu.get_barrier_semaphore()
    count = 0
    if plane:
        def signal(step, _):
            peer = lax.rem(head + step, HEADS)
            pl.semaphore_signal(
                barrier, inc=1, device_id=(samp, half * HEADS + peer), device_id_type=MESH
            )
            return 0

        lax.fori_loop(1, HEADS, signal, 0)
        count += HEADS - 1
    for apart in range(1, 8):
        if apart >= 4 and group < 7:
            break
        other = lax.rem(samp + apart, 4)
        side = half if apart < 4 else 1 - half
        pl.semaphore_signal(
            barrier, inc=1, device_id=(other, side * HEADS + head), device_id_type=MESH
        )
        count += 1
    pl.semaphore_wait(barrier, count)


def pack_kernel(q_ref, o_ref, k_ref, v_ref, out_ref):
    for part, ref in enumerate((q_ref, o_ref, k_ref, v_ref)):
        turned = ref[...].T
        for head in range(HEADS):
            out_ref[head, part * SIZE : (part + 1) * SIZE, :] = turned[
                head * SIZE : (head + 1) * SIZE
            ]


def normalise(entries):
    wide = entries.astype(F32)
    average = jnp.sum(wide, -1, keepdims=True) * (1.0 / 128)
    centred = wide - average
    variance = jnp.sum(centred * centred, -1, keepdims=True) * (1.0 / 128)
    inverse = lax.rsqrt(variance + 1e-05)
    return centred * inverse, inverse


def bias_kernel(pair_ref, gain_ref, spread_ref, bias_ref, normed_ref):
    gain = gain_ref[...]

    def each(i, _):
        lanes = pl.ds(pl.multiple_of(i * 128, 128), 128)
        for part in range(4):
            rows = pl.ds(part * 128, 128)
            standard, _ = normalise(pair_ref[i, rows, :])
            normed_ref[rows, lanes] = (standard * gain).astype(BF16)
        return 0

    lax.fori_loop(0, 16, each, 0)
    bias = jnp.dot(normed_ref[...], spread_ref[...], preferred_element_type=F32)
    bias_ref[...] = bias.T.reshape(HEADS, 16, 512).astype(BF16)


def spread_kernel(
    pack_ref, bias_ref, qo_ref, kv_ref, all_bias_ref, kv_near, out_sem, in_sem, own_sem, out2_sem, in2_sem
):
    samp, half, head = place()
    greet(samp, half, head, True, 7)
    chunk = pl.multiple_of(head * 64, 64)

    def copy_pack(step, which):
        peer = lax.rem(head + step, HEADS)
        land = kv_near if which else qo_ref.at[samp]
        return remote(
            pack_ref.at[peer, pl.ds(which * 96, 96)], land.at[head],
            out_sem.at[which, step], in_sem.at[which, step], samp, half, peer,
        )

    def copy_bias(step):
        peer = lax.rem(head + step, HEADS)
        return remote(
            bias_ref.at[peer], all_bias_ref.at[pl.ds(chunk, 64)],
            out_sem.at[2, step], in_sem.at[2, step], samp, half, peer,
        )

    def start_pack(step, _):
        copy_pack(step, 0).start()
        copy_pack(step, 1).start()
        return 0

    def start_bias(step, _):
        copy_bias(step).start()
        return 0

    def wait_pack(step, _):
        copy_pack(step, 0).wait()
        copy_pack(step, 1).wait()
        return 0

    def wait_bias(step, _):
        copy_bias(step).wait()
        return 0

    lax.fori_loop(1, HEADS, start_pack, 0)
    own = (
        pltpu.make_async_copy(pack_ref.at[head, pl.ds(0, 96)], qo_ref.at[samp, head], own_sem.at[0]),
        pltpu.make_async_copy(pack_ref.at[head, pl.ds(96, 96)], kv_near.at[head], own_sem.at[1]),
        pltpu.make_async_copy(bias_ref.at[head], all_bias_ref.at[pl.ds(chunk, 64)], own_sem.at[2]),
    )
    for copy in own:
        copy.start()
    lax.fori_loop(1, HEADS, start_bias, 0)
    lax.fori_loop(1, HEADS, wait_pack, 0)
    own[0].wait()
    own[1].wait()

    def send_qo(apart):
        return remote(
            qo_ref.at[samp], qo_ref.at[samp], out2_sem.at[apart], in2_sem.at[apart], lax.rem(samp + apart, 4), half, head
        )

    def send_kv(part, across):
        side = half if across == 0 else 1 - half
        return remote(
            kv_near.at[pl.ds(part * 8, 8)],
            kv_ref.at[samp],
            out2_sem.at[4 + part * 2 + across],
            in2_sem.at[4 + samp],
            2 * half + part,
            side,
            head,
        )

    def keep_kv(part):
        return pltpu.make_async_copy(kv_near.at[pl.ds(part * 8, 8)], kv_ref.at[samp], own_sem.at[3])

    for apart in (2, 3, 1):
        send_qo(apart).start()
    for part in range(2):
        send_kv(part, 1).start()
        mine = samp == 2 * half + part

        @pl.when(mine)
        def _():
            keep_kv(part).start()

        @pl.when(jnp.logical_not(mine))
        def _():
            send_kv(part, 0).start()

    source = samp // 2
    for other in range(4):
        @pl.when(jnp.logical_not((source == half) & (samp == other)))
        def _():
            pltpu.make_async_remote_copy(
                src_ref=kv_near.at[pl.ds(0, 8)],
                dst_ref=kv_ref.at[other],
                send_sem=out2_sem.at[4],
                recv_sem=in2_sem.at[4 + other],
                device_id=(other, source * HEADS + head),
                device_id_type=MESH,
            ).wait_recv()

    for part in range(2):
        send_kv(part, 1).wait_send()
        mine = samp == 2 * half + part

        @pl.when(mine)
        def _():
            keep_kv(part).wait()

        @pl.when(jnp.logical_not(mine))
        def _():
            send_kv(part, 0).wait_send()

    for apart in range(1, 4):
        send_qo(apart).wait_send()
        other = lax.rem(samp + 4 - apart, 4)
        pltpu.make_async_remote_copy(
            src_ref=qo_ref.at[other],
            dst_ref=qo_ref.at[other],
            send_sem=out2_sem.at[apart],
            recv_sem=in2_sem.at[apart],
            device_id=(other, half * HEADS + head),
            device_id_type=MESH,
        ).wait_recv()
    own[2].wait()
    lax.fori_loop(1, HEADS, wait_bias, 0)


def untangle(first, second):
    first, second = first.astype(F32), second.astype(F32)
    low = lax.broadcasted_iota(jnp.int32, first.shape, 1) < 64
    return (
        jnp.where(low, first, pltpu.roll(second, 64, 1)),
        jnp.where(low, pltpu.roll(first, 64, 1), second),
    )


def attend_kernel(
    qo_ref, kv_ref, bias_ref, keep_ref, dq_ref, dkv_ref, dbias_ref,
    raised_ref, along_ref, bias_t, dbias_t, qo_t, qo_rows, kv_t, kv_rows,
    probs_low, score_low, tops, stats, out_sem, in_sem,
):
    samp, half, head = place()
    greet(samp, half, head, False, 3)
    inv_root = 1.0 / math.sqrt(SIZE)

    def turn_bias(block, _):
        at = pl.ds(pl.multiple_of(block * 128, 128), 128)
        turned = bias_ref[at, :].astype(F32).T * LOG2E
        bias_t[:, at] = jnp.where(keep_ref[...] > 0, turned, MASKED)
        return 0

    lax.fori_loop(0, 8, turn_bias, 0)
    filler = jnp.zeros((32, 128), F32)

    def unpack(source, turned_ref, rows_ref, pairs):
        def body(index, _):
            owner, pair = index // pairs, lax.rem(index, pairs)
            at = pl.ds(pl.multiple_of(pair * 128, 128), 128)
            both = untangle(source[owner, 2 * pair], source[owner, 2 * pair + 1])
            for which in range(2):
                filled = jnp.concatenate([both[which], filler], 0)
                turned_ref[2 * owner + which, :, at] = filled.astype(BF16)
                rows_ref[2 * owner + which, at, :] = filled.T.astype(BF16)
            return 0

        lax.fori_loop(0, 4 * pairs, body, 0)

    unpack(qo_ref, qo_t, qo_rows, 8)
    unpack(kv_ref, kv_t, kv_rows, 4)

    def stat_copy(sample, apart):
        return remote(
            stats.at[samp, sample], stats.at[samp, sample],
            out_sem.at[sample, apart], in_sem.at[sample, apart],
            lax.rem(samp + apart, 4), half, head,
        )

    lane = lax.broadcasted_iota(jnp.int32, (128, 128), 1)

    def first_pass(sample, _):
        def block_body(block, _):
            at = pl.ds(pl.multiple_of(block * 256, 256), 256)
            right = qo_t[sample, :, at]
            partial = []
            for part in range(4):
                rows = pl.ds(part * 128, 128)
                kv = kv_rows[sample, rows, :]
                kept = jnp.where((lane < SIZE) & (keep_ref[rows, :] > 0), kv, 0).astype(BF16)
                vals = jnp.where(lane >= SIZE, kv, 0).astype(BF16)
                score = jnp.dot(kept, right, preferred_element_type=F32)
                score = score * (inv_root * LOG2E) + bias_t[rows, at]
                top = jnp.max(score, 0, keepdims=True)
                raised = jnp.exp2(score - top)
                along = jnp.dot(vals, right, preferred_element_type=F32)
                raised_ref[sample, rows, at] = raised
                along_ref[sample, rows, at] = along
                total = jnp.sum(raised, 0, keepdims=True)
                mixed = jnp.sum(raised * along, 0, keepdims=True)
                tops[sample, part : part + 1, at] = top
                partial.append((top, total, mixed))
            peak = functools.reduce(jnp.maximum, [p[0] for p in partial])
            scale = [jnp.exp2(p[0] - peak) for p in partial]
            stats[samp, sample, 0:1, at] = peak
            stats[samp, sample, 1:2, at] = sum(p[1] * w for p, w in zip(partial, scale))
            stats[samp, sample, 2:3, at] = sum(p[2] * w for p, w in zip(partial, scale))
            return 0

        lax.fori_loop(0, 4, block_body, 0)
        for apart in range(1, 4):
            stat_copy(sample, apart).start()
        return 0

    stats[samp] = jnp.zeros((8, 8, 1024), F32)
    lax.fori_loop(0, 8, first_pass, 0)
    dbias_t[...] = jnp.zeros((512, 1024), F32)

    def second_pass(sample, _):
        for apart in range(1, 4):
            stat_copy(sample, apart).wait_recv()

        def block_body(block, _):
            at = pl.ds(pl.multiple_of(block * 256, 256), 256)
            peaks = [stats[other, sample, 0:1, at] for other in range(4)]
            peak = functools.reduce(jnp.maximum, peaks)
            scale = [jnp.exp2(p - peak) for p in peaks]
            total = sum(stats[other, sample, 1:2, at] * scale[other] for other in range(4))
            mixed = sum(stats[other, sample, 2:3, at] * scale[other] for other in range(4))
            share = 1.0 / total
            mean = mixed * share
            for part in range(4):
                rows = pl.ds(part * 128, 128)
                factor = jnp.exp2(tops[sample, part : part + 1, at] - peak) * share
                probs = raised_ref[sample, rows, at] * factor
                grad = probs * (along_ref[sample, rows, at] - mean)
                dbias_t[rows, at] += grad
                probs_low[rows, at] = probs.astype(BF16)
                score_low[rows, at] = grad.astype(BF16)
            return 0

        lax.fori_loop(0, 4, block_body, 0)
        right = qo_rows[sample]
        dk = jnp.dot(score_low[...], right, preferred_element_type=F32)
        dv = jnp.dot(probs_low[...], right, preferred_element_type=F32)
        wide = lax.broadcasted_iota(jnp.int32, (512, 128), 1)
        both = jnp.where(wide < SIZE, dk * inv_root, dv).T
        dkv_ref[sample] = both[:96].astype(BF16)
        dq = jnp.dot(kv_t[sample, :SIZE, :], score_low[...], preferred_element_type=F32)
        dq_ref[sample] = (dq * inv_root).astype(BF16)
        return 0

    lax.fori_loop(0, 8, second_pass, 0)

    def turn_back(block, _):
        at = pl.ds(pl.multiple_of(block * 128, 128), 128)
        dbias_ref[at, :] = dbias_t[:, at].T.astype(BF16)
        return 0

    lax.fori_loop(0, 8, turn_back, 0)

    def sent(sample, _):
        for apart in range(1, 4):
            stat_copy(sample, apart).wait_send()
        return 0

    lax.fori_loop(0, 8, sent, 0)


def collect_kernel(
    dq_ref, dkv_ref, dbias_ref, own_bias, own_dq, own_dkv,
    dq_parts, dkv_parts, dq_sum, dkv_sum, out_sem, in_sem, own_sem, out2_sem, in2_sem,
):
    samp, half, head = place()
    greet(samp, half, head, True, 7)
    owner = samp // 2
    part = lax.rem(samp, 2)

    def send_dq(apart):
        other = lax.rem(samp + apart, 4)
        return remote(
            dq_ref.at[pl.ds(2 * other, 2)], dq_parts.at[apart], out2_sem.at[apart], in2_sem.at[apart], other, half, head
        )

    def send_dkv(other):
        return remote(
            dkv_ref.at[pl.ds(2 * other, 2)], dkv_parts.at[part, half],
            out2_sem.at[4 + other], in2_sem.at[4 + 2 * part + half], other, owner, head,
        )

    keep_dkv = pltpu.make_async_copy(dkv_ref.at[pl.ds(2 * samp, 2)], dkv_parts.at[part, half], own_sem.at[0])
    keep_dq = pltpu.make_async_copy(dq_ref.at[pl.ds(2 * samp, 2)], dq_parts.at[0], own_sem.at[1])
    keep_bias = pltpu.make_async_copy(
        dbias_ref.at[pl.ds(pl.multiple_of(head * 64, 64), 64)], own_bias.at[head], own_sem.at[2]
    )
    for apart in (2, 3, 1):
        send_dq(apart).start()
    for other in range(4):
        mine = (owner == half) & (samp == other)

        @pl.when(mine)
        def _():
            keep_dkv.start()

        @pl.when(jnp.logical_not(mine))
        def _():
            send_dkv(other).start()

    keep_dq.start()
    keep_bias.start()

    def send_bias(step):
        peer = lax.rem(head + step, HEADS)
        return remote(
            dbias_ref.at[pl.ds(pl.multiple_of(peer * 64, 64), 64)], own_bias.at[head],
            out_sem.at[0, step], in_sem.at[0, step], samp, half, peer,
        )

    def start_bias(step, _):
        send_bias(step).start()
        return 0

    lax.fori_loop(1, HEADS, start_bias, 0)

    keep_dq.wait()
    for apart in range(1, 4):
        send_dq(apart).wait()
    for block in range(8):
        at = pl.ds(block * 128, 128)
        total = sum(dq_parts[apart, :, :, at].astype(F32) for apart in range(4))
        dq_sum[block] = total.astype(BF16)

    for other in range(4):
        mine = (owner == half) & (samp == other)

        @pl.when(mine)
        def _():
            keep_dkv.wait()

        @pl.when(jnp.logical_not(mine))
        def _():
            send_dkv(other).wait_send()

    for piece in range(2):
        for side in range(2):
            from_samp = 2 * half + piece

            @pl.when(jnp.logical_not((from_samp == samp) & (side == half)))
            def _():
                pltpu.make_async_remote_copy(
                    src_ref=dkv_ref.at[pl.ds(0, 2)],
                    dst_ref=dkv_parts.at[piece, side],
                    send_sem=out2_sem.at[4],
                    recv_sem=in2_sem.at[4 + 2 * piece + side],
                    device_id=(from_samp, side * HEADS + head),
                    device_id_type=MESH,
                ).wait_recv()

    for block in range(8):
        at = pl.ds((block % 4) * 128, 128)
        total = dkv_parts[block // 4, 0, :, :, at].astype(F32) + dkv_parts[block // 4, 1, :, :, at].astype(F32)
        dkv_sum[block] = total.astype(BF16)

    def send_out(step):
        peer = lax.rem(head + step, HEADS)
        to = (samp, half, peer)
        return (
            remote(dq_sum.at[peer // 2], own_dq.at[head], out_sem.at[1, step], in_sem.at[1, step], *to),
            remote(dkv_sum.at[peer // 2], own_dkv.at[head], out_sem.at[2, step], in_sem.at[2, step], *to),
        )

    def start_out(step, _):
        for copy in send_out(step):
            copy.start()
        return 0

    lax.fori_loop(1, HEADS, start_out, 0)
    keep_q = pltpu.make_async_copy(dq_sum.at[head // 2], own_dq.at[head], own_sem.at[3])
    keep_kv = pltpu.make_async_copy(dkv_sum.at[head // 2], own_dkv.at[head], own_sem.at[4])
    keep_q.start()
    keep_kv.start()
    keep_q.wait()
    keep_kv.wait()
    keep_bias.wait()

    def finish(step, _):
        send_bias(step).wait()
        for copy in send_out(step):
            copy.wait()
        return 0

    lax.fori_loop(1, HEADS, finish, 0)


def unpack_kernel(dq_ref, dkv_ref, q_out, k_out, v_out):
    odd = lax.rem(lax.axis_index("row"), 2) == 1
    for which in range(2):
        for out, source in (
            (q_out, dq_ref[:, which]),
            (k_out, dkv_ref[:, which, :SIZE]),
            (v_out, dkv_ref[:, which, SIZE:]),
        ):
            turned = source.reshape(HEADS * SIZE, 128).astype(F32).T
            out[which] = jnp.where(odd, turned[64:], turned[:64]).astype(BF16)


def pair_kernel(pair_ref, dbias_ref, back_ref, out_ref, mixed_ref, turned_ref, wide_ref, scaled_ref, standard_ref):
    dbias = dbias_ref[...].reshape(256, 512).astype(F32)
    for part in range(4):
        wide_ref[part] = dbias[:, part * 128 : (part + 1) * 128]
    turned_ref[...] = dbias.T.astype(BF16)

    @pl.when(pl.program_id(0) == 0)
    def _():
        mixed_ref[...] = jnp.zeros_like(mixed_ref)

    def each(couple, _):
        scaled_ref[...] = jnp.dot(turned_ref[...], back_ref[couple], preferred_element_type=F32)
        for which in range(2):
            lanes = pl.ds(which * 128, 128)
            for part in range(4):
                rows = pl.ds(part * 128, 128)
                standard, inverse = normalise(pair_ref[2 * couple + which, rows, :])
                scaled = scaled_ref[rows, lanes]
                along = jnp.sum(scaled * standard, -1, keepdims=True) * (1.0 / 128)
                out_ref[2 * couple + which, rows, :] = (inverse * (scaled - standard * along)).astype(BF16)
                standard_ref[rows, lanes] = standard.astype(BF16)
        left = jnp.concatenate(
            [
                jnp.concatenate(
                    [wide_ref[part, pl.ds(2 * couple + which, 16, stride=16), :] for part in range(4)], 1
                )
                for which in range(2)
            ],
            0,
        )
        mixed_ref[...] += jnp.dot(left.astype(BF16), standard_ref[...], preferred_element_type=F32)
        return 0

    lax.fori_loop(0, 8, each, 0)


def on_device(queries, keys, values, out_grad, pair_repr, norm_gain, bias_weight, token_mask):
    samp = lax.axis_index("samp")
    flat = [array.reshape(128, 768) for array in (queries, out_grad, keys, values)]
    packed = pl.pallas_call(
        pack_kernel,
        out_shape=shape((HEADS, 4 * SIZE, 128)),
        in_specs=[WHOLE] * 4,
        out_specs=WHOLE,
    )(*flat)

    eye = jnp.eye(16, dtype=F32)
    weight = bias_weight.astype(F32)
    spread = (weight[None, :, :, None] * eye[:, None, None, :]).reshape(16 * 128, 256).astype(BF16)
    bias = pl.pallas_call(
        bias_kernel,
        grid=(4,),
        out_shape=shape((HEADS, 64, 512)),
        in_specs=[
            pl.BlockSpec((16, 512, 128), lambda i: (i, 0, 0)),
            pl.BlockSpec((1, 128), lambda i: (0, 0)),
            pl.BlockSpec((2048, 256), lambda i: (0, 0)),
        ],
        out_specs=pl.BlockSpec((HEADS, 16, 512), lambda i: (0, i, 0)),
        scratch_shapes=[pltpu.VMEM((512, 2048), BF16)],
        compiler_params=pltpu.CompilerParams(vmem_limit_bytes=32 * MIB),
    )(pair_repr, norm_gain.reshape(1, 128), spread)

    qo, kv, all_bias, _ = pl.pallas_call(
        spread_kernel,
        out_shape=(
            shape((4, 16, 96, 128)),
            shape((4, 8, 96, 128)),
            shape((1024, 512)),
            shape((16, 96, 128)),
        ),
        in_specs=[ANY] * 2,
        out_specs=[ANY] * 4,
        scratch_shapes=[
            pltpu.SemaphoreType.DMA((3, 16)),
            pltpu.SemaphoreType.DMA((3, 16)),
            pltpu.SemaphoreType.DMA((4,)),
            pltpu.SemaphoreType.DMA((8,)),
            pltpu.SemaphoreType.DMA((8,)),
        ],
        compiler_params=pltpu.CompilerParams(collective_id=0, has_side_effects=True),
    )(packed, bias)

    keep = lax.dynamic_slice_in_dim((token_mask > 0).astype(F32), samp * 512, 512)
    keep = jnp.broadcast_to(keep[:, None], (512, 128))
    dq, dkv, dbias = pl.pallas_call(
        attend_kernel,
        out_shape=(shape((8, SIZE, 1024)), shape((8, 96, 512)), shape((1024, 512))),
        in_specs=[WHOLE] * 4,
        out_specs=[WHOLE] * 3,
        scratch_shapes=[
            pltpu.VMEM((8, 512, 1024), F32),
            pltpu.VMEM((8, 512, 1024), F32),
            pltpu.VMEM((512, 1024), F32),
            pltpu.VMEM((512, 1024), F32),
            pltpu.VMEM((8, 128, 1024), BF16),
            pltpu.VMEM((8, 1024, 128), BF16),
            pltpu.VMEM((8, 128, 512), BF16),
            pltpu.VMEM((8, 512, 128), BF16),
            pltpu.VMEM((512, 1024), BF16),
            pltpu.VMEM((512, 1024), BF16),
            pltpu.VMEM((8, 8, 1024), F32),
            pltpu.VMEM((4, 8, 8, 1024), F32),
            pltpu.SemaphoreType.DMA((8, 4)),
            pltpu.SemaphoreType.DMA((8, 4)),
        ],
        compiler_params=pltpu.CompilerParams(
            collective_id=1, has_side_effects=True, vmem_limit_bytes=60 * MIB
        ),
    )(qo, kv, all_bias, keep)

    own_bias, own_dq, own_dkv = pl.pallas_call(
        collect_kernel,
        out_shape=(shape((HEADS, 64, 512)), shape((HEADS, 2, SIZE, 128)), shape((HEADS, 2, 96, 128))),
        in_specs=[ANY] * 3,
        out_specs=[ANY] * 3,
        scratch_shapes=[
            pltpu.VMEM((4, 2, SIZE, 1024), BF16),
            pltpu.VMEM((2, 2, 2, 96, 512), BF16),
            pltpu.VMEM((8, 2, SIZE, 128), BF16),
            pltpu.VMEM((8, 2, 96, 128), BF16),
            pltpu.SemaphoreType.DMA((3, 16)),
            pltpu.SemaphoreType.DMA((3, 16)),
            pltpu.SemaphoreType.DMA((5,)),
            pltpu.SemaphoreType.DMA((8,)),
            pltpu.SemaphoreType.DMA((8,)),
        ],
        compiler_params=pltpu.CompilerParams(
            collective_id=2, has_side_effects=True, vmem_limit_bytes=32 * MIB
        ),
    )(dq, dkv, dbias)

    grad_queries, grad_keys, grad_values = pl.pallas_call(
        unpack_kernel,
        out_shape=(shape((2, 64, 768)),) * 3,
        in_specs=[WHOLE] * 2,
        out_specs=[WHOLE] * 3,
    )(own_dq, own_dkv)

    scaled = weight * norm_gain[:, None]
    scaled = scaled - jnp.mean(scaled, 0, keepdims=True)
    picks = eye.reshape(8, 2, 16)
    back = jnp.einsum("ch,ktj->khjtc", scaled, picks).reshape(8, 256, 256).astype(BF16)
    grad_pair, mixed = pl.pallas_call(
        pair_kernel,
        grid=(4,),
        out_shape=(shape((64, 512, 128)), shape((32, 256), F32)),
        in_specs=[
            pl.BlockSpec((16, 512, 128), lambda i: (i, 0, 0)),
            pl.BlockSpec((HEADS, 16, 512), lambda i: (0, i, 0)),
            pl.BlockSpec((8, 256, 256), lambda i: (0, 0, 0)),
        ],
        out_specs=(
            pl.BlockSpec((16, 512, 128), lambda i: (i, 0, 0)),
            pl.BlockSpec((32, 256), lambda i: (0, 0)),
        ),
        scratch_shapes=[
            pltpu.VMEM((512, 256), BF16),
            pltpu.VMEM((4, 256, 128), F32),
            pltpu.VMEM((512, 256), F32),
            pltpu.VMEM((512, 256), BF16),
        ],
        compiler_params=pltpu.CompilerParams(vmem_limit_bytes=32 * MIB),
    )(pair_repr, own_bias, back)
    mixed = (mixed[:16, :128] + mixed[16:, 128:]).T
    mixed = lax.psum(mixed, ("samp", "row"))
    grad_weight = mixed * norm_gain[:, None]
    grad_gain = jnp.sum(mixed * weight, 1)
    return grad_queries, grad_keys, grad_values, grad_pair, grad_weight, grad_gain


def solution(mesh):
    tokens = P("samp", "row", None)
    pairs = P("row", "samp", None)
    return jax.shard_map(
        on_device,
        mesh=mesh,
        in_specs=(tokens, tokens, tokens, tokens, pairs, P(), P(), P()),
        out_specs=(tokens, tokens, tokens, pairs, P(), P()),
        check_vma=False,
    )
```

```python
import functools
import math

import jax
import jax.numpy as jnp
from jax import lax
from jax.experimental import pallas as pl
from jax.experimental.pallas import tpu as pltpu
from jax.sharding import PartitionSpec as P

MESH = pl.DeviceIdType.MESH
F32 = jnp.float32
BF16 = jnp.bfloat16
LOG2E = math.log2(math.e)
MASKED = -1e9 * LOG2E
HEADS = 16
SIZE = 48
ANY = pl.BlockSpec(memory_space=pl.ANY)
WHOLE = pl.BlockSpec(memory_space=pltpu.VMEM)
MIB = 1024 * 1024


def shape(dims, dtype=BF16):
    return jax.ShapeDtypeStruct(dims, dtype)


def place():
    samp, row = lax.axis_index("samp"), lax.axis_index("row")
    return samp, row // HEADS, lax.rem(row, HEADS)


def remote(src, dst, send, recv, samp, half, head):
    return pltpu.make_async_remote_copy(
        src_ref=src,
        dst_ref=dst,
        send_sem=send,
        recv_sem=recv,
        device_id=(samp, half * HEADS + head),
        device_id_type=MESH,
    )


def greet(samp, half, head, plane, group):
    barrier = pltpu.get_barrier_semaphore()
    count = 0
    if plane:
        def signal(step, _):
            peer = lax.rem(head + step, HEADS)
            pl.semaphore_signal(
                barrier, inc=1, device_id=(samp, half * HEADS + peer), device_id_type=MESH
            )
            return 0

        lax.fori_loop(1, HEADS, signal, 0)
        count += HEADS - 1
    for apart in range(1, 8):
        if apart >= 4 and group < 7:
            break
        other = lax.rem(samp + apart, 4)
        side = half if apart < 4 else 1 - half
        pl.semaphore_signal(
            barrier, inc=1, device_id=(other, side * HEADS + head), device_id_type=MESH
        )
        count += 1
    pl.semaphore_wait(barrier, count)


def pack_kernel(q_ref, o_ref, k_ref, v_ref, out_ref):
    for part, ref in enumerate((q_ref, o_ref, k_ref, v_ref)):
        turned = ref[...].T
        for head in range(HEADS):
            out_ref[head, part * SIZE : (part + 1) * SIZE, :] = turned[
                head * SIZE : (head + 1) * SIZE
            ]


def normalise(entries):
    wide = entries.astype(F32)
    average = jnp.sum(wide, -1, keepdims=True) * (1.0 / 128)
    centred = wide - average
    variance = jnp.sum(centred * centred, -1, keepdims=True) * (1.0 / 128)
    inverse = lax.rsqrt(variance + 1e-05)
    return centred * inverse, inverse


def bias_kernel(pair_ref, gain_ref, spread_ref, bias_ref, normed_ref):
    gain = gain_ref[...]

    def each(i, _):
        lanes = pl.ds(pl.multiple_of(i * 128, 128), 128)
        for part in range(4):
            rows = pl.ds(part * 128, 128)
            standard, _ = normalise(pair_ref[i, rows, :])
            normed_ref[rows, lanes] = (standard * gain).astype(BF16)
        return 0

    lax.fori_loop(0, 16, each, 0)
    bias = jnp.dot(normed_ref[...], spread_ref[...], preferred_element_type=F32)
    bias_ref[...] = bias.T.reshape(HEADS, 16, 512).astype(BF16)


def spread_kernel(
    pack_ref, bias_ref, qo_ref, kv_ref, all_bias_ref, kv_near, out_sem, in_sem, own_sem, out2_sem, in2_sem
):
    samp, half, head = place()
    greet(samp, half, head, True, 7)
    chunk = pl.multiple_of(head * 64, 64)

    def copy_pack(step, which):
        peer = lax.rem(head + step, HEADS)
        land = kv_near if which else qo_ref.at[samp]
        return remote(
            pack_ref.at[peer, pl.ds(which * 96, 96)], land.at[head],
            out_sem.at[which, step], in_sem.at[which, step], samp, half, peer,
        )

    def copy_bias(step):
        peer = lax.rem(head + step, HEADS)
        return remote(
            bias_ref.at[peer], all_bias_ref.at[pl.ds(chunk, 64)],
            out_sem.at[2, step], in_sem.at[2, step], samp, half, peer,
        )

    def start_pack(step, _):
        copy_pack(step, 0).start()
        copy_pack(step, 1).start()
        return 0

    def start_bias(step, _):
        copy_bias(step).start()
        return 0

    def wait_pack(step, _):
        copy_pack(step, 0).wait()
        copy_pack(step, 1).wait()
        return 0

    def wait_bias(step, _):
        copy_bias(step).wait()
        return 0

    lax.fori_loop(1, HEADS, start_pack, 0)
    own = (
        pltpu.make_async_copy(pack_ref.at[head, pl.ds(0, 96)], qo_ref.at[samp, head], own_sem.at[0]),
        pltpu.make_async_copy(pack_ref.at[head, pl.ds(96, 96)], kv_near.at[head], own_sem.at[1]),
        pltpu.make_async_copy(bias_ref.at[head], all_bias_ref.at[pl.ds(chunk, 64)], own_sem.at[2]),
    )
    for copy in own:
        copy.start()
    lax.fori_loop(1, HEADS, start_bias, 0)
    lax.fori_loop(1, HEADS, wait_pack, 0)
    own[0].wait()
    own[1].wait()

    def send_qo(apart):
        return remote(
            qo_ref.at[samp], qo_ref.at[samp], out2_sem.at[apart], in2_sem.at[apart], lax.rem(samp + apart, 4), half, head
        )

    def send_kv(part, across):
        side = half if across == 0 else 1 - half
        return remote(
            kv_near.at[pl.ds(part * 8, 8)],
            kv_ref.at[samp],
            out2_sem.at[4 + part * 2 + across],
            in2_sem.at[4 + samp],
            2 * half + part,
            side,
            head,
        )

    def keep_kv(part):
        return pltpu.make_async_copy(kv_near.at[pl.ds(part * 8, 8)], kv_ref.at[samp], own_sem.at[3])

    for apart in (2, 3, 1):
        send_qo(apart).start()
    for part in range(2):
        send_kv(part, 1).start()
        mine = samp == 2 * half + part

        @pl.when(mine)
        def _():
            keep_kv(part).start()

        @pl.when(jnp.logical_not(mine))
        def _():
            send_kv(part, 0).start()

    source = samp // 2
    for other in range(4):
        @pl.when(jnp.logical_not((source == half) & (samp == other)))
        def _():
            pltpu.make_async_remote_copy(
                src_ref=kv_near.at[pl.ds(0, 8)],
                dst_ref=kv_ref.at[other],
                send_sem=out2_sem.at[4],
                recv_sem=in2_sem.at[4 + other],
                device_id=(other, source * HEADS + head),
                device_id_type=MESH,
            ).wait_recv()

    for part in range(2):
        send_kv(part, 1).wait_send()
        mine = samp == 2 * half + part

        @pl.when(mine)
        def _():
            keep_kv(part).wait()

        @pl.when(jnp.logical_not(mine))
        def _():
            send_kv(part, 0).wait_send()

    for apart in range(1, 4):
        send_qo(apart).wait_send()
        other = lax.rem(samp + 4 - apart, 4)
        pltpu.make_async_remote_copy(
            src_ref=qo_ref.at[other],
            dst_ref=qo_ref.at[other],
            send_sem=out2_sem.at[apart],
            recv_sem=in2_sem.at[apart],
            device_id=(other, half * HEADS + head),
            device_id_type=MESH,
        ).wait_recv()
    own[2].wait()
    lax.fori_loop(1, HEADS, wait_bias, 0)


def untangle(first, second):
    first, second = first.astype(F32), second.astype(F32)
    low = lax.broadcasted_iota(jnp.int32, first.shape, 1) < 64
    return (
        jnp.where(low, first, pltpu.roll(second, 64, 1)),
        jnp.where(low, pltpu.roll(first, 64, 1), second),
    )


def attend_kernel(
    qo_ref, kv_ref, bias_ref, keep_ref, dq_ref, dkv_ref, dbias_ref,
    raised_ref, along_ref, bias_t, dbias_t, qo_t, qo_rows, kv_t, kv_rows,
    probs_low, score_low, tops, stats, out_sem, in_sem,
):
    samp, half, head = place()
    greet(samp, half, head, False, 3)
    inv_root = 1.0 / math.sqrt(SIZE)

    def turn_bias(block, _):
        at = pl.ds(pl.multiple_of(block * 128, 128), 128)
        turned = bias_ref[at, :].astype(F32).T * LOG2E
        bias_t[:, at] = jnp.where(keep_ref[...] > 0, turned, MASKED)
        return 0

    lax.fori_loop(0, 8, turn_bias, 0)
    filler = jnp.zeros((32, 128), F32)

    def unpack(source, turned_ref, rows_ref, pairs):
        def body(index, _):
            owner, pair = index // pairs, lax.rem(index, pairs)
            at = pl.ds(pl.multiple_of(pair * 128, 128), 128)
            both = untangle(source[owner, 2 * pair], source[owner, 2 * pair + 1])
            for which in range(2):
                filled = jnp.concatenate([both[which], filler], 0)
                turned_ref[2 * owner + which, :, at] = filled.astype(BF16)
                rows_ref[2 * owner + which, at, :] = filled.T.astype(BF16)
            return 0

        lax.fori_loop(0, 4 * pairs, body, 0)

    unpack(qo_ref, qo_t, qo_rows, 8)
    unpack(kv_ref, kv_t, kv_rows, 4)

    def stat_copy(sample, apart):
        return remote(
            stats.at[samp, sample], stats.at[samp, sample],
            out_sem.at[sample, apart], in_sem.at[sample, apart],
            lax.rem(samp + apart, 4), half, head,
        )

    lane = lax.broadcasted_iota(jnp.int32, (128, 128), 1)

    def first_pass(sample, _):
        def block_body(block, _):
            at = pl.ds(pl.multiple_of(block * 256, 256), 256)
            right = qo_t[sample, :, at]
            partial = []
            for part in range(4):
                rows = pl.ds(part * 128, 128)
                kv = kv_rows[sample, rows, :]
                kept = jnp.where((lane < SIZE) & (keep_ref[rows, :] > 0), kv, 0).astype(BF16)
                vals = jnp.where(lane >= SIZE, kv, 0).astype(BF16)
                score = jnp.dot(kept, right, preferred_element_type=F32)
                score = score * (inv_root * LOG2E) + bias_t[rows, at]
                top = jnp.max(score, 0, keepdims=True)
                raised = jnp.exp2(score - top)
                along = jnp.dot(vals, right, preferred_element_type=F32)
                raised_ref[sample, rows, at] = raised
                along_ref[sample, rows, at] = along
                total = jnp.sum(raised, 0, keepdims=True)
                mixed = jnp.sum(raised * along, 0, keepdims=True)
                tops[sample, part : part + 1, at] = top
                partial.append((top, total, mixed))
            peak = functools.reduce(jnp.maximum, [p[0] for p in partial])
            scale = [jnp.exp2(p[0] - peak) for p in partial]
            stats[samp, sample, 0:1, at] = peak
            stats[samp, sample, 1:2, at] = sum(p[1] * w for p, w in zip(partial, scale))
            stats[samp, sample, 2:3, at] = sum(p[2] * w for p, w in zip(partial, scale))
            return 0

        lax.fori_loop(0, 4, block_body, 0)
        for apart in range(1, 4):
            stat_copy(sample, apart).start()
        return 0

    stats[samp] = jnp.zeros((8, 8, 1024), F32)
    lax.fori_loop(0, 8, first_pass, 0)
    dbias_t[...] = jnp.zeros((512, 1024), F32)

    def second_pass(sample, _):
        for apart in range(1, 4):
            stat_copy(sample, apart).wait_recv()

        def block_body(block, _):
            at = pl.ds(pl.multiple_of(block * 256, 256), 256)
            peaks = [stats[other, sample, 0:1, at] for other in range(4)]
            peak = functools.reduce(jnp.maximum, peaks)
            scale = [jnp.exp2(p - peak) for p in peaks]
            total = sum(stats[other, sample, 1:2, at] * scale[other] for other in range(4))
            mixed = sum(stats[other, sample, 2:3, at] * scale[other] for other in range(4))
            share = 1.0 / total
            mean = mixed * share
            for part in range(4):
                rows = pl.ds(part * 128, 128)
                factor = jnp.exp2(tops[sample, part : part + 1, at] - peak) * share
                probs = raised_ref[sample, rows, at] * factor
                grad = probs * (along_ref[sample, rows, at] - mean)
                dbias_t[rows, at] += grad
                probs_low[rows, at] = probs.astype(BF16)
                score_low[rows, at] = grad.astype(BF16)
            return 0

        lax.fori_loop(0, 4, block_body, 0)
        right = qo_rows[sample]
        dk = jnp.dot(score_low[...], right, preferred_element_type=F32)
        dv = jnp.dot(probs_low[...], right, preferred_element_type=F32)
        wide = lax.broadcasted_iota(jnp.int32, (512, 128), 1)
        both = jnp.where(wide < SIZE, dk * inv_root, dv).T
        dkv_ref[sample] = both[:96].astype(BF16)
        dq = jnp.dot(kv_t[sample, :SIZE, :], score_low[...], preferred_element_type=F32)
        dq_ref[sample] = (dq * inv_root).astype(BF16)
        return 0

    lax.fori_loop(0, 8, second_pass, 0)

    def turn_back(block, _):
        at = pl.ds(pl.multiple_of(block * 128, 128), 128)
        dbias_ref[at, :] = dbias_t[:, at].T.astype(BF16)
        return 0

    lax.fori_loop(0, 8, turn_back, 0)

    def sent(sample, _):
        for apart in range(1, 4):
            stat_copy(sample, apart).wait_send()
        return 0

    lax.fori_loop(0, 8, sent, 0)


def collect_kernel(
    dq_ref, dkv_ref, dbias_ref, own_bias, dq_sum, dkv_sum,
    dq_parts, dkv_parts, out_sem, in_sem, own_sem, out2_sem, in2_sem,
):
    samp, half, head = place()
    greet(samp, half, head, True, 7)
    owner = samp // 2
    part = lax.rem(samp, 2)

    def send_dq(apart):
        other = lax.rem(samp + apart, 4)
        return remote(
            dq_ref.at[pl.ds(2 * other, 2)], dq_parts.at[apart], out2_sem.at[apart], in2_sem.at[apart], other, half, head
        )

    def send_dkv(other):
        return remote(
            dkv_ref.at[pl.ds(2 * other, 2)], dkv_parts.at[part, half],
            out2_sem.at[4 + other], in2_sem.at[4 + 2 * part + half], other, owner, head,
        )

    keep_dkv = pltpu.make_async_copy(dkv_ref.at[pl.ds(2 * samp, 2)], dkv_parts.at[part, half], own_sem.at[0])
    keep_dq = pltpu.make_async_copy(dq_ref.at[pl.ds(2 * samp, 2)], dq_parts.at[0], own_sem.at[1])
    keep_bias = pltpu.make_async_copy(
        dbias_ref.at[pl.ds(pl.multiple_of(head * 64, 64), 64)], own_bias.at[head], own_sem.at[2]
    )
    for apart in (2, 3, 1):
        send_dq(apart).start()
    for other in range(4):
        mine = (owner == half) & (samp == other)

        @pl.when(mine)
        def _():
            keep_dkv.start()

        @pl.when(jnp.logical_not(mine))
        def _():
            send_dkv(other).start()

    keep_dq.start()
    keep_bias.start()

    def send_bias(step):
        peer = lax.rem(head + step, HEADS)
        return remote(
            dbias_ref.at[pl.ds(pl.multiple_of(peer * 64, 64), 64)], own_bias.at[head],
            out_sem.at[0, step], in_sem.at[0, step], samp, half, peer,
        )

    def start_bias(step, _):
        send_bias(step).start()
        return 0

    lax.fori_loop(1, HEADS, start_bias, 0)

    keep_dq.wait()
    for apart in range(1, 4):
        send_dq(apart).wait()
    for block in range(8):
        at = pl.ds(block * 128, 128)
        total = sum(dq_parts[apart, :, :, at].astype(F32) for apart in range(4))
        dq_sum[block] = total.astype(BF16)

    for other in range(4):
        mine = (owner == half) & (samp == other)

        @pl.when(mine)
        def _():
            keep_dkv.wait()

        @pl.when(jnp.logical_not(mine))
        def _():
            send_dkv(other).wait_send()

    for piece in range(2):
        for side in range(2):
            from_samp = 2 * half + piece

            @pl.when(jnp.logical_not((from_samp == samp) & (side == half)))
            def _():
                pltpu.make_async_remote_copy(
                    src_ref=dkv_ref.at[pl.ds(0, 2)],
                    dst_ref=dkv_parts.at[piece, side],
                    send_sem=out2_sem.at[4],
                    recv_sem=in2_sem.at[4 + 2 * piece + side],
                    device_id=(from_samp, side * HEADS + head),
                    device_id_type=MESH,
                ).wait_recv()

    for block in range(8):
        at = pl.ds((block % 4) * 128, 128)
        total = dkv_parts[block // 4, 0, :, :, at].astype(F32) + dkv_parts[block // 4, 1, :, :, at].astype(F32)
        dkv_sum[block] = total.astype(BF16)

    keep_bias.wait()

    def finish(step, _):
        send_bias(step).wait()
        return 0

    lax.fori_loop(1, HEADS, finish, 0)


def finish_kernel(
    mixed_ref, gain_ref, weight_ref, dq_ref, dkv_ref, q_out, k_out, v_out, weight_out, gain_out,
    plane_parts, group_parts, own_dq, own_dkv, out_sem, in_sem, out2_sem, in2_sem, own_sem,
):
    samp, half, head = place()
    greet(samp, half, head, True, 7)

    def share(step):
        return remote(
            mixed_ref, plane_parts.at[head], out_sem.at[0, step], in_sem.at[0, step],
            samp, half, lax.rem(head + step, HEADS),
        )

    def send_dq(step):
        peer = lax.rem(head + step, HEADS)
        return remote(
            dq_ref.at[peer // 2], own_dq.at[head], out_sem.at[1, step], in_sem.at[1, step], samp, half, peer
        )

    def send_dkv(step):
        peer = lax.rem(head + step, HEADS)
        return remote(
            dkv_ref.at[peer // 2], own_dkv.at[head], out_sem.at[2, step], in_sem.at[2, step], samp, half, peer
        )

    def start_share(step, _):
        share(step).start()
        return 0

    def start_grads(step, _):
        send_dq(step).start()
        send_dkv(step).start()
        return 0

    def wait_share(step, _):
        share(step).wait()
        return 0

    def wait_grads(step, _):
        send_dq(step).wait()
        send_dkv(step).wait()
        return 0

    lax.fori_loop(1, HEADS, start_share, 0)
    lax.fori_loop(1, HEADS, start_grads, 0)
    keep_dq = pltpu.make_async_copy(dq_ref.at[head // 2], own_dq.at[head], own_sem.at[0])
    keep_dkv = pltpu.make_async_copy(dkv_ref.at[head // 2], own_dkv.at[head], own_sem.at[1])
    keep_dq.start()
    keep_dkv.start()
    plane_parts[head] = mixed_ref[...]
    lax.fori_loop(1, HEADS, wait_share, 0)
    spot = samp * 2 + half
    group_parts[spot] = sum(plane_parts[other] for other in range(HEADS))

    def share_group(apart):
        return remote(
            group_parts.at[spot], group_parts.at[spot], out2_sem.at[apart], in2_sem.at[apart],
            lax.rem(samp + apart % 4, 4), half if apart < 4 else 1 - half, head,
        )

    for apart in range(1, 8):
        share_group(apart).start()
    keep_dq.wait()
    keep_dkv.wait()
    lax.fori_loop(1, HEADS, wait_grads, 0)
    odd = lax.rem(head, 2) == 1
    for which in range(2):
        for out, source in (
            (q_out, own_dq[:, which]),
            (k_out, own_dkv[:, which, :SIZE]),
            (v_out, own_dkv[:, which, SIZE:]),
        ):
            turned = source.reshape(HEADS * SIZE, 128).astype(F32).T
            out[which] = jnp.where(odd, turned[64:], turned[:64]).astype(BF16)
    for apart in range(1, 8):
        share_group(apart).wait()
    total = sum(group_parts[other] for other in range(8))
    gain_out[...] = jnp.sum(total * weight_ref[...], 0, keepdims=True)
    weight_out[...] = (total * gain_ref[...]).T


def pair_kernel(pair_ref, dbias_ref, back_ref, out_ref, total_ref, mixed_ref, turned_ref, wide_ref, scaled_ref, standard_ref):
    dbias = dbias_ref[...].reshape(256, 512).astype(F32)
    for part in range(4):
        wide_ref[part] = dbias[:, part * 128 : (part + 1) * 128]
    turned_ref[...] = dbias.T.astype(BF16)

    @pl.when(pl.program_id(0) == 0)
    def _():
        mixed_ref[...] = jnp.zeros_like(mixed_ref)

    def each(couple, _):
        scaled_ref[...] = jnp.dot(turned_ref[...], back_ref[couple], preferred_element_type=F32)
        for which in range(2):
            lanes = pl.ds(which * 128, 128)
            for part in range(4):
                rows = pl.ds(part * 128, 128)
                standard, inverse = normalise(pair_ref[2 * couple + which, rows, :])
                scaled = scaled_ref[rows, lanes]
                along = jnp.sum(scaled * standard, -1, keepdims=True) * (1.0 / 128)
                out_ref[2 * couple + which, rows, :] = (inverse * (scaled - standard * along)).astype(BF16)
                standard_ref[rows, lanes] = standard.astype(BF16)
        left = jnp.concatenate(
            [
                jnp.concatenate(
                    [wide_ref[part, pl.ds(2 * couple + which, 16, stride=16), :] for part in range(4)], 1
                )
                for which in range(2)
            ],
            0,
        )
        mixed_ref[...] += jnp.dot(left.astype(BF16), standard_ref[...], preferred_element_type=F32)
        return 0

    lax.fori_loop(0, 8, each, 0)

    @pl.when(pl.program_id(0) == 3)
    def _():
        total_ref[...] = mixed_ref[:16, :128] + mixed_ref[16:, 128:]


def on_device(queries, keys, values, out_grad, pair_repr, norm_gain, bias_weight, token_mask):
    samp = lax.axis_index("samp")
    flat = [array.reshape(128, 768) for array in (queries, out_grad, keys, values)]
    packed = pl.pallas_call(
        pack_kernel,
        out_shape=shape((HEADS, 4 * SIZE, 128)),
        in_specs=[WHOLE] * 4,
        out_specs=WHOLE,
    )(*flat)

    eye = jnp.eye(16, dtype=F32)
    weight = bias_weight.astype(F32)
    spread = (weight[None, :, :, None] * eye[:, None, None, :]).reshape(16 * 128, 256).astype(BF16)
    bias = pl.pallas_call(
        bias_kernel,
        grid=(4,),
        out_shape=shape((HEADS, 64, 512)),
        in_specs=[
            pl.BlockSpec((16, 512, 128), lambda i: (i, 0, 0)),
            pl.BlockSpec((1, 128), lambda i: (0, 0)),
            pl.BlockSpec((2048, 256), lambda i: (0, 0)),
        ],
        out_specs=pl.BlockSpec((HEADS, 16, 512), lambda i: (0, i, 0)),
        scratch_shapes=[pltpu.VMEM((512, 2048), BF16)],
        compiler_params=pltpu.CompilerParams(vmem_limit_bytes=32 * MIB),
    )(pair_repr, norm_gain.reshape(1, 128), spread)

    qo, kv, all_bias, _ = pl.pallas_call(
        spread_kernel,
        out_shape=(
            shape((4, 16, 96, 128)),
            shape((4, 8, 96, 128)),
            shape((1024, 512)),
            shape((16, 96, 128)),
        ),
        in_specs=[ANY] * 2,
        out_specs=[ANY] * 4,
        scratch_shapes=[
            pltpu.SemaphoreType.DMA((3, 16)),
            pltpu.SemaphoreType.DMA((3, 16)),
            pltpu.SemaphoreType.DMA((4,)),
            pltpu.SemaphoreType.DMA((8,)),
            pltpu.SemaphoreType.DMA((8,)),
        ],
        compiler_params=pltpu.CompilerParams(collective_id=0, has_side_effects=True),
    )(packed, bias)

    keep = lax.dynamic_slice_in_dim((token_mask > 0).astype(F32), samp * 512, 512)
    keep = jnp.broadcast_to(keep[:, None], (512, 128))
    dq, dkv, dbias = pl.pallas_call(
        attend_kernel,
        out_shape=(shape((8, SIZE, 1024)), shape((8, 96, 512)), shape((1024, 512))),
        in_specs=[WHOLE] * 4,
        out_specs=[WHOLE] * 3,
        scratch_shapes=[
            pltpu.VMEM((8, 512, 1024), F32),
            pltpu.VMEM((8, 512, 1024), F32),
            pltpu.VMEM((512, 1024), F32),
            pltpu.VMEM((512, 1024), F32),
            pltpu.VMEM((8, 128, 1024), BF16),
            pltpu.VMEM((8, 1024, 128), BF16),
            pltpu.VMEM((8, 128, 512), BF16),
            pltpu.VMEM((8, 512, 128), BF16),
            pltpu.VMEM((512, 1024), BF16),
            pltpu.VMEM((512, 1024), BF16),
            pltpu.VMEM((8, 8, 1024), F32),
            pltpu.VMEM((4, 8, 8, 1024), F32),
            pltpu.SemaphoreType.DMA((8, 4)),
            pltpu.SemaphoreType.DMA((8, 4)),
        ],
        compiler_params=pltpu.CompilerParams(
            collective_id=1, has_side_effects=True, vmem_limit_bytes=60 * MIB
        ),
    )(qo, kv, all_bias, keep)

    own_bias, dq_sum, dkv_sum = pl.pallas_call(
        collect_kernel,
        out_shape=(shape((HEADS, 64, 512)), shape((8, 2, SIZE, 128)), shape((8, 2, 96, 128))),
        in_specs=[ANY] * 3,
        out_specs=[ANY, WHOLE, WHOLE],
        scratch_shapes=[
            pltpu.VMEM((4, 2, SIZE, 1024), BF16),
            pltpu.VMEM((2, 2, 2, 96, 512), BF16),
            pltpu.SemaphoreType.DMA((1, 16)),
            pltpu.SemaphoreType.DMA((1, 16)),
            pltpu.SemaphoreType.DMA((3,)),
            pltpu.SemaphoreType.DMA((8,)),
            pltpu.SemaphoreType.DMA((8,)),
        ],
        compiler_params=pltpu.CompilerParams(
            collective_id=2, has_side_effects=True, vmem_limit_bytes=32 * MIB
        ),
    )(dq, dkv, dbias)

    scaled = weight * norm_gain[:, None]
    scaled = scaled - jnp.mean(scaled, 0, keepdims=True)
    picks = eye.reshape(8, 2, 16)
    back = jnp.einsum("ch,ktj->khjtc", scaled, picks).reshape(8, 256, 256).astype(BF16)
    grad_pair, mixed = pl.pallas_call(
        pair_kernel,
        grid=(4,),
        out_shape=(shape((64, 512, 128)), shape((HEADS, 128), F32)),
        in_specs=[
            pl.BlockSpec((16, 512, 128), lambda i: (i, 0, 0)),
            pl.BlockSpec((HEADS, 16, 512), lambda i: (0, i, 0)),
            pl.BlockSpec((8, 256, 256), lambda i: (0, 0, 0)),
        ],
        out_specs=(
            pl.BlockSpec((16, 512, 128), lambda i: (i, 0, 0)),
            pl.BlockSpec((HEADS, 128), lambda i: (0, 0)),
        ),
        scratch_shapes=[
            pltpu.VMEM((32, 256), F32),
            pltpu.VMEM((512, 256), BF16),
            pltpu.VMEM((4, 256, 128), F32),
            pltpu.VMEM((512, 256), F32),
            pltpu.VMEM((512, 256), BF16),
        ],
        compiler_params=pltpu.CompilerParams(vmem_limit_bytes=32 * MIB),
    )(pair_repr, own_bias, back)
    grad_queries, grad_keys, grad_values, grad_weight, grad_gain = pl.pallas_call(
        finish_kernel,
        out_shape=(shape((2, 64, 768)),) * 3 + (shape((128, HEADS), F32), shape((1, 128), F32)),
        in_specs=[WHOLE] * 5,
        out_specs=[WHOLE] * 5,
        scratch_shapes=[
            pltpu.VMEM((HEADS, HEADS, 128), F32),
            pltpu.VMEM((8, HEADS, 128), F32),
            pltpu.VMEM((HEADS, 2, SIZE, 128), BF16),
            pltpu.VMEM((HEADS, 2, 96, 128), BF16),
            pltpu.SemaphoreType.DMA((3, 16)),
            pltpu.SemaphoreType.DMA((3, 16)),
            pltpu.SemaphoreType.DMA((8,)),
            pltpu.SemaphoreType.DMA((8,)),
            pltpu.SemaphoreType.DMA((2,)),
        ],
        compiler_params=pltpu.CompilerParams(
            collective_id=3, has_side_effects=True, vmem_limit_bytes=32 * MIB
        ),
    )(mixed, norm_gain.reshape(1, 128), weight.T, dq_sum, dkv_sum)
    return grad_queries, grad_keys, grad_values, grad_pair, grad_weight, grad_gain.reshape(128)


def solution(mesh):
    tokens = P("samp", "row", None)
    pairs = P("row", "samp", None)
    return jax.shard_map(
        on_device,
        mesh=mesh,
        in_specs=(tokens, tokens, tokens, tokens, pairs, P(), P(), P()),
        out_specs=(tokens, tokens, tokens, pairs, P(), P()),
        check_vma=False,
    )
```

```python
import functools
import math

import jax
import jax.numpy as jnp
import numpy as np
from jax import lax
from jax.experimental import pallas as pl
from jax.experimental.pallas import tpu as pltpu
from jax.sharding import PartitionSpec as P

MESH = pl.DeviceIdType.MESH
F32 = jnp.float32
BF16 = jnp.bfloat16
LOG2E = math.log2(math.e)
MASKED = -1e9 * LOG2E
HEADS = 16
SIZE = 48
ANY = pl.BlockSpec(memory_space=pl.ANY)
WHOLE = pl.BlockSpec(memory_space=pltpu.VMEM)
MIB = 1024 * 1024


def shape(dims, dtype=BF16):
    return jax.ShapeDtypeStruct(dims, dtype)


def place():
    samp, row = lax.axis_index("samp"), lax.axis_index("row")
    return samp, row // HEADS, lax.rem(row, HEADS)


def remote(src, dst, send, recv, samp, half, head):
    return pltpu.make_async_remote_copy(
        src_ref=src,
        dst_ref=dst,
        send_sem=send,
        recv_sem=recv,
        device_id=(samp, half * HEADS + head),
        device_id_type=MESH,
    )


def greet(samp, half, head, plane, group):
    barrier = pltpu.get_barrier_semaphore()
    count = 0
    if plane:
        def signal(step, _):
            peer = lax.rem(head + step, HEADS)
            pl.semaphore_signal(
                barrier, inc=1, device_id=(samp, half * HEADS + peer), device_id_type=MESH
            )
            return 0

        lax.fori_loop(1, HEADS, signal, 0)
        count += HEADS - 1
    for apart in range(1, 8):
        if apart >= 4 and group < 7:
            break
        other = lax.rem(samp + apart, 4)
        side = half if apart < 4 else 1 - half
        pl.semaphore_signal(
            barrier, inc=1, device_id=(other, side * HEADS + head), device_id_type=MESH
        )
        count += 1
    pl.semaphore_wait(barrier, count)


def dot(left, right):
    return jnp.dot(left, right, preferred_element_type=F32)


def untangle(first, second):
    first, second = first.astype(F32), second.astype(F32)
    low = lax.broadcasted_iota(jnp.int32, first.shape, 1) < 64
    return (
        jnp.where(low, first, pltpu.roll(second, 64, 1)),
        jnp.where(low, pltpu.roll(first, 64, 1), second),
    )


def main_kernel(
    q_ref, o_ref, k_ref, v_ref, pair_ref, gain_ref, spread_ref, centre_ref, mean_ref, keep_ref,
    standard_out, inverse_out, own_bias, dq_sum, dkv_sum,
    packed, qo, kv, kv_near, all_bias, bias, pairs, inverse_wide,
    raised_ref, along_ref, bias_t, qo_t, qo_rows, kv_t, kv_rows, kept_ref, vals_ref,
    low_ref, tops, stats, dq_ref, dkv_ref, dq_parts, dkv_parts,
    load_sem, store_sem, own_sem, plane_out, plane_in, bias_out, bias_in, group_out, group_in,
    stat_out, stat_in, part_out, part_in, back_out, back_in,
):
    samp, half, head = place()
    core, high = lax.rem(samp, 2), samp // 2
    kin = (samp, high * 2 + 1 - core, (1 - high) * 2 + core, (1 - high) * 2 + 1 - core)
    inv_root = 1.0 / math.sqrt(SIZE)

    def load(block):
        return pltpu.make_async_copy(
            pair_ref.at[pl.ds(block * 16, 16)], pairs.at[block % 3], load_sem.at[block]
        )

    def store(block):
        return pltpu.make_async_copy(
            pairs.at[block % 3], standard_out.at[pl.ds(block * 16, 16)], store_sem.at[block]
        )

    load(0).start()
    load(1).start()
    for part, ref in enumerate((q_ref, o_ref, k_ref, v_ref)):
        turned = ref[...].T
        for each in range(HEADS):
            packed[each, part * SIZE : (part + 1) * SIZE, :] = turned[each * SIZE : (each + 1) * SIZE]
    greet(samp, half, head, True, 7)

    def copy_pack(step, which):
        peer = lax.rem(head + step, HEADS)
        land = kv_near if which else qo.at[samp]
        return remote(
            packed.at[peer, pl.ds(which * 96, 96)], land.at[head],
            plane_out.at[which, step], plane_in.at[which, step], samp, half, peer,
        )

    def start_pack(which):
        def body(step, _):
            copy_pack(step, which).start()
            return 0

        lax.fori_loop(1, HEADS, body, 0)

    def wait_pack(which):
        def body(step, _):
            copy_pack(step, which).wait()
            return 0

        lax.fori_loop(1, HEADS, body, 0)

    start_pack(1)
    start_pack(0)
    own_kv = pltpu.make_async_copy(packed.at[head, pl.ds(96, 96)], kv_near.at[head], own_sem.at[0])
    own_qo = pltpu.make_async_copy(packed.at[head, pl.ds(0, 96)], qo.at[samp, head], own_sem.at[1])
    own_kv.start()
    own_qo.start()

    gain = gain_ref[...]
    narrow = lax.broadcasted_iota(jnp.int32, (128, 128), 1)

    def norm_block(block):
        slot = block % 3
        load(block).wait()

        def couple(index, _):
            lanes = pl.ds(pl.multiple_of(index * 256, 256), 256)
            for part in range(4):
                rows = pl.ds(part * 128, 128)
                both = jnp.concatenate(
                    [pairs[slot, 2 * index, rows, :], pairs[slot, 2 * index + 1, rows, :]], 1
                )
                centred = dot(both, centre_ref[...])
                variance = dot((centred * centred).astype(BF16), mean_ref[...])
                inverse = lax.rsqrt(variance + 1e-05)
                standard = centred * inverse
                low = standard.astype(BF16)
                pairs[slot, 2 * index, rows, :] = low[:, :128]
                pairs[slot, 2 * index + 1, rows, :] = low[:, 128:]
                low_ref[rows, lanes] = (standard * gain).astype(BF16)
                old = jnp.where(narrow == 2 * index, inverse[:, :128], inverse_wide[rows, :])
                inverse_wide[rows, :] = jnp.where(narrow == 2 * index + 1, inverse[:, 128:], old)
            return 0

        lax.fori_loop(0, 8, couple, 0, unroll=2)
        store(block).start()
        rows = pl.ds(block * 16, 16)
        bias[:, rows, :] = dot(low_ref[...], spread_ref[...]).T.reshape(HEADS, 16, 512).astype(BF16)
        inverse_out[rows, :] = inverse_wide[...].T[:16]

    def copy_bias(block, step):
        peer = lax.rem(head + step, HEADS)
        start = pl.multiple_of(head * 64 + block * 16, 16)
        return remote(
            bias.at[peer, pl.ds(block * 16, 16)], all_bias.at[pl.ds(start, 16)],
            bias_out.at[block, step], bias_in.at[block, step], samp, half, peer,
        )

    def start_bias(block):
        def body(step, _):
            copy_bias(block, step).start()
            return 0

        lax.fori_loop(1, HEADS, body, 0)

    def send_kv(part, across):
        return remote(
            kv_near.at[pl.ds(part * 8, 8)], kv.at[samp],
            group_out.at[4 + part * 2 + across], group_in.at[4 + samp],
            2 * half + part, 1 - half if across else half, head,
        )

    def keep_kv(part):
        return pltpu.make_async_copy(kv_near.at[pl.ds(part * 8, 8)], kv.at[samp], own_sem.at[2])

    def send_qo(which):
        slot = kin[2] if which == 3 else samp
        to = kin[1] if which == 3 else kin[which]
        return remote(qo.at[slot], qo.at[slot], group_out.at[which], group_in.at[which], to, half, head)

    def wait_qo(which):
        slot = kin[which]
        remote(
            qo.at[slot], qo.at[slot], group_out.at[which], group_in.at[which],
            kin[1] if which == 3 else kin[which], half, head,
        ).wait_recv()

    norm_block(0)
    start_bias(0)
    load(2).start()
    norm_block(1)
    start_bias(1)
    store(0).wait()
    load(3).start()
    wait_pack(1)
    own_kv.wait()
    for part in range(2):
        send_kv(part, 1).start()
        mine = samp == 2 * half + part

        @pl.when(mine)
        def _():
            keep_kv(part).start()

        @pl.when(jnp.logical_not(mine))
        def _():
            send_kv(part, 0).start()

    norm_block(2)
    start_bias(2)
    wait_pack(0)
    own_qo.wait()
    send_qo(2).start()
    send_qo(1).start()
    norm_block(3)
    start_bias(3)
    own_rows = pl.ds(pl.multiple_of(head * 64, 64), 64)
    own_move = pltpu.make_async_copy(bias.at[head], all_bias.at[own_rows], own_sem.at[3])
    own_move.start()

    filler = jnp.zeros((32, 128), F32)

    def unpack(source, turned_ref, rows_ref, owner, count):
        def body(pair, _):
            at = pl.ds(pl.multiple_of(pair * 128, 128), 128)
            both = untangle(source[owner, 2 * pair], source[owner, 2 * pair + 1])
            for which in range(2):
                filled = jnp.concatenate([both[which], filler], 0)
                turned_ref[2 * owner + which, :, at] = filled.astype(BF16)
                rows_ref[2 * owner + which, at, :] = filled.T.astype(BF16)
            return 0

        lax.fori_loop(0, count, body, 0, unroll=2)

    unpack(qo, qo_t, qo_rows, samp, 8)
    wait_qo(2)
    send_qo(3).start()

    for other in range(4):
        @pl.when(jnp.logical_not((high == half) & (samp == other)))
        def _():
            pltpu.make_async_remote_copy(
                src_ref=kv_near.at[pl.ds(0, 8)],
                dst_ref=kv.at[other],
                send_sem=group_out.at[4],
                recv_sem=group_in.at[4 + other],
                device_id=(other, high * HEADS + head),
                device_id_type=MESH,
            ).wait_recv()

    for part in range(2):
        @pl.when(samp == 2 * half + part)
        def _():
            keep_kv(part).wait()

    def unpack_kv(owner, _):
        unpack(kv, kv_t, kv_rows, owner, 4)
        return 0

    lax.fori_loop(0, 4, unpack_kv, 0)

    own_move.wait()
    for block in range(4):
        def wait_bias(step, _):
            copy_bias(block, step).wait()
            return 0

        lax.fori_loop(1, HEADS, wait_bias, 0)

    def turn_bias(block, _):
        at = pl.ds(pl.multiple_of(block * 128, 128), 128)
        turned = all_bias[at, :].astype(F32).T * LOG2E
        bias_t[:, at] = jnp.where(keep_ref[...] > 0, turned, MASKED)
        return 0

    lax.fori_loop(0, 8, turn_bias, 0)

    def stat_copy(sample, apart):
        return remote(
            stats.at[samp, sample], stats.at[samp, sample],
            stat_out.at[sample, apart], stat_in.at[sample, apart],
            lax.rem(samp + apart, 4), half, head,
        )

    wide = lax.broadcasted_iota(jnp.int32, (512, 128), 1)

    def first_pass(owner):
        def sample_body(which, _):
            sample = 2 * owner + which
            both = kv_rows[sample]
            kept_ref[...] = jnp.where((wide < SIZE) & (keep_ref[...] > 0), both, 0).astype(BF16)
            vals_ref[...] = jnp.where(wide >= SIZE, both, 0).astype(BF16)

            def block_body(block, _):
                at = pl.ds(pl.multiple_of(block * 512, 512), 512)
                right = qo_t[sample, :, at]
                partial = []
                for part in range(4):
                    rows = pl.ds(part * 128, 128)
                    score = dot(kept_ref[rows, :], right)
                    along = dot(vals_ref[rows, :], right)
                    score = score * (inv_root * LOG2E) + bias_t[rows, at]
                    top = jnp.max(score, 0, keepdims=True)
                    raised = jnp.exp2(score - top)
                    raised_ref[sample, rows, at] = raised
                    along_ref[sample, rows, at] = along
                    tops[sample, part : part + 1, at] = top
                    partial.append(
                        (top, jnp.sum(raised, 0, keepdims=True), jnp.sum(raised * along, 0, keepdims=True))
                    )
                peak = functools.reduce(jnp.maximum, [p[0] for p in partial])
                scale = [jnp.exp2(p[0] - peak) for p in partial]
                stats[samp, sample, 0:1, at] = peak
                stats[samp, sample, 1:2, at] = sum(p[1] * w for p, w in zip(partial, scale))
                stats[samp, sample, 2:3, at] = sum(p[2] * w for p, w in zip(partial, scale))
                return 0

            lax.fori_loop(0, 2, block_body, 0)
            for apart in range(1, 4):
                stat_copy(sample, apart).start()
            return 0

        lax.fori_loop(0, 2, sample_body, 0)

    stats[samp] = jnp.zeros((8, 8, 1024), F32)
    first_pass(samp)
    for which in range(1, 4):
        if which != 2:
            wait_qo(which)
        unpack(qo, qo_t, qo_rows, kin[which], 8)
        first_pass(kin[which])

    dbias_t = bias_t
    dbias_t[...] = jnp.zeros((512, 1024), F32)

    def second_pass(owner):
        def sample_body(which, _):
            sample = 2 * owner + which
            for apart in range(1, 4):
                stat_copy(sample, apart).wait_recv()

            def block_body(block, _):
                at = pl.ds(pl.multiple_of(block * 256, 256), 256)
                after = pl.ds(pl.multiple_of(block * 256 + 1024, 256), 256)
                peaks = [stats[other, sample, 0:1, at] for other in range(4)]
                peak = functools.reduce(jnp.maximum, peaks)
                scale = [jnp.exp2(p - peak) for p in peaks]
                total = sum(stats[other, sample, 1:2, at] * scale[other] for other in range(4))
                mixed = sum(stats[other, sample, 2:3, at] * scale[other] for other in range(4))
                share = 1.0 / total
                mean = mixed * share
                for part in range(4):
                    rows = pl.ds(part * 128, 128)
                    factor = jnp.exp2(tops[sample, part : part + 1, at] - peak) * share
                    probs = raised_ref[sample, rows, at] * factor
                    grad = probs * (along_ref[sample, rows, at] - mean)
                    dbias_t[rows, at] += grad
                    low_ref[rows, at] = probs.astype(BF16)
                    low_ref[rows, after] = grad.astype(BF16)
                return 0

            lax.fori_loop(0, 4, block_body, 0)
            right = qo_rows[sample]
            dv = dot(low_ref[:, :1024], right)
            dk = dot(low_ref[:, 1024:], right)
            turned = jnp.where(wide < SIZE, dk * inv_root, dv).T
            dkv_ref[sample] = turned[:96].astype(BF16)
            dq = dot(kv_t[sample, :SIZE, :], low_ref[:, 1024:])
            dq_ref[sample] = (dq * inv_root).astype(BF16)
            return 0

        lax.fori_loop(0, 2, sample_body, 0)

    def send_dq(which):
        return remote(
            dq_ref.at[pl.ds(2 * kin[which], 2)], dq_parts.at[which - 1],
            part_out.at[which], part_in.at[which], kin[which], half, head,
        )

    def send_dkv(which):
        return remote(
            dkv_ref.at[pl.ds(2 * kin[which], 2)], dkv_parts.at[core, half],
            part_out.at[4 + which], part_in.at[4 + 2 * core + half], kin[which], high, head,
        )

    keep_dkv = pltpu.make_async_copy(dkv_ref.at[pl.ds(2 * samp, 2)], dkv_parts.at[core, half], own_sem.at[4])
    for which in (2, 3, 1):
        second_pass(kin[which])
        send_dq(which).start()
        send_dkv(which).start()
    second_pass(samp)

    @pl.when(high == half)
    def _():
        keep_dkv.start()

    @pl.when(high != half)
    def _():
        send_dkv(0).start()

    def send_back(peer):
        at = pl.ds(pl.multiple_of(peer * 64, 64), 64)
        return remote(
            all_bias.at[at], own_bias.at[head], back_out.at[peer], back_in.at[head], samp, half, peer
        )

    keep_back = pltpu.make_async_copy(all_bias.at[own_rows], own_bias.at[head], own_sem.at[5])

    def turn_back(step, _):
        block = lax.rem(head // 2 + step, 8)
        at = pl.ds(pl.multiple_of(block * 128, 128), 128)
        all_bias[at, :] = dbias_t[:, at].T.astype(BF16)
        for odd in range(2):
            peer = 2 * block + odd

            @pl.when(peer == head)
            def _():
                keep_back.start()

            @pl.when(peer != head)
            def _():
                send_back(peer).start()

        return 0

    lax.fori_loop(0, 8, turn_back, 0)

    for which in range(1, 4):
        send_dq(which).wait()
    for block in range(8):
        at = pl.ds(block * 128, 128)
        total = dq_ref[pl.ds(2 * samp, 2), :, at].astype(F32)
        for which in range(3):
            total = total + dq_parts[which, :, :, at].astype(F32)
        dq_sum[block] = total.astype(BF16)

    @pl.when(high == half)
    def _():
        keep_dkv.wait()

    @pl.when(high != half)
    def _():
        send_dkv(0).wait_send()

    for which in range(1, 4):
        send_dkv(which).wait_send()
    for piece in range(2):
        for side in range(2):
            source = 2 * half + piece

            @pl.when(jnp.logical_not((source == samp) & (half == side)))
            def _():
                pltpu.make_async_remote_copy(
                    src_ref=dkv_ref.at[pl.ds(0, 2)],
                    dst_ref=dkv_parts.at[piece, side],
                    send_sem=part_out.at[4],
                    recv_sem=part_in.at[4 + 2 * piece + side],
                    device_id=(source, side * HEADS + head),
                    device_id_type=MESH,
                ).wait_recv()

    for block in range(8):
        at = pl.ds((block % 4) * 128, 128)
        total = dkv_parts[block // 4, 0, :, :, at].astype(F32) + dkv_parts[block // 4, 1, :, :, at].astype(F32)
        dkv_sum[block] = total.astype(BF16)

    for part in range(2):
        send_kv(part, 1).wait_send()

        @pl.when(samp != 2 * half + part)
        def _():
            send_kv(part, 0).wait_send()

    for which in range(1, 4):
        send_qo(which).wait_send()

    def sent(sample, _):
        for apart in range(1, 4):
            stat_copy(sample, apart).wait_send()
        return 0

    lax.fori_loop(0, 8, sent, 0)
    for block in range(1, 4):
        store(block).wait()
    keep_back.wait()

    def arrived(step, _):
        other = lax.rem(head + step, HEADS)
        at = pl.ds(pl.multiple_of(other * 64, 64), 64)
        remote(
            all_bias.at[at], own_bias.at[other], back_out.at[other], back_in.at[other], samp, half, other
        ).wait()
        return 0

    lax.fori_loop(1, HEADS, arrived, 0)


def pair_kernel(
    standard_ref, dbias_ref, inverse_ref, back_ref, out_ref, total_ref, mixed_ref, turned_ref, wide_ref
):
    dbias = dbias_ref[...].reshape(256, 512).astype(F32)
    for part in range(4):
        wide_ref[part] = dbias[:, part * 128 : (part + 1) * 128]
    shrunk = dbias.reshape(HEADS, 16, 512) * inverse_ref[...][None]
    turned_ref[...] = shrunk.reshape(256, 512).T.astype(BF16)

    @pl.when(pl.program_id(0) == 0)
    def _():
        mixed_ref[...] = jnp.zeros_like(mixed_ref)

    def couple(index, _):
        left = jnp.concatenate(
            [
                jnp.concatenate(
                    [wide_ref[part, pl.ds(2 * index + which, 16, stride=16), :] for part in range(4)], 1
                )
                for which in range(2)
            ],
            0,
        ).astype(BF16)
        mixed = mixed_ref[...]
        for part in range(4):
            rows = pl.ds(part * 128, 128)
            low = jnp.concatenate([standard_ref[2 * index, rows, :], standard_ref[2 * index + 1, rows, :]], 1)
            standard = low.astype(F32)
            scaled = dot(turned_ref[rows, :], back_ref[index])
            for which in range(2):
                lanes = slice(which * 128, which * 128 + 128)
                mine = standard[:, lanes]
                along = jnp.sum(scaled[:, lanes] * mine, -1, keepdims=True) * (1.0 / 128)
                out_ref[2 * index + which, rows, :] = (scaled[:, lanes] - mine * along).astype(BF16)
            mixed = mixed + dot(left[:, part * 128 : (part + 1) * 128], low)
        mixed_ref[...] = mixed
        return 0

    lax.fori_loop(0, 8, couple, 0)

    @pl.when(pl.program_id(0) == 3)
    def _():
        total_ref[...] = mixed_ref[:16, :128] + mixed_ref[16:, 128:]


def finish_kernel(
    mixed_ref, gain_ref, weight_ref, dq_ref, dkv_ref, q_out, k_out, v_out, weight_out, gain_out,
    plane_parts, group_parts, own_dq, own_dkv, out_sem, in_sem, out2_sem, in2_sem, own_sem,
):
    samp, half, head = place()
    greet(samp, half, head, True, 7)

    def share(step):
        return remote(
            mixed_ref, plane_parts.at[head], out_sem.at[0, step], in_sem.at[0, step],
            samp, half, lax.rem(head + step, HEADS),
        )

    def send_dq(step):
        peer = lax.rem(head + step, HEADS)
        return remote(
            dq_ref.at[peer // 2], own_dq.at[head], out_sem.at[1, step], in_sem.at[1, step], samp, half, peer
        )

    def send_dkv(step):
        peer = lax.rem(head + step, HEADS)
        return remote(
            dkv_ref.at[peer // 2], own_dkv.at[head], out_sem.at[2, step], in_sem.at[2, step], samp, half, peer
        )

    def start_share(step, _):
        share(step).start()
        return 0

    def start_grads(step, _):
        send_dq(step).start()
        send_dkv(step).start()
        return 0

    def wait_share(step, _):
        share(step).wait()
        return 0

    def wait_grads(step, _):
        send_dq(step).wait()
        send_dkv(step).wait()
        return 0

    lax.fori_loop(1, HEADS, start_share, 0)
    lax.fori_loop(1, HEADS, start_grads, 0)
    keep_dq = pltpu.make_async_copy(dq_ref.at[head // 2], own_dq.at[head], own_sem.at[0])
    keep_dkv = pltpu.make_async_copy(dkv_ref.at[head // 2], own_dkv.at[head], own_sem.at[1])
    keep_dq.start()
    keep_dkv.start()
    plane_parts[head] = mixed_ref[...]
    lax.fori_loop(1, HEADS, wait_share, 0)
    spot = samp * 2 + half
    group_parts[spot] = sum(plane_parts[other] for other in range(HEADS))

    def share_group(apart):
        return remote(
            group_parts.at[spot], group_parts.at[spot], out2_sem.at[apart], in2_sem.at[apart],
            lax.rem(samp + apart % 4, 4), half if apart < 4 else 1 - half, head,
        )

    for apart in range(1, 8):
        share_group(apart).start()
    keep_dq.wait()
    keep_dkv.wait()
    lax.fori_loop(1, HEADS, wait_grads, 0)
    odd = lax.rem(head, 2) == 1
    for which in range(2):
        for out, source in (
            (q_out, own_dq[:, which]),
            (k_out, own_dkv[:, which, :SIZE]),
            (v_out, own_dkv[:, which, SIZE:]),
        ):
            turned = source.reshape(HEADS * SIZE, 128).astype(F32).T
            out[which] = jnp.where(odd, turned[64:], turned[:64]).astype(BF16)
    for apart in range(1, 8):
        share_group(apart).wait()
    total = sum(group_parts[other] for other in range(8))
    gain_out[...] = jnp.sum(total * weight_ref[...], 0, keepdims=True)
    weight_out[...] = (total * gain_ref[...]).T


def on_device(queries, keys, values, out_grad, pair_repr, norm_gain, bias_weight, token_mask):
    samp = lax.axis_index("samp")
    flat = [array.reshape(128, 768) for array in (queries, out_grad, keys, values)]
    eye = jnp.eye(16, dtype=F32)
    weight = bias_weight.astype(F32)
    spread = (weight[None, :, :, None] * eye[:, None, None, :]).reshape(16 * 128, 256).astype(BF16)
    mean = np.kron(np.eye(2), np.full((128, 128), 1.0 / 128))
    centre = jnp.asarray(np.eye(256) - mean, BF16)
    mean = jnp.asarray(mean, BF16)
    keep = lax.dynamic_slice_in_dim((token_mask > 0).astype(F32), samp * 512, 512)
    keep = jnp.broadcast_to(keep[:, None], (512, 128))
    sems = pltpu.SemaphoreType.DMA
    standard, inverse, own_bias, dq_sum, dkv_sum = pl.pallas_call(
        main_kernel,
        out_shape=(
            shape((64, 512, 128)),
            shape((64, 512), F32),
            shape((HEADS, 64, 512)),
            shape((8, 2, SIZE, 128)),
            shape((8, 2, 96, 128)),
        ),
        in_specs=[WHOLE] * 4 + [ANY] + [WHOLE] * 5,
        out_specs=[ANY, WHOLE, ANY, WHOLE, WHOLE],
        scratch_shapes=[
            pltpu.VMEM((HEADS, 4 * SIZE, 128), BF16),
            pltpu.VMEM((4, HEADS, 96, 128), BF16),
            pltpu.VMEM((4, 8, 96, 128), BF16),
            pltpu.VMEM((HEADS, 96, 128), BF16),
            pltpu.VMEM((1024, 512), BF16),
            pltpu.VMEM((HEADS, 64, 512), BF16),
            pltpu.VMEM((3, 16, 512, 128), BF16),
            pltpu.VMEM((512, 128), F32),
            pltpu.VMEM((8, 512, 1024), F32),
            pltpu.VMEM((8, 512, 1024), F32),
            pltpu.VMEM((512, 1024), F32),
            pltpu.VMEM((8, 128, 1024), BF16),
            pltpu.VMEM((8, 1024, 128), BF16),
            pltpu.VMEM((8, 128, 512), BF16),
            pltpu.VMEM((8, 512, 128), BF16),
            pltpu.VMEM((512, 128), BF16),
            pltpu.VMEM((512, 128), BF16),
            pltpu.VMEM((512, 2048), BF16),
            pltpu.VMEM((8, 8, 1024), F32),
            pltpu.VMEM((4, 8, 8, 1024), F32),
            pltpu.VMEM((8, SIZE, 1024), BF16),
            pltpu.VMEM((8, 96, 512), BF16),
            pltpu.VMEM((3, 2, SIZE, 1024), BF16),
            pltpu.VMEM((2, 2, 2, 96, 512), BF16),
            sems((4,)),
            sems((4,)),
            sems((6,)),
            sems((2, 16)),
            sems((2, 16)),
            sems((4, 16)),
            sems((4, 16)),
            sems((8,)),
            sems((8,)),
            sems((8, 4)),
            sems((8, 4)),
            sems((8,)),
            sems((8,)),
            sems((16,)),
            sems((16,)),
        ],
        compiler_params=pltpu.CompilerParams(
            collective_id=0, has_side_effects=True, vmem_limit_bytes=63 * MIB
        ),
    )(*flat, pair_repr, jnp.tile(norm_gain.reshape(1, 128), (1, 2)), spread, centre, mean, keep)

    scaled = weight * norm_gain[:, None]
    scaled = scaled - jnp.mean(scaled, 0, keepdims=True)
    back = jnp.einsum("ch,ktj->khjtc", scaled, eye.reshape(8, 2, 16)).reshape(8, 256, 256).astype(BF16)
    grad_pair, mixed = pl.pallas_call(
        pair_kernel,
        grid=(4,),
        out_shape=(shape((64, 512, 128)), shape((HEADS, 128), F32)),
        in_specs=[
            pl.BlockSpec((16, 512, 128), lambda i: (i, 0, 0)),
            pl.BlockSpec((HEADS, 16, 512), lambda i: (0, i, 0)),
            pl.BlockSpec((16, 512), lambda i: (i, 0)),
            pl.BlockSpec((8, 256, 256), lambda i: (0, 0, 0)),
        ],
        out_specs=(
            pl.BlockSpec((16, 512, 128), lambda i: (i, 0, 0)),
            pl.BlockSpec((HEADS, 128), lambda i: (0, 0)),
        ),
        scratch_shapes=[
            pltpu.VMEM((32, 256), F32),
            pltpu.VMEM((512, 256), BF16),
            pltpu.VMEM((4, 256, 128), F32),
        ],
        compiler_params=pltpu.CompilerParams(vmem_limit_bytes=32 * MIB),
    )(standard, own_bias, inverse, back)
    grad_queries, grad_keys, grad_values, grad_weight, grad_gain = pl.pallas_call(
        finish_kernel,
        out_shape=(shape((2, 64, 768)),) * 3 + (shape((128, HEADS), F32), shape((1, 128), F32)),
        in_specs=[WHOLE] * 5,
        out_specs=[WHOLE] * 5,
        scratch_shapes=[
            pltpu.VMEM((HEADS, HEADS, 128), F32),
            pltpu.VMEM((8, HEADS, 128), F32),
            pltpu.VMEM((HEADS, 2, SIZE, 128), BF16),
            pltpu.VMEM((HEADS, 2, 96, 128), BF16),
            pltpu.SemaphoreType.DMA((3, 16)),
            pltpu.SemaphoreType.DMA((3, 16)),
            pltpu.SemaphoreType.DMA((8,)),
            pltpu.SemaphoreType.DMA((8,)),
            pltpu.SemaphoreType.DMA((2,)),
        ],
        compiler_params=pltpu.CompilerParams(
            collective_id=3, has_side_effects=True, vmem_limit_bytes=32 * MIB
        ),
    )(mixed, norm_gain.reshape(1, 128), weight.T, dq_sum, dkv_sum)
    return grad_queries, grad_keys, grad_values, grad_pair, grad_weight, grad_gain.reshape(128)


def solution(mesh):
    tokens = P("samp", "row", None)
    pairs = P("row", "samp", None)
    return jax.shard_map(
        on_device,
        mesh=mesh,
        in_specs=(tokens, tokens, tokens, tokens, pairs, P(), P(), P()),
        out_specs=(tokens, tokens, tokens, pairs, P(), P()),
        check_vma=False,
    )
```

```python
import functools
import math

import jax
import jax.numpy as jnp
from jax import lax
from jax.experimental import pallas as pl
from jax.experimental.pallas import tpu as pltpu
from jax.sharding import PartitionSpec as P

MESH = pl.DeviceIdType.MESH
F32 = jnp.float32
BF16 = jnp.bfloat16
LOG2E = math.log2(math.e)
MASKED = -1e9 * LOG2E
HEADS = 16
SIZE = 48
ANY = pl.BlockSpec(memory_space=pl.ANY)
WHOLE = pl.BlockSpec(memory_space=pltpu.VMEM)
MIB = 1024 * 1024


def shape(dims, dtype=BF16):
    return jax.ShapeDtypeStruct(dims, dtype)


def place():
    samp, row = lax.axis_index("samp"), lax.axis_index("row")
    return samp, row // HEADS, lax.rem(row, HEADS)


def remote(src, dst, send, recv, samp, half, head):
    return pltpu.make_async_remote_copy(
        src_ref=src,
        dst_ref=dst,
        send_sem=send,
        recv_sem=recv,
        device_id=(samp, half * HEADS + head),
        device_id_type=MESH,
    )


def dot(left, right):
    return jnp.dot(left, right, preferred_element_type=F32)


def untangle(first, second):
    first, second = first.astype(F32), second.astype(F32)
    low = lax.broadcasted_iota(jnp.int32, first.shape, 1) < 64
    return (
        jnp.where(low, first, pltpu.roll(second, 64, 1)),
        jnp.where(low, pltpu.roll(first, 64, 1), second),
    )


def steps(count, body, start=0, unroll=1):
    def wrapped(index, _):
        body(index)
        return 0

    lax.fori_loop(start, count, wrapped, 0, unroll=unroll)


def kernel(
    q_ref, o_ref, k_ref, v_ref, pair_ref, gain_ref, weight_ref, mask_ref,
    grad_pair, q_out, k_out, v_out, weight_out, gain_out, spilled,
    packed, qo, kv, kv_near, all_bias, bias, pairs, inverse_wide, inverse_ref,
    raised_ref, along_ref, bias_t, qo_rows, kv_t, kv_rows, kept_ref, vals_ref,
    low_ref, tops, stats, dq_parts, dkv_parts, own_bias, weights, turned_ref, wide_ref, mixed_ref,
    centre_ref, mean_ref, keep_ref, dq_sum, dkv_sum, own_dq, own_dkv, mine_ref, plane_parts, group_parts,
    load_sem, store_sem, own_sem, plane_out, plane_in, bias_out, bias_in, group_out, group_in,
    stat_out, stat_in, part_out, part_in, back_out, back_in, last_out, last_in, share_out, share_in,
):
    samp, half, head = place()
    core, high = lax.rem(samp, 2), samp // 2
    kin = (samp, high * 2 + 1 - core, (1 - high) * 2 + core, (1 - high) * 2 + 1 - core)
    inv_root = 1.0 / math.sqrt(SIZE)

    barrier = pltpu.get_barrier_semaphore()

    def hello(step):
        peer = lax.rem(head + step, HEADS)
        pl.semaphore_signal(barrier, inc=1, device_id=(samp, half * HEADS + peer), device_id_type=MESH)

    steps(HEADS, hello, 1)
    for apart in range(1, 8):
        side = half if apart < 4 else 1 - half
        pl.semaphore_signal(
            barrier, inc=1, device_id=(lax.rem(samp + apart, 4), side * HEADS + head), device_id_type=MESH
        )

    def load(block):
        return pltpu.make_async_copy(
            pair_ref.at[pl.ds(block * 16, 16)], pairs.at[min(block, 2)], load_sem.at[block]
        )

    spill = pltpu.make_async_copy(pairs.at[2], spilled, store_sem.at[0])
    reload = pltpu.make_async_copy(spilled, pairs.at[0], store_sem.at[1])

    for block in range(3):
        load(block).start()
    for part, ref in enumerate((k_ref, v_ref, q_ref, o_ref)):
        turned = ref[...].T
        for each in range(HEADS):
            packed[each, part * SIZE : (part + 1) * SIZE, :] = turned[each * SIZE : (each + 1) * SIZE]
    pl.semaphore_wait(barrier, 22)

    def copy_pack(step, which):
        peer = lax.rem(head + step, HEADS)
        land = qo.at[samp] if which else kv_near
        return remote(
            packed.at[peer, pl.ds(which * 96, 96)], land.at[head],
            plane_out.at[which, step], plane_in.at[which, step], samp, half, peer,
        )

    for which in range(2):
        steps(HEADS, lambda step: copy_pack(step, which).start(), 1)
    own_kv = pltpu.make_async_copy(packed.at[head, pl.ds(0, 96)], kv_near.at[head], own_sem.at[0])
    own_qo = pltpu.make_async_copy(packed.at[head, pl.ds(96, 96)], qo.at[samp, head], own_sem.at[1])
    own_kv.start()
    own_qo.start()

    row = lax.broadcasted_iota(jnp.int32, (256, 256), 0)
    lane = lax.broadcasted_iota(jnp.int32, (256, 256), 1)
    averager = jnp.where(row // 128 == lane // 128, 1.0 / 128, 0.0)
    mean_ref[...] = averager.astype(BF16)
    centre_ref[...] = (jnp.where(row == lane, 1.0, 0.0) - averager).astype(BF16)
    gain_row = gain_ref[...]
    gain = jnp.concatenate([gain_row, gain_row], 1)
    weight = weight_ref[...]
    chooser = (
        lax.broadcasted_iota(jnp.int32, (HEADS, 256), 1) // 16 == lax.broadcasted_iota(jnp.int32, (HEADS, 256), 0)
    ).astype(F32).astype(BF16)
    wider = dot(weight, chooser)
    lane_in = lax.rem(lax.broadcasted_iota(jnp.int32, (128, 256), 1), 16)
    for each in range(16):
        weights[each * 128 : (each + 1) * 128, :] = jnp.where(lane_in == each, wider, 0.0).astype(BF16)
    for part in range(4):
        at = pl.ds(pl.multiple_of(samp * 512 + part * 128, 128), 128)
        kept = (mask_ref[0:1, at] > 0).astype(F32)
        keep_ref[part * 128 : (part + 1) * 128, :] = jnp.broadcast_to(kept, (128, 128)).T

    narrow = lax.broadcasted_iota(jnp.int32, (128, 128), 1)

    def norm_block(block):
        slot = min(block, 2)
        load(block).wait()

        def couple(index):
            lanes = pl.ds(pl.multiple_of(index * 256, 256), 256)
            for part in range(4):
                rows = pl.ds(part * 128, 128)
                both = jnp.concatenate(
                    [pairs[slot, 2 * index, rows, :], pairs[slot, 2 * index + 1, rows, :]], 1
                )
                centred = dot(both, centre_ref[...])
                variance = dot((centred * centred).astype(BF16), mean_ref[...])
                inverse = lax.rsqrt(variance + 1e-05)
                standard = centred * inverse
                low = standard.astype(BF16)
                pairs[slot, 2 * index, rows, :] = low[:, :128]
                pairs[slot, 2 * index + 1, rows, :] = low[:, 128:]
                low_ref[rows, lanes] = (standard * gain).astype(BF16)
                old = jnp.where(narrow == 2 * index, inverse[:, :128], inverse_wide[rows, :])
                inverse_wide[rows, :] = jnp.where(narrow == 2 * index + 1, inverse[:, 128:], old)

        steps(8, couple, unroll=2)
        if block == 2:
            spill.start()
        rows = pl.ds(block * 16, 16)
        bias[:, rows, :] = dot(low_ref[...], weights[...]).T.reshape(HEADS, 16, 512).astype(BF16)
        inverse_ref[rows, :] = inverse_wide[...].T[:16]

    def bias_rows(block):
        return pl.ds(pl.multiple_of(block // 2 * 512 + head * 32 + block % 2 * 16, 16), 16)

    def copy_bias(block, step):
        return remote(
            bias.at[lax.rem(head + step, HEADS), pl.ds(block * 16, 16)], all_bias.at[bias_rows(block)],
            bias_out.at[block, step], bias_in.at[block, step], samp, half, lax.rem(head + step, HEADS),
        )

    def keep_bias(block):
        return pltpu.make_async_copy(
            bias.at[head, pl.ds(block * 16, 16)], all_bias.at[bias_rows(block)], own_sem.at[2 + block]
        )

    def start_bias(block):
        steps(HEADS, lambda step: copy_bias(block, step).start(), 1)
        keep_bias(block).start()

    def send_kv(part, across):
        return remote(
            kv_near.at[pl.ds(part * 8, 8)], kv.at[samp],
            group_out.at[4 + part * 2 + across], group_in.at[4 + samp],
            2 * half + part, 1 - half if across else half, head,
        )

    def keep_kv(part):
        return pltpu.make_async_copy(kv_near.at[pl.ds(part * 8, 8)], kv.at[samp], own_sem.at[6])

    def wait_kv(owner):
        here = jnp.logical_and(owner == samp, high == half)

        @pl.when(here)
        def _():
            pltpu.make_async_copy(kv_near.at[pl.ds(0, 8)], kv.at[owner], own_sem.at[6]).wait()

        @pl.when(jnp.logical_not(here))
        def _():
            pltpu.make_async_remote_copy(
                src_ref=kv_near.at[pl.ds(0, 8)],
                dst_ref=kv.at[owner],
                send_sem=group_out.at[4],
                recv_sem=group_in.at[4 + owner],
                device_id=(owner, high * HEADS + head),
                device_id_type=MESH,
            ).wait_recv()

    def send_qo(which):
        slot = kin[2] if which == 3 else samp
        to = kin[1] if which == 3 else kin[which]
        return remote(qo.at[slot], qo.at[slot], group_out.at[which], group_in.at[which], to, half, head)

    def wait_qo(which):
        slot = kin[which]
        remote(
            qo.at[slot], qo.at[slot], group_out.at[which], group_in.at[which],
            kin[1] if which == 3 else kin[which], half, head,
        ).wait_recv()

    norm_block(0)
    start_bias(0)
    steps(HEADS, lambda step: copy_pack(step, 0).wait(), 1)
    own_kv.wait()
    for part in range(2):
        send_kv(part, 1).start()
        mine = samp == 2 * half + part

        @pl.when(mine)
        def _():
            keep_kv(part).start()

        @pl.when(jnp.logical_not(mine))
        def _():
            send_kv(part, 0).start()

    norm_block(1)
    start_bias(1)
    steps(HEADS, lambda step: copy_pack(step, 1).wait(), 1)
    own_qo.wait()
    send_qo(2).start()
    send_qo(1).start()
    norm_block(2)
    start_bias(2)
    spill.wait()
    load(3).start()

    filler = jnp.zeros((32, 128), F32)

    def unpack_qo(owner):
        def body(peer):
            filled = jnp.concatenate([qo[owner, peer].astype(F32), filler], 0).T.astype(BF16)
            for which in range(2):
                for part in range(2):
                    at = pl.ds(pl.multiple_of(part * 512 + peer * 32, 32), 32)
                    start = which * 64 + part * 32
                    qo_rows[2 * owner + which, at, :] = filled[start : start + 32]

        steps(HEADS, body, unroll=2)

    def unpack_kv(owner):
        def body(pair):
            at = pl.ds(pl.multiple_of(pair * 128, 128), 128)
            both = untangle(kv[owner, 2 * pair], kv[owner, 2 * pair + 1])
            for which in range(2):
                filled = jnp.concatenate([both[which], filler], 0)
                kv_t[2 * owner + which, :, at] = filled.astype(BF16)
                kv_rows[2 * owner + which, at, :] = filled.T.astype(BF16)

        steps(4, body, unroll=2)

    unpack_qo(samp)
    norm_block(3)
    start_bias(3)
    wait_qo(2)
    send_qo(3).start()
    wait_kv(samp)
    unpack_kv(samp)

    def turn_bias(part):
        for block in (2 * part, 2 * part + 1):
            keep_bias(block).wait()
            steps(HEADS, lambda step: copy_bias(block, step).wait(), 1)

        def body(block):
            at = pl.ds(pl.multiple_of(part * 512 + block * 128, 128), 128)
            turned = all_bias[at, :].astype(F32).T * LOG2E
            bias_t[:, at] = jnp.where(keep_ref[...] > 0, turned, MASKED)

        steps(4, body)

    def stat_copy(sample, apart):
        return remote(
            stats.at[samp, sample], stats.at[samp, sample],
            stat_out.at[sample, apart], stat_in.at[sample, apart],
            lax.rem(samp + apart, 4), half, head,
        )

    wide = lax.broadcasted_iota(jnp.int32, (512, 128), 1)

    def first_pass(sample, block):
        both = kv_rows[sample]
        kept_ref[...] = jnp.where((wide < SIZE) & (keep_ref[...] > 0), both, 0).astype(BF16)
        vals_ref[...] = jnp.where(wide >= SIZE, both, 0).astype(BF16)
        at = pl.ds(pl.multiple_of(block * 512, 512), 512)
        right = qo_rows[sample, at, :].T
        partial = []
        for part in range(4):
            rows = pl.ds(part * 128, 128)
            score = dot(kept_ref[rows, :], right)
            along = dot(vals_ref[rows, :], right)
            score = score * (inv_root * LOG2E) + bias_t[rows, at]
            top = jnp.max(score, 0, keepdims=True)
            raised = jnp.exp2(score - top)
            raised_ref[sample, rows, at] = raised
            along_ref[sample, rows, at] = along
            tops[sample, part : part + 1, at] = top
            partial.append((top, jnp.sum(raised, 0, keepdims=True), jnp.sum(raised * along, 0, keepdims=True)))
        peak = functools.reduce(jnp.maximum, [p[0] for p in partial])
        scale = [jnp.exp2(p[0] - peak) for p in partial]
        stats[samp, sample, 0:1, at] = peak
        stats[samp, sample, 1:2, at] = sum(p[1] * w for p, w in zip(partial, scale))
        stats[samp, sample, 2:3, at] = sum(p[2] * w for p, w in zip(partial, scale))

    stats[samp] = jnp.zeros((8, 8, 1024), F32)
    for part in range(2):
        turn_bias(part)
        steps(2, lambda which: first_pass(2 * samp + which, part))
    for which in range(2):
        for apart in range(1, 4):
            stat_copy(2 * samp + which, apart).start()

    for which in range(1, 4):
        if which != 2:
            wait_qo(which)
        wait_kv(kin[which])
        unpack_qo(kin[which])
        unpack_kv(kin[which])

        def one(index):
            sample = 2 * kin[which] + index
            steps(2, lambda block: first_pass(sample, block))
            for apart in range(1, 4):
                stat_copy(sample, apart).start()

        steps(2, one)

    for which in range(1, 4):
        send_qo(which).wait_send()
    bias_t[...] = jnp.zeros((512, 1024), F32)

    def second_pass(owner, index, block):
        sample = 2 * owner + index

        def quarter(piece):
            at = pl.ds(pl.multiple_of(block * 512 + piece * 256, 256), 256)
            here = pl.ds(pl.multiple_of(piece * 256, 256), 256)
            after = pl.ds(pl.multiple_of(piece * 256 + 512, 256), 256)
            peaks = [stats[other, sample, 0:1, at] for other in range(4)]
            peak = functools.reduce(jnp.maximum, peaks)
            scale = [jnp.exp2(p - peak) for p in peaks]
            total = sum(stats[other, sample, 1:2, at] * scale[other] for other in range(4))
            blend = sum(stats[other, sample, 2:3, at] * scale[other] for other in range(4))
            share = 1.0 / total
            mean = blend * share
            for part in range(4):
                rows = pl.ds(part * 128, 128)
                factor = jnp.exp2(tops[sample, part : part + 1, at] - peak) * share
                probs = raised_ref[sample, rows, at] * factor
                grad = probs * (along_ref[sample, rows, at] - mean)
                bias_t[rows, at] += grad
                low_ref[rows, here] = probs.astype(BF16)
                low_ref[rows, after] = grad.astype(BF16)

        steps(2, quarter)
        right = qo_rows[sample, block * 512 : block * 512 + 512, :]
        dv = dot(low_ref[:, :512], right)
        dk = dot(low_ref[:, 512:1024], right)
        both = jnp.where(wide < SIZE, dk * inv_root, dv)
        if block == 0:
            raised_ref[sample, :, 0:128] = both
        else:
            turned = (both + raised_ref[sample, :, 0:128]).T
            for piece in range(4):
                packed[2 * sample + piece // 2, piece % 2 * 96 : piece % 2 * 96 + 96, :] = turned[
                    :96, piece * 128 : piece * 128 + 128
                ].astype(BF16)
        dq = (dot(kv_t[sample, :SIZE, :], low_ref[:, 512:1024]) * inv_root).astype(BF16)
        for piece in range(4):
            qo[owner, 2 * (block * 4 + piece) + index, :SIZE, :] = dq[:, piece * 128 : piece * 128 + 128]

    def send_dq(which):
        return remote(
            qo.at[kin[which], :, pl.ds(0, SIZE)], dq_parts.at[which - 1],
            part_out.at[which], part_in.at[which], kin[which], half, head,
        )

    def send_dkv(which):
        return remote(
            packed.at[pl.ds(4 * kin[which], 4)], dkv_parts.at[core, half],
            part_out.at[4 + which], part_in.at[4 + 2 * core + half], kin[which], high, head,
        )

    keep_dkv = pltpu.make_async_copy(packed.at[pl.ds(4 * samp, 4)], dkv_parts.at[core, half], own_sem.at[7])

    def send_back(peer, part):
        at = pl.ds(pl.multiple_of(part * 512 + peer * 32, 32), 32)
        return remote(
            all_bias.at[at], own_bias.at[head, pl.ds(part * 32, 32)],
            back_out.at[part, peer], back_in.at[part, head], samp, half, peer,
        )

    def keep_back(part):
        at = pl.ds(pl.multiple_of(part * 512 + head * 32, 32), 32)
        return pltpu.make_async_copy(
            all_bias.at[at], own_bias.at[head, pl.ds(part * 32, 32)], own_sem.at[8 + part]
        )

    def turn_back(part):
        def body(step):
            block = lax.rem(head // 4 + step, 4)
            at = pl.ds(pl.multiple_of(part * 512 + block * 128, 128), 128)
            all_bias[at, :] = bias_t[:, at].T.astype(BF16)

            def send(index):
                peer = 4 * block + lax.rem(head + index, 4)

                @pl.when(peer == head)
                def _():
                    keep_back(part).start()

                @pl.when(peer != head)
                def _():
                    send_back(peer, part).start()

            steps(4, send)

        steps(4, body)

    def wait_back(part):
        keep_back(part).wait()

        def body(step):
            other = lax.rem(head + step, HEADS)
            at = pl.ds(pl.multiple_of(part * 512 + other * 32, 32), 32)
            remote(
                all_bias.at[at], own_bias.at[other, pl.ds(part * 32, 32)],
                back_out.at[part, other], back_in.at[part, other], samp, half, other,
            ).wait()

        steps(HEADS, body, 1)

    for part in range(2):
        for which in (2, 3, 1, 0):
            def one(index):
                if part == 0:
                    for apart in range(1, 4):
                        stat_copy(2 * kin[which] + index, apart).wait_recv()
                second_pass(kin[which], index, part)

            steps(2, one)
            if part == 1 and which:
                send_dq(which).start()
                send_dkv(which).start()
        turn_back(part)

    @pl.when(high == half)
    def _():
        keep_dkv.start()

    @pl.when(high != half)
    def _():
        send_dkv(0).start()

    scaled_weight = weight.astype(F32).T * gain_row
    scaled_weight = scaled_weight - jnp.mean(scaled_weight, -1, keepdims=True)
    picker = (
        lax.broadcasted_iota(jnp.int32, (256, HEADS), 0) // 16 == lax.broadcasted_iota(jnp.int32, (256, HEADS), 1)
    ).astype(F32).astype(BF16)
    taller = dot(picker, scaled_weight.astype(BF16))
    taller = jnp.concatenate([taller, taller], 1)
    for each in range(8):
        weights[each * 256 : (each + 1) * 256, :] = jnp.where(
            lax.rem(row, 16) == 2 * each + lane // 128, taller, 0.0
        ).astype(BF16)
    mixed_ref[...] = jnp.zeros((32, 256), F32)

    def unload(block):
        slot = 0 if block == 2 else min(block, 2)
        return pltpu.make_async_copy(
            pairs.at[slot], grad_pair.at[pl.ds(block * 16, 16)], load_sem.at[block]
        )

    def pair_block(block):
        slot = 0 if block == 2 else min(block, 2)
        ours = pl.ds(block * 16, 16)
        dbias = own_bias[:, ours, :].reshape(256, 512).astype(F32)
        for part in range(4):
            wide_ref[part] = dbias[:, part * 128 : (part + 1) * 128]
        shrunk = dbias.reshape(HEADS, 16, 512) * inverse_ref[ours, :][None]
        turned_ref[...] = shrunk.reshape(256, 512).T.astype(BF16)

        def couple(index):
            left = jnp.concatenate(
                [
                    jnp.concatenate(
                        [wide_ref[part, pl.ds(2 * index + which, 16, stride=16), :] for part in range(4)], 1
                    )
                    for which in range(2)
                ],
                0,
            ).astype(BF16)
            mixed = mixed_ref[...]
            spread = weights[pl.ds(pl.multiple_of(index * 256, 256), 256), :]
            for part in range(4):
                rows = pl.ds(part * 128, 128)
                low = jnp.concatenate(
                    [pairs[slot, 2 * index, rows, :], pairs[slot, 2 * index + 1, rows, :]], 1
                )
                standard = low.astype(F32)
                scaled = dot(turned_ref[rows, :], spread)
                for which in range(2):
                    lanes = slice(which * 128, which * 128 + 128)
                    mine = standard[:, lanes]
                    along = jnp.sum(scaled[:, lanes] * mine, -1, keepdims=True) * (1.0 / 128)
                    pairs[slot, 2 * index + which, rows, :] = (scaled[:, lanes] - mine * along).astype(BF16)
                mixed = mixed + dot(left[:, part * 128 : (part + 1) * 128], low)
            mixed_ref[...] = mixed

        steps(8, couple)
        unload(block).start()

    wait_back(0)
    pair_block(0)
    pair_block(1)
    unload(0).wait()
    reload.start()
    wait_back(1)
    pair_block(3)

    for which in range(1, 4):
        send_dq(which).wait()
    for block in range(8):
        pieces = []
        for which in range(2):
            total = qo[samp, 2 * block + which, :SIZE, :].astype(F32)
            for other in range(3):
                total = total + dq_parts[other, 2 * block + which].astype(F32)
            pieces.append(total)
        turned = jnp.concatenate(pieces + [filler], 0).T.astype(BF16)
        for each in range(4):
            dq_sum[block % 4 * 4 + each, block // 4 * 32 : block // 4 * 32 + 32, :] = turned[
                each * 32 : each * 32 + 32
            ]

    @pl.when(high == half)
    def _():
        keep_dkv.wait()

    @pl.when(high != half)
    def _():
        send_dkv(0).wait_send()

    for which in range(1, 4):
        send_dkv(which).wait_send()
    for piece in range(2):
        for side in range(2):
            source = 2 * half + piece

            @pl.when(jnp.logical_not((source == samp) & (half == side)))
            def _():
                pltpu.make_async_remote_copy(
                    src_ref=packed.at[pl.ds(0, 4)],
                    dst_ref=dkv_parts.at[piece, side],
                    send_sem=part_out.at[4],
                    recv_sem=part_in.at[4 + 2 * piece + side],
                    device_id=(source, side * HEADS + head),
                    device_id_type=MESH,
                ).wait_recv()

    for piece in range(2):
        for which in range(2):
            for block in range(4):
                spot = (2 * which + block // 2, slice(block % 2 * 96, block % 2 * 96 + 96))
                total = dkv_parts[piece, 0, spot[0], spot[1], :].astype(F32)
                total = total + dkv_parts[piece, 1, spot[0], spot[1], :].astype(F32)
                dkv_sum[piece * 4 + block, which] = total.astype(BF16)

    def last_dq(step):
        peer = lax.rem(head + step, HEADS)
        return remote(
            dq_sum.at[peer], own_dq.at[head], last_out.at[0, step], last_in.at[0, step], samp, half, peer
        )

    def last_dkv(step):
        peer = lax.rem(head + step, HEADS)
        return remote(
            dkv_sum.at[peer // 2], own_dkv.at[head], last_out.at[1, step], last_in.at[1, step], samp, half, peer
        )

    steps(HEADS, lambda step: last_dq(step).start(), 1)
    steps(HEADS, lambda step: last_dkv(step).start(), 1)
    keep_dq = pltpu.make_async_copy(dq_sum.at[head], own_dq.at[head], own_sem.at[10])
    keep_last = pltpu.make_async_copy(dkv_sum.at[head // 2], own_dkv.at[head], own_sem.at[11])
    keep_dq.start()
    keep_last.start()

    reload.wait()
    pair_block(2)

    mine_ref[...] = mixed_ref[:16, :128] + mixed_ref[16:, 128:]

    def share(step):
        return remote(
            mine_ref, plane_parts.at[head], last_out.at[2, step], last_in.at[2, step],
            samp, half, lax.rem(head + step, HEADS),
        )

    steps(HEADS, lambda step: share(step).start(), 1)
    plane_parts[head] = mine_ref[...]
    steps(HEADS, lambda step: share(step).wait(), 1)
    spot = samp * 2 + half
    group_parts[spot] = sum(plane_parts[other] for other in range(HEADS))

    def share_group(apart):
        return remote(
            group_parts.at[spot], group_parts.at[spot], share_out.at[apart], share_in.at[apart],
            lax.rem(samp + apart % 4, 4), half if apart < 4 else 1 - half, head,
        )

    for apart in range(1, 8):
        share_group(apart).start()

    keep_dq.wait()
    keep_last.wait()
    steps(HEADS, lambda step: last_dq(step).wait(), 1)
    steps(HEADS, lambda step: last_dkv(step).wait(), 1)
    odd = lax.rem(head, 2) == 1
    for which in range(2):
        pieces = [own_dq[each, :, which * SIZE : which * SIZE + SIZE].astype(F32) for each in range(HEADS)]
        q_out[which] = jnp.concatenate(pieces, 1).astype(BF16)
        for out, source in ((k_out, own_dkv[:, which, :SIZE]), (v_out, own_dkv[:, which, SIZE:])):
            turned = source.reshape(HEADS * SIZE, 128).astype(F32).T
            out[which] = jnp.where(odd, turned[64:], turned[:64]).astype(BF16)
    for apart in range(1, 8):
        share_group(apart).wait()
    total = sum(group_parts[other] for other in range(8))
    gain_out[...] = jnp.sum(total * weight.astype(F32).T, 0, keepdims=True)
    weight_out[...] = (total * gain_row).T

    for part in range(2):
        send_kv(part, 1).wait_send()

        @pl.when(samp != 2 * half + part)
        def _():
            send_kv(part, 0).wait_send()

    def sent(sample):
        for apart in range(1, 4):
            stat_copy(sample, apart).wait_send()

    steps(8, sent)
    for block in (1, 2, 3):
        unload(block).wait()


def on_device(queries, keys, values, out_grad, pair_repr, norm_gain, bias_weight, token_mask):
    flat = [array.reshape(128, 768) for array in (queries, out_grad, keys, values)]
    sems = pltpu.SemaphoreType.DMA
    outs = pl.pallas_call(
        kernel,
        out_shape=(
            shape((64, 512, 128)),
            shape((2, 64, 768)),
            shape((2, 64, 768)),
            shape((2, 64, 768)),
            shape((128, HEADS), F32),
            shape((1, 128), F32),
            shape((16, 512, 128)),
        ),
        in_specs=[WHOLE] * 4 + [ANY] + [WHOLE] * 3,
        out_specs=[ANY] + [WHOLE] * 5 + [ANY],
        scratch_shapes=[
            pltpu.VMEM((HEADS, 4 * SIZE, 128), BF16),
            pltpu.VMEM((4, HEADS, 96, 128), BF16),
            pltpu.VMEM((4, 8, 96, 128), BF16),
            pltpu.VMEM((HEADS, 96, 128), BF16),
            pltpu.VMEM((1024, 512), BF16),
            pltpu.VMEM((HEADS, 64, 512), BF16),
            pltpu.VMEM((3, 16, 512, 128), BF16),
            pltpu.VMEM((512, 128), F32),
            pltpu.VMEM((64, 512), F32),
            pltpu.VMEM((8, 512, 1024), F32),
            pltpu.VMEM((8, 512, 1024), F32),
            pltpu.VMEM((512, 1024), F32),
            pltpu.VMEM((8, 1024, 128), BF16),
            pltpu.VMEM((8, 128, 512), BF16),
            pltpu.VMEM((8, 512, 128), BF16),
            pltpu.VMEM((512, 128), BF16),
            pltpu.VMEM((512, 128), BF16),
            pltpu.VMEM((512, 2048), BF16),
            pltpu.VMEM((8, 8, 1024), F32),
            pltpu.VMEM((4, 8, 8, 1024), F32),
            pltpu.VMEM((3, HEADS, SIZE, 128), BF16),
            pltpu.VMEM((2, 2, 4, 192, 128), BF16),
            pltpu.VMEM((HEADS, 64, 512), BF16),
            pltpu.VMEM((2048, 256), BF16),
            pltpu.VMEM((512, 256), BF16),
            pltpu.VMEM((4, 256, 128), F32),
            pltpu.VMEM((32, 256), F32),
            pltpu.VMEM((256, 256), BF16),
            pltpu.VMEM((256, 256), BF16),
            pltpu.VMEM((512, 128), F32),
            pltpu.VMEM((HEADS, 64, 128), BF16),
            pltpu.VMEM((8, 2, 96, 128), BF16),
            pltpu.VMEM((HEADS, 64, 128), BF16),
            pltpu.VMEM((HEADS, 2, 96, 128), BF16),
            pltpu.VMEM((HEADS, 128), F32),
            pltpu.VMEM((HEADS, HEADS, 128), F32),
            pltpu.VMEM((8, HEADS, 128), F32),
            sems((4,)),
            sems((2,)),
            sems((12,)),
            sems((2, 16)),
            sems((2, 16)),
            sems((4, 16)),
            sems((4, 16)),
            sems((8,)),
            sems((8,)),
            sems((8, 4)),
            sems((8, 4)),
            sems((8,)),
            sems((8,)),
            sems((2, 16)),
            sems((2, 16)),
            sems((3, 16)),
            sems((3, 16)),
            sems((8,)),
            sems((8,)),
        ],
        compiler_params=pltpu.CompilerParams(
            collective_id=0, has_side_effects=True, vmem_limit_bytes=63 * MIB
        ),
    )(*flat, pair_repr, norm_gain.reshape(1, 128), bias_weight, token_mask.reshape(1, 2048))
    grad_pair, grad_queries, grad_keys, grad_values, grad_weight, grad_gain, _ = outs
    return grad_queries, grad_keys, grad_values, grad_pair, grad_weight, grad_gain.reshape(128)


def solution(mesh):
    tokens = P("samp", "row", None)
    pairs = P("row", "samp", None)
    return jax.shard_map(
        on_device,
        mesh=mesh,
        in_specs=(tokens, tokens, tokens, tokens, pairs, P(), P(), P()),
        out_specs=(tokens, tokens, tokens, pairs, P(), P()),
        check_vma=False,
    )
```

```python
import functools
import math

import jax
import jax.numpy as jnp
from jax import lax
from jax.experimental import pallas as pl
from jax.experimental.pallas import tpu as pltpu
from jax.sharding import PartitionSpec as P

MESH = pl.DeviceIdType.MESH
F32 = jnp.float32
BF16 = jnp.bfloat16
LOG2E = math.log2(math.e)
MASKED = -1e9 * LOG2E
HEADS = 16
SIZE = 48
ANY = pl.BlockSpec(memory_space=pl.ANY)
WHOLE = pl.BlockSpec(memory_space=pltpu.VMEM)
MIB = 1024 * 1024


def shape(dims, dtype=BF16):
    return jax.ShapeDtypeStruct(dims, dtype)


def place():
    samp, row = lax.axis_index("samp"), lax.axis_index("row")
    return samp, row // HEADS, lax.rem(row, HEADS)


def remote(src, dst, send, recv, samp, half, head):
    return pltpu.make_async_remote_copy(
        src_ref=src,
        dst_ref=dst,
        send_sem=send,
        recv_sem=recv,
        device_id=(samp, half * HEADS + head),
        device_id_type=MESH,
    )


def dot(left, right):
    return jnp.dot(left, right, preferred_element_type=F32)


def untangle(first, second):
    first, second = first.astype(F32), second.astype(F32)
    low = lax.broadcasted_iota(jnp.int32, first.shape, 1) < 64
    return (
        jnp.where(low, first, pltpu.roll(second, 64, 1)),
        jnp.where(low, pltpu.roll(first, 64, 1), second),
    )


def steps(count, body, start=0, unroll=1):
    def wrapped(index, _):
        body(index)
        return 0

    lax.fori_loop(start, count, wrapped, 0, unroll=unroll)


def kernel(
    q_ref, o_ref, k_ref, v_ref, pair_ref, gain_ref, weight_ref, mask_ref,
    grad_pair, own_dq, own_dkv, weight_out, gain_out, spilled,
    packed, qo, kv, kv_near, all_bias, bias, pairs, inverse_wide, inverse_ref,
    raised_ref, along_ref, bias_t, qo_rows, kv_t, kv_rows, kept_ref, vals_ref,
    low_ref, tops, stats, dq_parts, dkv_parts, own_bias, weights, turned_ref, wide_ref, mixed_ref,
    centre_ref, mean_ref, keep_ref, dq_sum, dkv_sum, mine_ref, plane_parts, group_parts,
    load_sem, store_sem, own_sem, plane_out, plane_in, bias_out, bias_in, group_out, group_in,
    stat_out, stat_in, dq_out, dq_in, part_out, part_in, back_out, back_in, last_out, last_in, share_out, share_in,
):
    samp, half, head = place()
    core, high = lax.rem(samp, 2), samp // 2
    kin = (samp, high * 2 + 1 - core, (1 - high) * 2 + core, (1 - high) * 2 + 1 - core)
    inv_root = 1.0 / math.sqrt(SIZE)

    barrier = pltpu.get_barrier_semaphore()

    def hello(step):
        peer = lax.rem(head + step, HEADS)
        pl.semaphore_signal(barrier, inc=1, device_id=(samp, half * HEADS + peer), device_id_type=MESH)

    steps(HEADS, hello, 1)
    for apart in range(1, 8):
        side = half if apart < 4 else 1 - half
        pl.semaphore_signal(
            barrier, inc=1, device_id=(lax.rem(samp + apart, 4), side * HEADS + head), device_id_type=MESH
        )

    def load(block):
        return pltpu.make_async_copy(
            pair_ref.at[pl.ds(block * 16, 16)], pairs.at[min(block, 2)], load_sem.at[block]
        )

    spill = pltpu.make_async_copy(pairs.at[2], spilled, store_sem.at[0])
    reload = pltpu.make_async_copy(spilled, pairs.at[0], store_sem.at[1])

    for block in range(3):
        load(block).start()
    for part, ref in enumerate((k_ref, v_ref, q_ref, o_ref)):
        turned = ref[...].T
        for each in range(HEADS):
            packed[each, part * SIZE : (part + 1) * SIZE, :] = turned[each * SIZE : (each + 1) * SIZE]
    pl.semaphore_wait(barrier, 22)

    def copy_pack(step, which):
        peer = lax.rem(head + step, HEADS)
        land = qo.at[samp] if which else kv_near
        return remote(
            packed.at[peer, pl.ds(which * 96, 96)], land.at[head],
            plane_out.at[which, step], plane_in.at[which, step], samp, half, peer,
        )

    for which in range(2):
        steps(HEADS, lambda step: copy_pack(step, which).start(), 1)
    own_kv = pltpu.make_async_copy(packed.at[head, pl.ds(0, 96)], kv_near.at[head], own_sem.at[0])
    own_qo = pltpu.make_async_copy(packed.at[head, pl.ds(96, 96)], qo.at[samp, head], own_sem.at[1])
    own_kv.start()
    own_qo.start()

    row = lax.broadcasted_iota(jnp.int32, (256, 256), 0)
    lane = lax.broadcasted_iota(jnp.int32, (256, 256), 1)
    averager = jnp.where(row // 128 == lane // 128, 1.0 / 128, 0.0)
    mean_ref[...] = averager.astype(BF16)
    centre_ref[...] = (jnp.where(row == lane, 1.0, 0.0) - averager).astype(BF16)
    gain_row = gain_ref[...]
    gain = jnp.concatenate([gain_row, gain_row], 1)
    weight = weight_ref[...]
    chooser = (
        lax.broadcasted_iota(jnp.int32, (HEADS, 256), 1) // 16 == lax.broadcasted_iota(jnp.int32, (HEADS, 256), 0)
    ).astype(F32).astype(BF16)
    wider = dot(weight, chooser)
    lane_in = lax.rem(lax.broadcasted_iota(jnp.int32, (128, 256), 1), 16)
    for each in range(16):
        weights[each * 128 : (each + 1) * 128, :] = jnp.where(lane_in == each, wider, 0.0).astype(BF16)
    for part in range(4):
        at = pl.ds(pl.multiple_of(samp * 512 + part * 128, 128), 128)
        kept = (mask_ref[0:1, at] > 0).astype(F32)
        keep_ref[part * 128 : (part + 1) * 128, :] = jnp.broadcast_to(kept, (128, 128)).T

    narrow = lax.broadcasted_iota(jnp.int32, (128, 128), 1)

    def norm_block(block):
        slot = min(block, 2)
        load(block).wait()

        def couple(index):
            lanes = pl.ds(pl.multiple_of(index * 256, 256), 256)
            for part in range(4):
                rows = pl.ds(part * 128, 128)
                both = jnp.concatenate(
                    [pairs[slot, 2 * index, rows, :], pairs[slot, 2 * index + 1, rows, :]], 1
                )
                centred = dot(both, centre_ref[...])
                variance = dot((centred * centred).astype(BF16), mean_ref[...])
                inverse = lax.rsqrt(variance + 1e-05)
                standard = centred * inverse
                low = standard.astype(BF16)
                pairs[slot, 2 * index, rows, :] = low[:, :128]
                pairs[slot, 2 * index + 1, rows, :] = low[:, 128:]
                low_ref[rows, lanes] = (standard * gain).astype(BF16)
                old = jnp.where(narrow == 2 * index, inverse[:, :128], inverse_wide[rows, :])
                inverse_wide[rows, :] = jnp.where(narrow == 2 * index + 1, inverse[:, 128:], old)

        steps(8, couple, unroll=2)
        if block == 2:
            spill.start()
        rows = pl.ds(block * 16, 16)
        bias[:, rows, :] = dot(low_ref[...], weights[...]).T.reshape(HEADS, 16, 512).astype(BF16)
        inverse_ref[rows, :] = inverse_wide[...].T[:16]

    def bias_rows(block):
        return pl.ds(pl.multiple_of(block // 2 * 512 + head * 32 + block % 2 * 16, 16), 16)

    def copy_bias(block, step):
        return remote(
            bias.at[lax.rem(head + step, HEADS), pl.ds(block * 16, 16)], all_bias.at[bias_rows(block)],
            bias_out.at[block, step], bias_in.at[block, step], samp, half, lax.rem(head + step, HEADS),
        )

    def keep_bias(block):
        return pltpu.make_async_copy(
            bias.at[head, pl.ds(block * 16, 16)], all_bias.at[bias_rows(block)], own_sem.at[2 + block]
        )

    def start_bias(block):
        steps(HEADS, lambda step: copy_bias(block, step).start(), 1)
        keep_bias(block).start()

    def send_kv(part, across):
        return remote(
            kv_near.at[pl.ds(part * 8, 8)], kv.at[samp],
            group_out.at[4 + part * 2 + across], group_in.at[4 + samp],
            2 * half + part, 1 - half if across else half, head,
        )

    def keep_kv(part):
        return pltpu.make_async_copy(kv_near.at[pl.ds(part * 8, 8)], kv.at[samp], own_sem.at[6])

    def wait_kv(owner):
        here = jnp.logical_and(owner == samp, high == half)

        @pl.when(here)
        def _():
            pltpu.make_async_copy(kv_near.at[pl.ds(0, 8)], kv.at[owner], own_sem.at[6]).wait()

        @pl.when(jnp.logical_not(here))
        def _():
            pltpu.make_async_remote_copy(
                src_ref=kv_near.at[pl.ds(0, 8)],
                dst_ref=kv.at[owner],
                send_sem=group_out.at[4],
                recv_sem=group_in.at[4 + owner],
                device_id=(owner, high * HEADS + head),
                device_id_type=MESH,
            ).wait_recv()

    def send_qo(which):
        slot = kin[2] if which == 3 else samp
        to = kin[1] if which == 3 else kin[which]
        return remote(qo.at[slot], qo.at[slot], group_out.at[which], group_in.at[which], to, half, head)

    def wait_qo(which):
        slot = kin[which]
        remote(
            qo.at[slot], qo.at[slot], group_out.at[which], group_in.at[which],
            kin[1] if which == 3 else kin[which], half, head,
        ).wait_recv()

    norm_block(0)
    start_bias(0)
    steps(HEADS, lambda step: copy_pack(step, 0).wait(), 1)
    own_kv.wait()
    for part in range(2):
        send_kv(part, 1).start()
        mine = samp == 2 * half + part

        @pl.when(mine)
        def _():
            keep_kv(part).start()

        @pl.when(jnp.logical_not(mine))
        def _():
            send_kv(part, 0).start()

    norm_block(1)
    start_bias(1)
    steps(HEADS, lambda step: copy_pack(step, 1).wait(), 1)
    own_qo.wait()
    send_qo(2).start()
    send_qo(1).start()
    norm_block(2)
    start_bias(2)
    spill.wait()
    load(3).start()

    filler = jnp.zeros((32, 128), F32)

    def unpack_qo(owner):
        def body(peer):
            filled = jnp.concatenate([qo[owner, peer].astype(F32), filler], 0).T.astype(BF16)
            for which in range(2):
                for part in range(2):
                    at = pl.ds(pl.multiple_of(part * 512 + peer * 32, 32), 32)
                    start = which * 64 + part * 32
                    qo_rows[2 * owner + which, at, :] = filled[start : start + 32]

        steps(HEADS, body, unroll=2)

    def unpack_kv(owner):
        def body(pair):
            at = pl.ds(pl.multiple_of(pair * 128, 128), 128)
            both = untangle(kv[owner, 2 * pair], kv[owner, 2 * pair + 1])
            for which in range(2):
                filled = jnp.concatenate([both[which], filler], 0)
                kv_t[2 * owner + which, :, at] = filled.astype(BF16)
                kv_rows[2 * owner + which, at, :] = filled.T.astype(BF16)

        steps(4, body, unroll=2)

    unpack_qo(samp)
    norm_block(3)
    start_bias(3)
    wait_qo(2)
    send_qo(3).start()
    wait_kv(samp)
    unpack_kv(samp)

    def turn_bias(part):
        for block in (2 * part, 2 * part + 1):
            keep_bias(block).wait()
            steps(HEADS, lambda step: copy_bias(block, step).wait(), 1)

        def body(block):
            at = pl.ds(pl.multiple_of(part * 512 + block * 128, 128), 128)
            turned = all_bias[at, :].astype(F32).T * LOG2E
            bias_t[:, at] = jnp.where(keep_ref[...] > 0, turned, MASKED)

        steps(4, body)

    def stat_copy(sample, apart):
        return remote(
            stats.at[samp, sample], stats.at[samp, sample],
            stat_out.at[sample, apart], stat_in.at[sample, apart],
            lax.rem(samp + apart, 4), half, head,
        )

    wide = lax.broadcasted_iota(jnp.int32, (512, 128), 1)

    def first_pass(sample, block):
        both = kv_rows[sample]
        kept_ref[...] = jnp.where((wide < SIZE) & (keep_ref[...] > 0), both, 0).astype(BF16)
        vals_ref[...] = jnp.where(wide >= SIZE, both, 0).astype(BF16)
        at = pl.ds(pl.multiple_of(block * 512, 512), 512)
        right = qo_rows[sample, at, :].T
        partial = []
        for part in range(4):
            rows = pl.ds(part * 128, 128)
            score = dot(kept_ref[rows, :], right)
            along = dot(vals_ref[rows, :], right)
            score = score * (inv_root * LOG2E) + bias_t[rows, at]
            top = jnp.max(score, 0, keepdims=True)
            raised = jnp.exp2(score - top)
            raised_ref[sample, rows, at] = raised
            along_ref[sample, rows, at] = along
            tops[sample, part : part + 1, at] = top
            partial.append((top, jnp.sum(raised, 0, keepdims=True), jnp.sum(raised * along, 0, keepdims=True)))
        peak = functools.reduce(jnp.maximum, [p[0] for p in partial])
        scale = [jnp.exp2(p[0] - peak) for p in partial]
        stats[samp, sample, 0:1, at] = peak
        stats[samp, sample, 1:2, at] = sum(p[1] * w for p, w in zip(partial, scale))
        stats[samp, sample, 2:3, at] = sum(p[2] * w for p, w in zip(partial, scale))

    stats[samp] = jnp.zeros((8, 8, 1024), F32)
    for part in range(2):
        turn_bias(part)
        steps(2, lambda which: first_pass(2 * samp + which, part))
    for which in range(2):
        for apart in range(1, 4):
            stat_copy(2 * samp + which, apart).start()

    for which in range(1, 4):
        if which != 2:
            wait_qo(which)
        wait_kv(kin[which])
        unpack_qo(kin[which])
        unpack_kv(kin[which])

        def one(index):
            sample = 2 * kin[which] + index
            steps(2, lambda block: first_pass(sample, block))
            for apart in range(1, 4):
                stat_copy(sample, apart).start()

        steps(2, one)

    for which in range(1, 4):
        send_qo(which).wait_send()
    bias_t[...] = jnp.zeros((512, 1024), F32)

    def second_pass(owner, index, block):
        sample = 2 * owner + index

        def quarter(piece):
            at = pl.ds(pl.multiple_of(block * 512 + piece * 256, 256), 256)
            here = pl.ds(pl.multiple_of(piece * 256, 256), 256)
            after = pl.ds(pl.multiple_of(piece * 256 + 512, 256), 256)
            peaks = [stats[other, sample, 0:1, at] for other in range(4)]
            peak = functools.reduce(jnp.maximum, peaks)
            scale = [jnp.exp2(p - peak) for p in peaks]
            total = sum(stats[other, sample, 1:2, at] * scale[other] for other in range(4))
            blend = sum(stats[other, sample, 2:3, at] * scale[other] for other in range(4))
            share = 1.0 / total
            mean = blend * share
            for part in range(4):
                rows = pl.ds(part * 128, 128)
                factor = jnp.exp2(tops[sample, part : part + 1, at] - peak) * share
                probs = raised_ref[sample, rows, at] * factor
                grad = probs * (along_ref[sample, rows, at] - mean)
                bias_t[rows, at] += grad
                low_ref[rows, here] = probs.astype(BF16)
                low_ref[rows, after] = grad.astype(BF16)

        steps(2, quarter)
        right = qo_rows[sample, block * 512 : block * 512 + 512, :]
        dv = dot(low_ref[:, :512], right)
        dk = dot(low_ref[:, 512:1024], right)
        both = jnp.where(wide < SIZE, dk * inv_root, dv)
        if block == 0:
            raised_ref[sample, :, 0:128] = both
        else:
            turned = (both + raised_ref[sample, :, 0:128]).T
            for piece in range(4):
                packed[2 * sample + piece // 2, piece % 2 * 96 : piece % 2 * 96 + 96, :] = turned[
                    :96, piece * 128 : piece * 128 + 128
                ].astype(BF16)
        dq = (dot(kv_t[sample, :SIZE, :], low_ref[:, 512:1024]) * inv_root).astype(BF16)
        for piece in range(4):
            qo[owner, 2 * (block * 4 + piece) + index, :SIZE, :] = dq[:, piece * 128 : piece * 128 + 128]

    def send_dq(which, part):
        some = pl.ds(part * 8, 8)
        return remote(
            qo.at[kin[which], some, pl.ds(0, SIZE)], dq_parts.at[which - 1, some],
            dq_out.at[part, which], dq_in.at[part, which], kin[which], half, head,
        )

    def send_dkv(which):
        return remote(
            packed.at[pl.ds(4 * kin[which], 4)], dkv_parts.at[core, half],
            part_out.at[4 + which], part_in.at[4 + 2 * core + half], kin[which], high, head,
        )

    keep_dkv = pltpu.make_async_copy(packed.at[pl.ds(4 * samp, 4)], dkv_parts.at[core, half], own_sem.at[7])

    def send_back(peer, part):
        at = pl.ds(pl.multiple_of(part * 512 + peer * 32, 32), 32)
        return remote(
            all_bias.at[at], own_bias.at[head, pl.ds(part * 32, 32)],
            back_out.at[part, peer], back_in.at[part, head], samp, half, peer,
        )

    def keep_back(part):
        at = pl.ds(pl.multiple_of(part * 512 + head * 32, 32), 32)
        return pltpu.make_async_copy(
            all_bias.at[at], own_bias.at[head, pl.ds(part * 32, 32)], own_sem.at[8 + part]
        )

    def turn_back(part):
        def body(step):
            block = lax.rem(head // 4 + step, 4)
            at = pl.ds(pl.multiple_of(part * 512 + block * 128, 128), 128)
            all_bias[at, :] = bias_t[:, at].T.astype(BF16)

            def send(index):
                peer = 4 * block + lax.rem(head + index, 4)

                @pl.when(peer == head)
                def _():
                    keep_back(part).start()

                @pl.when(peer != head)
                def _():
                    send_back(peer, part).start()

            steps(4, send)

        steps(4, body)

    def wait_back(part):
        keep_back(part).wait()

        def body(step):
            other = lax.rem(head + step, HEADS)
            at = pl.ds(pl.multiple_of(part * 512 + other * 32, 32), 32)
            remote(
                all_bias.at[at], own_bias.at[other, pl.ds(part * 32, 32)],
                back_out.at[part, other], back_in.at[part, other], samp, half, other,
            ).wait()

        steps(HEADS, body, 1)

    for part in range(2):
        for which in (2, 3, 1, 0):
            def one(index):
                if part == 0:
                    for apart in range(1, 4):
                        stat_copy(2 * kin[which] + index, apart).wait_recv()
                second_pass(kin[which], index, part)

            steps(2, one)
            if which:
                if part == 1:
                    send_dkv(which).start()
                send_dq(which, part).start()
        turn_back(part)

    @pl.when(high == half)
    def _():
        keep_dkv.start()

    @pl.when(high != half)
    def _():
        send_dkv(0).start()

    scaled_weight = weight.astype(F32).T * gain_row
    scaled_weight = scaled_weight - jnp.mean(scaled_weight, -1, keepdims=True)
    picker = (
        lax.broadcasted_iota(jnp.int32, (256, HEADS), 0) // 16 == lax.broadcasted_iota(jnp.int32, (256, HEADS), 1)
    ).astype(F32).astype(BF16)
    taller = dot(picker, scaled_weight.astype(BF16))
    taller = jnp.concatenate([taller, taller], 1)
    for each in range(8):
        weights[each * 256 : (each + 1) * 256, :] = jnp.where(
            lax.rem(row, 16) == 2 * each + lane // 128, taller, 0.0
        ).astype(BF16)
    mixed_ref[...] = jnp.zeros((32, 256), F32)

    def unload(block):
        slot = 0 if block == 2 else min(block, 2)
        return pltpu.make_async_copy(
            pairs.at[slot], grad_pair.at[pl.ds(block * 16, 16)], load_sem.at[block]
        )

    def pair_block(block):
        slot = 0 if block == 2 else min(block, 2)
        ours = pl.ds(block * 16, 16)
        dbias = own_bias[:, ours, :].reshape(256, 512).astype(F32)
        for part in range(4):
            wide_ref[part] = dbias[:, part * 128 : (part + 1) * 128]
        shrunk = dbias.reshape(HEADS, 16, 512) * inverse_ref[ours, :][None]
        turned_ref[...] = shrunk.reshape(256, 512).T.astype(BF16)

        def couple(index):
            left = jnp.concatenate(
                [
                    jnp.concatenate(
                        [wide_ref[part, pl.ds(2 * index + which, 16, stride=16), :] for part in range(4)], 1
                    )
                    for which in range(2)
                ],
                0,
            ).astype(BF16)
            mixed = mixed_ref[...]
            spread = weights[pl.ds(pl.multiple_of(index * 256, 256), 256), :]
            for part in range(4):
                rows = pl.ds(part * 128, 128)
                low = jnp.concatenate(
                    [pairs[slot, 2 * index, rows, :], pairs[slot, 2 * index + 1, rows, :]], 1
                )
                standard = low.astype(F32)
                scaled = dot(turned_ref[rows, :], spread)
                for which in range(2):
                    lanes = slice(which * 128, which * 128 + 128)
                    mine = standard[:, lanes]
                    along = jnp.sum(scaled[:, lanes] * mine, -1, keepdims=True) * (1.0 / 128)
                    pairs[slot, 2 * index + which, rows, :] = (scaled[:, lanes] - mine * along).astype(BF16)
                mixed = mixed + dot(left[:, part * 128 : (part + 1) * 128], low)
            mixed_ref[...] = mixed

        steps(8, couple)
        unload(block).start()

    wait_back(0)
    pair_block(0)
    pair_block(1)
    unload(0).wait()
    reload.start()
    wait_back(1)
    pair_block(3)
    reload.wait()
    pair_block(2)

    mine_ref[...] = mixed_ref[:16, :128] + mixed_ref[16:, 128:]

    def share(step):
        return remote(
            mine_ref, plane_parts.at[head], last_out.at[2, step], last_in.at[2, step],
            samp, half, lax.rem(head + step, HEADS),
        )

    steps(HEADS, lambda step: share(step).start(), 1)
    plane_parts[head] = mine_ref[...]

    for part in range(2):
        for which in range(1, 4):
            send_dq(which, part).wait()
    for block in range(8):
        pieces = []
        for which in range(2):
            total = qo[samp, 2 * block + which, :SIZE, :].astype(F32)
            for other in range(3):
                total = total + dq_parts[other, 2 * block + which].astype(F32)
            pieces.append(total)
        turned = jnp.concatenate(pieces + [filler], 0).T.astype(BF16)
        for each in range(4):
            dq_sum[block % 4 * 4 + each, block // 4 * 32 : block // 4 * 32 + 32, :] = turned[
                each * 32 : each * 32 + 32
            ]

    @pl.when(high == half)
    def _():
        keep_dkv.wait()

    @pl.when(high != half)
    def _():
        send_dkv(0).wait_send()

    for which in range(1, 4):
        send_dkv(which).wait_send()
    for piece in range(2):
        for side in range(2):
            source = 2 * half + piece

            @pl.when(jnp.logical_not((source == samp) & (half == side)))
            def _():
                pltpu.make_async_remote_copy(
                    src_ref=packed.at[pl.ds(0, 4)],
                    dst_ref=dkv_parts.at[piece, side],
                    send_sem=part_out.at[4],
                    recv_sem=part_in.at[4 + 2 * piece + side],
                    device_id=(source, side * HEADS + head),
                    device_id_type=MESH,
                ).wait_recv()

    for piece in range(2):
        for which in range(2):
            for block in range(4):
                spot = (2 * which + block // 2, slice(block % 2 * 96, block % 2 * 96 + 96))
                total = dkv_parts[piece, 0, spot[0], spot[1], :].astype(F32)
                total = total + dkv_parts[piece, 1, spot[0], spot[1], :].astype(F32)
                dkv_sum[piece * 4 + block, which] = total.astype(BF16)

    def last_dq(step):
        peer = lax.rem(head + step, HEADS)
        return remote(
            dq_sum.at[peer], own_dq.at[head], last_out.at[0, step], last_in.at[0, step], samp, half, peer
        )

    def last_dkv(step):
        peer = lax.rem(head + step, HEADS)
        return remote(
            dkv_sum.at[peer // 2], own_dkv.at[head], last_out.at[1, step], last_in.at[1, step], samp, half, peer
        )

    steps(HEADS, lambda step: last_dq(step).start(), 1)
    steps(HEADS, lambda step: last_dkv(step).start(), 1)
    keep_dq = pltpu.make_async_copy(dq_sum.at[head], own_dq.at[head], own_sem.at[10])
    keep_last = pltpu.make_async_copy(dkv_sum.at[head // 2], own_dkv.at[head], own_sem.at[11])
    keep_dq.start()
    keep_last.start()

    steps(HEADS, lambda step: share(step).wait(), 1)
    spot = samp * 2 + half
    group_parts[spot] = sum(plane_parts[other] for other in range(HEADS))

    def share_group(apart):
        return remote(
            group_parts.at[spot], group_parts.at[spot], share_out.at[apart], share_in.at[apart],
            lax.rem(samp + apart % 4, 4), half if apart < 4 else 1 - half, head,
        )

    for apart in range(1, 8):
        share_group(apart).start()

    for apart in range(1, 8):
        share_group(apart).wait()
    total = sum(group_parts[other] for other in range(8))
    gain_out[...] = jnp.sum(total * weight.astype(F32).T, 0, keepdims=True)
    weight_out[...] = (total * gain_row).T
    keep_dq.wait()
    keep_last.wait()
    steps(HEADS, lambda step: last_dq(step).wait(), 1)
    steps(HEADS, lambda step: last_dkv(step).wait(), 1)
    for part in range(2):
        send_kv(part, 1).wait_send()

        @pl.when(samp != 2 * half + part)
        def _():
            send_kv(part, 0).wait_send()

    def sent(sample):
        for apart in range(1, 4):
            stat_copy(sample, apart).wait_send()

    steps(8, sent)
    for block in (1, 2, 3):
        unload(block).wait()


def deliver_kernel(
    pair_ref, dq_ref, dkv_ref, weight_ref, gain_ref, pair_out, q_out, k_out, v_out, weight_out, gain_out
):
    pair_out[...] = pair_ref[...]
    step = pl.program_id(0)

    @pl.when(step == 0)
    def _():
        weight_out[...] = weight_ref[...]
        gain_out[...] = gain_ref[...]

    for which in range(2):
        @pl.when(step == which + 1)
        def _():
            pieces = [dq_ref[each, :, which * SIZE : which * SIZE + SIZE].astype(F32) for each in range(HEADS)]
            q_out[which] = jnp.concatenate(pieces, 1).astype(BF16)

        for at, (out, rows) in enumerate(((k_out, slice(0, SIZE)), (v_out, slice(SIZE, 2 * SIZE)))):
            @pl.when(step == 3 + 2 * at + which)
            def _():
                odd = lax.rem(lax.axis_index("row"), 2) == 1
                turned = dkv_ref[:, which, rows].reshape(HEADS * SIZE, 128).astype(F32).T
                out[which] = jnp.where(odd, turned[64:], turned[:64]).astype(BF16)


def on_device(queries, keys, values, out_grad, pair_repr, norm_gain, bias_weight, token_mask):
    flat = [array.reshape(128, 768) for array in (queries, out_grad, keys, values)]
    sems = pltpu.SemaphoreType.DMA
    outs = pl.pallas_call(
        kernel,
        out_shape=(
            shape((64, 512, 128)),
            shape((HEADS, 64, 128)),
            shape((HEADS, 2, 96, 128)),
            shape((128, HEADS), F32),
            shape((1, 128), F32),
            shape((16, 512, 128)),
        ),
        in_specs=[WHOLE] * 4 + [ANY] + [WHOLE] * 3,
        out_specs=[ANY] * 3 + [WHOLE] * 2 + [ANY],
        scratch_shapes=[
            pltpu.VMEM((HEADS, 4 * SIZE, 128), BF16),
            pltpu.VMEM((4, HEADS, 96, 128), BF16),
            pltpu.VMEM((4, 8, 96, 128), BF16),
            pltpu.VMEM((HEADS, 96, 128), BF16),
            pltpu.VMEM((1024, 512), BF16),
            pltpu.VMEM((HEADS, 64, 512), BF16),
            pltpu.VMEM((3, 16, 512, 128), BF16),
            pltpu.VMEM((512, 128), F32),
            pltpu.VMEM((64, 512), F32),
            pltpu.VMEM((8, 512, 1024), F32),
            pltpu.VMEM((8, 512, 1024), F32),
            pltpu.VMEM((512, 1024), F32),
            pltpu.VMEM((8, 1024, 128), BF16),
            pltpu.VMEM((8, 128, 512), BF16),
            pltpu.VMEM((8, 512, 128), BF16),
            pltpu.VMEM((512, 128), BF16),
            pltpu.VMEM((512, 128), BF16),
            pltpu.VMEM((512, 2048), BF16),
            pltpu.VMEM((8, 8, 1024), F32),
            pltpu.VMEM((4, 8, 8, 1024), F32),
            pltpu.VMEM((3, HEADS, SIZE, 128), BF16),
            pltpu.VMEM((2, 2, 4, 192, 128), BF16),
            pltpu.VMEM((HEADS, 64, 512), BF16),
            pltpu.VMEM((2048, 256), BF16),
            pltpu.VMEM((512, 256), BF16),
            pltpu.VMEM((4, 256, 128), F32),
            pltpu.VMEM((32, 256), F32),
            pltpu.VMEM((256, 256), BF16),
            pltpu.VMEM((256, 256), BF16),
            pltpu.VMEM((512, 128), F32),
            pltpu.VMEM((HEADS, 64, 128), BF16),
            pltpu.VMEM((8, 2, 96, 128), BF16),
            pltpu.VMEM((HEADS, 128), F32),
            pltpu.VMEM((HEADS, HEADS, 128), F32),
            pltpu.VMEM((8, HEADS, 128), F32),
            sems((4,)),
            sems((2,)),
            sems((12,)),
            sems((2, 16)),
            sems((2, 16)),
            sems((4, 16)),
            sems((4, 16)),
            sems((8,)),
            sems((8,)),
            sems((8, 4)),
            sems((8, 4)),
            sems((2, 4)),
            sems((2, 4)),
            sems((8,)),
            sems((8,)),
            sems((2, 16)),
            sems((2, 16)),
            sems((3, 16)),
            sems((3, 16)),
            sems((8,)),
            sems((8,)),
        ],
        compiler_params=pltpu.CompilerParams(
            collective_id=0, has_side_effects=True, vmem_limit_bytes=63 * MIB
        ),
    )(*flat, pair_repr, norm_gain.reshape(1, 128), bias_weight, token_mask.reshape(1, 2048))
    near_pair, near_dq, near_dkv, near_weight, near_gain, _ = outs
    fixed = lambda *dims: pl.BlockSpec(dims, lambda i: (0,) * len(dims))
    grad_pair, grad_queries, grad_keys, grad_values, grad_weight, grad_gain = pl.pallas_call(
        deliver_kernel,
        grid=(8,),
        out_shape=(
            shape((64, 512, 128)),
            shape((2, 64, 768)),
            shape((2, 64, 768)),
            shape((2, 64, 768)),
            shape((128, HEADS), F32),
            shape((1, 128), F32),
        ),
        in_specs=[
            pl.BlockSpec((8, 512, 128), lambda i: (i, 0, 0)),
            fixed(HEADS, 64, 128),
            fixed(HEADS, 2, 96, 128),
            fixed(128, HEADS),
            fixed(1, 128),
        ],
        out_specs=[pl.BlockSpec((8, 512, 128), lambda i: (i, 0, 0))]
        + [fixed(2, 64, 768)] * 3
        + [fixed(128, HEADS), fixed(1, 128)],
        compiler_params=pltpu.CompilerParams(vmem_limit_bytes=60 * MIB),
    )(near_pair, near_dq, near_dkv, near_weight, near_gain)
    return grad_queries, grad_keys, grad_values, grad_pair, grad_weight, grad_gain.reshape(128)


def solution(mesh):
    tokens = P("samp", "row", None)
    pairs = P("row", "samp", None)
    return jax.shard_map(
        on_device,
        mesh=mesh,
        in_specs=(tokens, tokens, tokens, tokens, pairs, P(), P(), P()),
        out_specs=(tokens, tokens, tokens, pairs, P(), P()),
        check_vma=False,
    )
```

```python
import functools
import math

import jax
import jax.numpy as jnp
from jax import lax
from jax.experimental import pallas as pl
from jax.experimental.pallas import tpu as pltpu
from jax.sharding import PartitionSpec as P

MESH = pl.DeviceIdType.MESH
F32 = jnp.float32
BF16 = jnp.bfloat16
LOG2E = math.log2(math.e)
MASKED = -1e9 * LOG2E
HEADS = 16
SIZE = 48
ANY = pl.BlockSpec(memory_space=pl.ANY)
WHOLE = pl.BlockSpec(memory_space=pltpu.VMEM)
MIB = 1024 * 1024


def shape(dims, dtype=BF16):
    return jax.ShapeDtypeStruct(dims, dtype)


def place():
    samp, row = lax.axis_index("samp"), lax.axis_index("row")
    return samp, row // HEADS, lax.rem(row, HEADS)


def remote(src, dst, send, recv, samp, half, head):
    return pltpu.make_async_remote_copy(
        src_ref=src,
        dst_ref=dst,
        send_sem=send,
        recv_sem=recv,
        device_id=(samp, half * HEADS + head),
        device_id_type=MESH,
    )


def dot(left, right):
    return jnp.dot(left, right, preferred_element_type=F32)


def untangle(first, second):
    first, second = first.astype(F32), second.astype(F32)
    low = lax.broadcasted_iota(jnp.int32, first.shape, 1) < 64
    return (
        jnp.where(low, first, pltpu.roll(second, 64, 1)),
        jnp.where(low, pltpu.roll(first, 64, 1), second),
    )


def steps(count, body, start=0, unroll=1):
    def wrapped(index, _):
        body(index)
        return 0

    lax.fori_loop(start, count, wrapped, 0, unroll=unroll)


def kernel(
    q_ref, o_ref, k_ref, v_ref, pair_ref, gain_ref, weight_ref, mask_ref,
    grad_pair, own_dq, own_dkv, weight_out, gain_out, spilled,
    packed, qo, kv, kv_near, all_bias, bias, pairs, inverse_wide, inverse_ref,
    raised_ref, along_ref, bias_t, qo_rows, kv_t, kv_rows, kept_ref, vals_ref,
    low_ref, tops, stats, dq_parts, dkv_parts, own_bias, weights, turned_ref, wide_ref, mixed_ref,
    centre_ref, mean_ref, keep_ref, dq_sum, dkv_sum, mine_ref, plane_parts, group_parts,
    load_sem, store_sem, own_sem, plane_out, plane_in, bias_out, bias_in, group_out, group_in,
    stat_out, stat_in, dq_out, dq_in, part_out, part_in, back_out, back_in, last_out, last_in, share_out, share_in,
):
    samp, half, head = place()
    core, high = lax.rem(samp, 2), samp // 2
    kin = (samp, high * 2 + 1 - core, (1 - high) * 2 + core, (1 - high) * 2 + 1 - core)
    inv_root = 1.0 / math.sqrt(SIZE)

    barrier = pltpu.get_barrier_semaphore()

    def hello(step):
        peer = lax.rem(head + step, HEADS)
        pl.semaphore_signal(barrier, inc=1, device_id=(samp, half * HEADS + peer), device_id_type=MESH)

    steps(HEADS, hello, 1)
    for apart in range(1, 8):
        side = half if apart < 4 else 1 - half
        pl.semaphore_signal(
            barrier, inc=1, device_id=(lax.rem(samp + apart, 4), side * HEADS + head), device_id_type=MESH
        )

    def load(block):
        return pltpu.make_async_copy(
            pair_ref.at[pl.ds(block * 16, 16)], pairs.at[min(block, 2)], load_sem.at[block]
        )

    spill = pltpu.make_async_copy(pairs.at[2], spilled, store_sem.at[0])
    reload = pltpu.make_async_copy(spilled, pairs.at[0], store_sem.at[1])

    for block in range(3):
        load(block).start()
    for part, ref in enumerate((k_ref, v_ref, q_ref, o_ref)):
        turned = ref[...].T
        for each in range(HEADS):
            packed[each, part * SIZE : (part + 1) * SIZE, :] = turned[each * SIZE : (each + 1) * SIZE]
    pl.semaphore_wait(barrier, 22)

    def copy_pack(step, which):
        peer = lax.rem(head + step, HEADS)
        land = qo.at[samp] if which else kv_near
        return remote(
            packed.at[peer, pl.ds(which * 96, 96)], land.at[head],
            plane_out.at[which, step], plane_in.at[which, step], samp, half, peer,
        )

    for which in range(2):
        steps(HEADS, lambda step: copy_pack(step, which).start(), 1)
    own_kv = pltpu.make_async_copy(packed.at[head, pl.ds(0, 96)], kv_near.at[head], own_sem.at[0])
    own_qo = pltpu.make_async_copy(packed.at[head, pl.ds(96, 96)], qo.at[samp, head], own_sem.at[1])
    own_kv.start()
    own_qo.start()

    row = lax.broadcasted_iota(jnp.int32, (256, 256), 0)
    lane = lax.broadcasted_iota(jnp.int32, (256, 256), 1)
    averager = jnp.where(row // 128 == lane // 128, 1.0 / 128, 0.0)
    mean_ref[...] = averager.astype(BF16)
    centre_ref[...] = (jnp.where(row == lane, 1.0, 0.0) - averager).astype(BF16)
    gain_row = gain_ref[...]
    gain = jnp.concatenate([gain_row, gain_row], 1)
    weight = weight_ref[...].astype(F32)
    chooser = (
        lax.broadcasted_iota(jnp.int32, (HEADS, 256), 1) // 16 == lax.broadcasted_iota(jnp.int32, (HEADS, 256), 0)
    ).astype(F32).astype(BF16)
    wider = dot(weight.T.astype(BF16), chooser)
    lane_in = lax.rem(lax.broadcasted_iota(jnp.int32, (128, 256), 1), 16)
    for each in range(16):
        weights[each * 128 : (each + 1) * 128, :] = jnp.where(lane_in == each, wider, 0.0).astype(BF16)
    for part in range(4):
        at = pl.ds(pl.multiple_of(samp * 512 + part * 128, 128), 128)
        kept = (mask_ref[0:1, at] > 0).astype(F32)
        keep_ref[part * 128 : (part + 1) * 128, :] = jnp.broadcast_to(kept, (128, 128)).T

    narrow = lax.broadcasted_iota(jnp.int32, (128, 128), 1)

    def norm_block(block):
        slot = min(block, 2)
        load(block).wait()

        def couple(index):
            lanes = pl.ds(pl.multiple_of(index * 256, 256), 256)
            for part in range(4):
                rows = pl.ds(part * 128, 128)
                both = jnp.concatenate(
                    [pairs[slot, 2 * index, rows, :], pairs[slot, 2 * index + 1, rows, :]], 1
                )
                centred = dot(both, centre_ref[...])
                variance = dot((centred * centred).astype(BF16), mean_ref[...])
                inverse = lax.rsqrt(variance + 1e-05)
                standard = centred * inverse
                low = standard.astype(BF16)
                pairs[slot, 2 * index, rows, :] = low[:, :128]
                pairs[slot, 2 * index + 1, rows, :] = low[:, 128:]
                low_ref[rows, lanes] = (standard * gain).astype(BF16)
                old = jnp.where(narrow == 2 * index, inverse[:, :128], inverse_wide[rows, :])
                inverse_wide[rows, :] = jnp.where(narrow == 2 * index + 1, inverse[:, 128:], old)

        steps(8, couple, unroll=2)
        if block == 2:
            spill.start()
        rows = pl.ds(block * 16, 16)
        bias[:, rows, :] = dot(low_ref[...], weights[...]).T.reshape(HEADS, 16, 512).astype(BF16)
        inverse_ref[rows, :] = inverse_wide[...].T[:16]

    def bias_rows(block):
        return pl.ds(pl.multiple_of(block // 2 * 512 + head * 32 + block % 2 * 16, 16), 16)

    def copy_bias(block, step):
        return remote(
            bias.at[lax.rem(head + step, HEADS), pl.ds(block * 16, 16)], all_bias.at[bias_rows(block)],
            bias_out.at[block, step], bias_in.at[block, step], samp, half, lax.rem(head + step, HEADS),
        )

    def keep_bias(block):
        return pltpu.make_async_copy(
            bias.at[head, pl.ds(block * 16, 16)], all_bias.at[bias_rows(block)], own_sem.at[2 + block]
        )

    def start_bias(block):
        steps(HEADS, lambda step: copy_bias(block, step).start(), 1)
        keep_bias(block).start()

    def send_kv(part, across):
        return remote(
            kv_near.at[pl.ds(part * 8, 8)], kv.at[samp],
            group_out.at[4 + part * 2 + across], group_in.at[4 + samp],
            2 * half + part, 1 - half if across else half, head,
        )

    def keep_kv(part):
        return pltpu.make_async_copy(kv_near.at[pl.ds(part * 8, 8)], kv.at[samp], own_sem.at[6])

    def wait_kv(owner):
        here = jnp.logical_and(owner == samp, high == half)

        @pl.when(here)
        def _():
            pltpu.make_async_copy(kv_near.at[pl.ds(0, 8)], kv.at[owner], own_sem.at[6]).wait()

        @pl.when(jnp.logical_not(here))
        def _():
            pltpu.make_async_remote_copy(
                src_ref=kv_near.at[pl.ds(0, 8)],
                dst_ref=kv.at[owner],
                send_sem=group_out.at[4],
                recv_sem=group_in.at[4 + owner],
                device_id=(owner, high * HEADS + head),
                device_id_type=MESH,
            ).wait_recv()

    def send_qo(which):
        slot = kin[2] if which == 3 else samp
        to = kin[1] if which == 3 else kin[which]
        return remote(qo.at[slot], qo.at[slot], group_out.at[which], group_in.at[which], to, half, head)

    def wait_qo(which):
        slot = kin[which]
        remote(
            qo.at[slot], qo.at[slot], group_out.at[which], group_in.at[which],
            kin[1] if which == 3 else kin[which], half, head,
        ).wait_recv()

    norm_block(0)
    start_bias(0)
    steps(HEADS, lambda step: copy_pack(step, 0).wait(), 1)
    own_kv.wait()
    for part in range(2):
        send_kv(part, 1).start()
        mine = samp == 2 * half + part

        @pl.when(mine)
        def _():
            keep_kv(part).start()

        @pl.when(jnp.logical_not(mine))
        def _():
            send_kv(part, 0).start()

    norm_block(1)
    start_bias(1)
    steps(HEADS, lambda step: copy_pack(step, 1).wait(), 1)
    own_qo.wait()
    send_qo(2).start()
    send_qo(1).start()
    norm_block(2)
    start_bias(2)
    spill.wait()
    load(3).start()

    filler = jnp.zeros((32, 128), F32)

    def unpack_qo(owner):
        def body(peer):
            filled = jnp.concatenate([qo[owner, peer].astype(F32), filler], 0).T.astype(BF16)
            for which in range(2):
                for part in range(2):
                    at = pl.ds(pl.multiple_of(part * 512 + peer * 32, 32), 32)
                    start = which * 64 + part * 32
                    qo_rows[2 * owner + which, at, :] = filled[start : start + 32]

        steps(HEADS, body, unroll=2)

    def unpack_kv(owner):
        def body(pair):
            at = pl.ds(pl.multiple_of(pair * 128, 128), 128)
            both = untangle(kv[owner, 2 * pair], kv[owner, 2 * pair + 1])
            for which in range(2):
                filled = jnp.concatenate([both[which], filler], 0)
                kv_t[2 * owner + which, :, at] = filled.astype(BF16)
                kv_rows[2 * owner + which, at, :] = filled.T.astype(BF16)

        steps(4, body, unroll=2)

    unpack_qo(samp)
    norm_block(3)
    start_bias(3)
    wait_qo(2)
    send_qo(3).start()
    wait_kv(samp)
    unpack_kv(samp)

    def turn_bias(part):
        for block in (2 * part, 2 * part + 1):
            keep_bias(block).wait()
            steps(HEADS, lambda step: copy_bias(block, step).wait(), 1)

        def body(block):
            at = pl.ds(pl.multiple_of(part * 512 + block * 128, 128), 128)
            turned = all_bias[at, :].astype(F32).T * LOG2E
            bias_t[:, at] = jnp.where(keep_ref[...] > 0, turned, MASKED)

        steps(4, body)

    def stat_copy(sample, apart):
        return remote(
            stats.at[samp, sample], stats.at[samp, sample],
            stat_out.at[sample, apart], stat_in.at[sample, apart],
            lax.rem(samp + apart, 4), half, head,
        )

    wide = lax.broadcasted_iota(jnp.int32, (512, 128), 1)

    def first_pass(sample, block):
        both = kv_rows[sample]
        kept_ref[...] = jnp.where((wide < SIZE) & (keep_ref[...] > 0), both, 0).astype(BF16)
        vals_ref[...] = jnp.where(wide >= SIZE, both, 0).astype(BF16)
        at = pl.ds(pl.multiple_of(block * 512, 512), 512)
        right = qo_rows[sample, at, :].T
        partial = []
        for part in range(4):
            rows = pl.ds(part * 128, 128)
            score = dot(kept_ref[rows, :], right)
            along = dot(vals_ref[rows, :], right)
            score = score * (inv_root * LOG2E) + bias_t[rows, at]
            top = jnp.max(score, 0, keepdims=True)
            raised = jnp.exp2(score - top)
            raised_ref[sample, rows, at] = raised
            along_ref[sample, rows, at] = along
            tops[sample, part : part + 1, at] = top
            partial.append((top, jnp.sum(raised, 0, keepdims=True), jnp.sum(raised * along, 0, keepdims=True)))
        peak = functools.reduce(jnp.maximum, [p[0] for p in partial])
        scale = [jnp.exp2(p[0] - peak) for p in partial]
        stats[samp, sample, 0:1, at] = peak
        stats[samp, sample, 1:2, at] = sum(p[1] * w for p, w in zip(partial, scale))
        stats[samp, sample, 2:3, at] = sum(p[2] * w for p, w in zip(partial, scale))

    stats[samp] = jnp.zeros((8, 8, 1024), F32)
    for part in range(2):
        turn_bias(part)
        steps(2, lambda which: first_pass(2 * samp + which, part))
    for which in range(2):
        for apart in range(1, 4):
            stat_copy(2 * samp + which, apart).start()

    for which in range(1, 4):
        if which != 2:
            wait_qo(which)
        wait_kv(kin[which])
        unpack_qo(kin[which])
        unpack_kv(kin[which])

        def one(index):
            sample = 2 * kin[which] + index
            steps(2, lambda block: first_pass(sample, block))
            for apart in range(1, 4):
                stat_copy(sample, apart).start()

        steps(2, one)

    for which in range(1, 4):
        send_qo(which).wait_send()
    bias_t[...] = jnp.zeros((512, 1024), F32)

    def kin_of(which):
        across, over = lax.rem(which, 2), which // 2
        return (high + over - 2 * high * over) * 2 + core + across - 2 * core * across

    def second_pass(owner, block):
        both = [None, None]
        for piece in range(2):
            start = block * 512 + piece * 256
            at = slice(start, start + 256)
            scales = []
            for index in range(2):
                sample = 2 * owner + index
                peaks = [stats[other, sample, 0:1, at] for other in range(4)]
                peak = functools.reduce(jnp.maximum, peaks)
                scale = [jnp.exp2(p - peak) for p in peaks]
                total = sum(stats[other, sample, 1:2, at] * scale[other] for other in range(4))
                blend = sum(stats[other, sample, 2:3, at] * scale[other] for other in range(4))
                share = 1.0 / total
                scales.append((peak, share, blend * share))
            for part in range(4):
                rows = pl.ds(part * 128, 128)
                grads = []
                for index in range(2):
                    sample = 2 * owner + index
                    peak, share, mean = scales[index]
                    factor = jnp.exp2(tops[sample, part : part + 1, at] - peak) * share
                    probs = raised_ref[sample, rows, at] * factor
                    grad = probs * (along_ref[sample, rows, at] - mean)
                    grads.append(grad)
                    spot = index * 1024 + piece * 256
                    low_ref[rows, spot : spot + 256] = probs.astype(BF16)
                    low_ref[rows, spot + 512 : spot + 768] = grad.astype(BF16)
                bias_t[rows, at] += grads[0] + grads[1]
            for index in range(2):
                sample = 2 * owner + index
                spot = index * 1024 + piece * 256
                right = qo_rows[sample, at, :]
                dv = dot(low_ref[:, spot : spot + 256], right)
                dk = dot(low_ref[:, spot + 512 : spot + 768], right)
                here = jnp.where(wide < SIZE, dk * inv_root, dv)
                both[index] = here if piece == 0 else both[index] + here
                dq = (dot(kv_t[sample, :SIZE, :], low_ref[:, spot + 512 : spot + 768]) * inv_root).astype(BF16)
                for side in range(2):
                    qo[owner, 2 * (block * 4 + piece * 2 + side) + index, :SIZE, :] = dq[
                        :, side * 128 : side * 128 + 128
                    ]
        for index in range(2):
            sample = 2 * owner + index
            if block == 0:
                raised_ref[sample, :, 0:128] = both[index]
            else:
                turned = (both[index] + raised_ref[sample, :, 0:128]).T
                for piece in range(4):
                    packed[2 * sample + piece // 2, piece % 2 * 96 : piece % 2 * 96 + 96, :] = turned[
                        :96, piece * 128 : piece * 128 + 128
                    ].astype(BF16)

    def send_dq(which, part):
        some = pl.ds(part * 8, 8)
        return remote(
            qo.at[kin_of(which), some, pl.ds(0, SIZE)], dq_parts.at[which - 1, some],
            dq_out.at[part, which], dq_in.at[part, which], kin_of(which), half, head,
        )

    def send_dkv(which):
        return remote(
            packed.at[pl.ds(4 * kin_of(which), 4)], dkv_parts.at[core, half],
            part_out.at[4 + which], part_in.at[4 + 2 * core + half], kin_of(which), high, head,
        )

    keep_dkv = pltpu.make_async_copy(packed.at[pl.ds(4 * samp, 4)], dkv_parts.at[core, half], own_sem.at[7])

    def send_back(peer, part):
        at = pl.ds(pl.multiple_of(part * 512 + peer * 32, 32), 32)
        return remote(
            all_bias.at[at], own_bias.at[head, pl.ds(part * 32, 32)],
            back_out.at[part, peer], back_in.at[part, head], samp, half, peer,
        )

    def keep_back(part):
        at = pl.ds(pl.multiple_of(part * 512 + head * 32, 32), 32)
        return pltpu.make_async_copy(
            all_bias.at[at], own_bias.at[head, pl.ds(part * 32, 32)], own_sem.at[8 + part]
        )

    def turn_back(part):
        def body(step):
            block = lax.rem(head // 4 + step, 4)
            at = pl.ds(pl.multiple_of(part * 512 + block * 128, 128), 128)
            all_bias[at, :] = bias_t[:, at].T.astype(BF16)

            def send(index):
                peer = 4 * block + lax.rem(head + index, 4)

                @pl.when(peer == head)
                def _():
                    keep_back(part).start()

                @pl.when(peer != head)
                def _():
                    send_back(peer, part).start()

            steps(4, send)

        steps(4, body)

    def wait_back(part):
        keep_back(part).wait()

        def body(step):
            other = lax.rem(head + step, HEADS)
            at = pl.ds(pl.multiple_of(part * 512 + other * 32, 32), 32)
            remote(
                all_bias.at[at], own_bias.at[other, pl.ds(part * 32, 32)],
                back_out.at[part, other], back_in.at[part, other], samp, half, other,
            ).wait()

        steps(HEADS, body, 1)

    for part in range(2):
        def pair_body(step):
            which = 3 - step
            owner = kin_of(which)
            if part == 0:
                for index in range(2):
                    for apart in range(1, 4):
                        stat_copy(2 * owner + index, apart).wait_recv()
            second_pass(owner, part)

            @pl.when(which > 0)
            def _():
                if part == 1:
                    send_dkv(which).start()
                send_dq(which, part).start()

        steps(4, pair_body)
        turn_back(part)

    @pl.when(high == half)
    def _():
        keep_dkv.start()

    @pl.when(high != half)
    def _():
        send_dkv(0).start()

    scaled_weight = weight * gain_row
    scaled_weight = scaled_weight - jnp.mean(scaled_weight, -1, keepdims=True)
    picker = (
        lax.broadcasted_iota(jnp.int32, (256, HEADS), 0) // 16 == lax.broadcasted_iota(jnp.int32, (256, HEADS), 1)
    ).astype(F32).astype(BF16)
    taller = dot(picker, scaled_weight.astype(BF16))
    taller = jnp.concatenate([taller, taller], 1)
    for each in range(8):
        weights[each * 256 : (each + 1) * 256, :] = jnp.where(
            lax.rem(row, 16) == 2 * each + lane // 128, taller, 0.0
        ).astype(BF16)
    mixed_ref[...] = jnp.zeros((32, 256), F32)

    def unload(block):
        slot = 0 if block == 2 else min(block, 2)
        return pltpu.make_async_copy(
            pairs.at[slot], grad_pair.at[pl.ds(block * 16, 16)], load_sem.at[block]
        )

    def pair_block(block):
        slot = 0 if block == 2 else min(block, 2)
        ours = pl.ds(block * 16, 16)
        dbias = own_bias[:, ours, :].reshape(256, 512).astype(F32)
        for part in range(4):
            wide_ref[part] = dbias[:, part * 128 : (part + 1) * 128]
        shrunk = dbias.reshape(HEADS, 16, 512) * inverse_ref[ours, :][None]
        turned_ref[...] = shrunk.reshape(256, 512).T.astype(BF16)

        def couple(index):
            left = jnp.concatenate(
                [
                    jnp.concatenate(
                        [wide_ref[part, pl.ds(2 * index + which, 16, stride=16), :] for part in range(4)], 1
                    )
                    for which in range(2)
                ],
                0,
            ).astype(BF16)
            mixed = mixed_ref[...]
            spread = weights[pl.ds(pl.multiple_of(index * 256, 256), 256), :]
            for part in range(4):
                rows = pl.ds(part * 128, 128)
                low = jnp.concatenate(
                    [pairs[slot, 2 * index, rows, :], pairs[slot, 2 * index + 1, rows, :]], 1
                )
                standard = low.astype(F32)
                scaled = dot(turned_ref[rows, :], spread)
                for which in range(2):
                    lanes = slice(which * 128, which * 128 + 128)
                    mine = standard[:, lanes]
                    along = jnp.sum(scaled[:, lanes] * mine, -1, keepdims=True) * (1.0 / 128)
                    pairs[slot, 2 * index + which, rows, :] = (scaled[:, lanes] - mine * along).astype(BF16)
                mixed = mixed + dot(left[:, part * 128 : (part + 1) * 128], low)
            mixed_ref[...] = mixed

        steps(8, couple)
        unload(block).start()

    wait_back(0)
    pair_block(0)
    pair_block(1)
    unload(0).wait()
    reload.start()
    wait_back(1)
    pair_block(3)
    reload.wait()
    pair_block(2)

    mine_ref[...] = mixed_ref[:16, :128] + mixed_ref[16:, 128:]

    def share(step):
        return remote(
            mine_ref, plane_parts.at[head], last_out.at[2, step], last_in.at[2, step],
            samp, half, lax.rem(head + step, HEADS),
        )

    steps(HEADS, lambda step: share(step).start(), 1)
    plane_parts[head] = mine_ref[...]

    for part in range(2):
        for which in range(1, 4):
            send_dq(which, part).wait()
    for block in range(8):
        pieces = []
        for which in range(2):
            total = qo[samp, 2 * block + which, :SIZE, :].astype(F32)
            for other in range(3):
                total = total + dq_parts[other, 2 * block + which].astype(F32)
            pieces.append(total)
        turned = jnp.concatenate(pieces + [filler], 0).T.astype(BF16)
        for each in range(4):
            dq_sum[block % 4 * 4 + each, block // 4 * 32 : block // 4 * 32 + 32, :] = turned[
                each * 32 : each * 32 + 32
            ]

    @pl.when(high == half)
    def _():
        keep_dkv.wait()

    @pl.when(high != half)
    def _():
        send_dkv(0).wait_send()

    for which in range(1, 4):
        send_dkv(which).wait_send()
    for piece in range(2):
        for side in range(2):
            source = 2 * half + piece

            @pl.when(jnp.logical_not((source == samp) & (half == side)))
            def _():
                pltpu.make_async_remote_copy(
                    src_ref=packed.at[pl.ds(0, 4)],
                    dst_ref=dkv_parts.at[piece, side],
                    send_sem=part_out.at[4],
                    recv_sem=part_in.at[4 + 2 * piece + side],
                    device_id=(source, side * HEADS + head),
                    device_id_type=MESH,
                ).wait_recv()

    for piece in range(2):
        for which in range(2):
            for block in range(4):
                spot = (2 * which + block // 2, slice(block % 2 * 96, block % 2 * 96 + 96))
                total = dkv_parts[piece, 0, spot[0], spot[1], :].astype(F32)
                total = total + dkv_parts[piece, 1, spot[0], spot[1], :].astype(F32)
                dkv_sum[piece * 4 + block, which] = total.astype(BF16)

    def last_dq(step):
        peer = lax.rem(head + step, HEADS)
        return remote(
            dq_sum.at[peer], own_dq.at[head], last_out.at[0, step], last_in.at[0, step], samp, half, peer
        )

    def last_dkv(step):
        peer = lax.rem(head + step, HEADS)
        return remote(
            dkv_sum.at[peer // 2], own_dkv.at[head], last_out.at[1, step], last_in.at[1, step], samp, half, peer
        )

    steps(HEADS, lambda step: last_dq(step).start(), 1)
    steps(HEADS, lambda step: last_dkv(step).start(), 1)
    keep_dq = pltpu.make_async_copy(dq_sum.at[head], own_dq.at[head], own_sem.at[10])
    keep_last = pltpu.make_async_copy(dkv_sum.at[head // 2], own_dkv.at[head], own_sem.at[11])
    keep_dq.start()
    keep_last.start()

    steps(HEADS, lambda step: share(step).wait(), 1)
    spot = samp * 2 + half
    group_parts[spot] = sum(plane_parts[other] for other in range(HEADS))

    def share_group(apart):
        return remote(
            group_parts.at[spot], group_parts.at[spot], share_out.at[apart], share_in.at[apart],
            lax.rem(samp + apart % 4, 4), half if apart < 4 else 1 - half, head,
        )

    for apart in range(1, 8):
        share_group(apart).start()

    for apart in range(1, 8):
        share_group(apart).wait()
    total = sum(group_parts[other] for other in range(8))
    gain_out[...] = jnp.sum(total * weight, 0, keepdims=True)
    weight_out[...] = total * gain_row
    keep_dq.wait()
    keep_last.wait()
    steps(HEADS, lambda step: last_dq(step).wait(), 1)
    steps(HEADS, lambda step: last_dkv(step).wait(), 1)
    for part in range(2):
        send_kv(part, 1).wait_send()

        @pl.when(samp != 2 * half + part)
        def _():
            send_kv(part, 0).wait_send()

    def sent(sample):
        for apart in range(1, 4):
            stat_copy(sample, apart).wait_send()

    steps(8, sent)
    for block in (1, 2, 3):
        unload(block).wait()


def deliver_kernel(
    pair_ref, dq_ref, dkv_ref, weight_ref, gain_ref, pair_out, q_out, k_out, v_out, weight_out, gain_out,
    held, load_sem, store_sem,
):
    def load(block):
        at = pl.ds(block * 8, 8)
        return pltpu.make_async_copy(pair_ref.at[at], held.at[at], load_sem.at[block])

    def store(block):
        at = pl.ds(block * 8, 8)
        return pltpu.make_async_copy(held.at[at], pair_out.at[at], store_sem.at[block])

    for block in range(8):
        load(block).start()
    weight_out[...] = weight_ref[...]
    gain_out[...] = gain_ref[...]
    odd = lax.rem(lax.axis_index("row"), 2) == 1
    for block in range(8):
        load(block).wait()
        store(block).start()
        which = block % 2
        if block // 2 == 0:
            pieces = [dq_ref[each, :, which * SIZE : which * SIZE + SIZE].astype(F32) for each in range(HEADS)]
            q_out[which] = jnp.concatenate(pieces, 1).astype(BF16)
        elif block // 2 < 3:
            out, rows = ((k_out, slice(0, SIZE)), (v_out, slice(SIZE, 2 * SIZE)))[block // 2 - 1]
            turned = dkv_ref[:, which, rows].reshape(HEADS * SIZE, 128).astype(F32).T
            out[which] = jnp.where(odd, turned[64:], turned[:64]).astype(BF16)
    for block in range(8):
        store(block).wait()


def on_device(queries, keys, values, out_grad, pair_repr, norm_gain, bias_weight, token_mask):
    flat = [array.reshape(128, 768) for array in (queries, out_grad, keys, values)]
    sems = pltpu.SemaphoreType.DMA
    outs = pl.pallas_call(
        kernel,
        out_shape=(
            shape((64, 512, 128)),
            shape((HEADS, 64, 128)),
            shape((HEADS, 2, 96, 128)),
            shape((HEADS, 128), F32),
            shape((1, 128), F32),
            shape((16, 512, 128)),
        ),
        in_specs=[WHOLE] * 4 + [ANY] + [WHOLE] * 3,
        out_specs=[ANY] * 3 + [WHOLE] * 2 + [ANY],
        scratch_shapes=[
            pltpu.VMEM((HEADS, 4 * SIZE, 128), BF16),
            pltpu.VMEM((4, HEADS, 96, 128), BF16),
            pltpu.VMEM((4, 8, 96, 128), BF16),
            pltpu.VMEM((HEADS, 96, 128), BF16),
            pltpu.VMEM((1024, 512), BF16),
            pltpu.VMEM((HEADS, 64, 512), BF16),
            pltpu.VMEM((3, 16, 512, 128), BF16),
            pltpu.VMEM((512, 128), F32),
            pltpu.VMEM((64, 512), F32),
            pltpu.VMEM((8, 512, 1024), F32),
            pltpu.VMEM((8, 512, 1024), F32),
            pltpu.VMEM((512, 1024), F32),
            pltpu.VMEM((8, 1024, 128), BF16),
            pltpu.VMEM((8, 128, 512), BF16),
            pltpu.VMEM((8, 512, 128), BF16),
            pltpu.VMEM((512, 128), BF16),
            pltpu.VMEM((512, 128), BF16),
            pltpu.VMEM((512, 2048), BF16),
            pltpu.VMEM((8, 8, 1024), F32),
            pltpu.VMEM((4, 8, 8, 1024), F32),
            pltpu.VMEM((3, HEADS, SIZE, 128), BF16),
            pltpu.VMEM((2, 2, 4, 192, 128), BF16),
            pltpu.VMEM((HEADS, 64, 512), BF16),
            pltpu.VMEM((2048, 256), BF16),
            pltpu.VMEM((512, 256), BF16),
            pltpu.VMEM((4, 256, 128), F32),
            pltpu.VMEM((32, 256), F32),
            pltpu.VMEM((256, 256), BF16),
            pltpu.VMEM((256, 256), BF16),
            pltpu.VMEM((512, 128), F32),
            pltpu.VMEM((HEADS, 64, 128), BF16),
            pltpu.VMEM((8, 2, 96, 128), BF16),
            pltpu.VMEM((HEADS, 128), F32),
            pltpu.VMEM((HEADS, HEADS, 128), F32),
            pltpu.VMEM((8, HEADS, 128), F32),
            sems((4,)),
            sems((2,)),
            sems((12,)),
            sems((2, 16)),
            sems((2, 16)),
            sems((4, 16)),
            sems((4, 16)),
            sems((8,)),
            sems((8,)),
            sems((8, 4)),
            sems((8, 4)),
            sems((2, 4)),
            sems((2, 4)),
            sems((8,)),
            sems((8,)),
            sems((2, 16)),
            sems((2, 16)),
            sems((3, 16)),
            sems((3, 16)),
            sems((8,)),
            sems((8,)),
        ],
        compiler_params=pltpu.CompilerParams(
            collective_id=0, has_side_effects=True, vmem_limit_bytes=63 * MIB
        ),
    )(*flat, pair_repr, norm_gain.reshape(1, 128), bias_weight.T, token_mask.reshape(1, 2048))
    near_pair, near_dq, near_dkv, near_weight, near_gain, _ = outs
    fixed = lambda *dims: pl.BlockSpec(dims, lambda i: (0,) * len(dims))
    grad_pair, grad_queries, grad_keys, grad_values, grad_weight, grad_gain = pl.pallas_call(
        deliver_kernel,
        grid=(1,),
        out_shape=(
            shape((64, 512, 128)),
            shape((2, 64, 768)),
            shape((2, 64, 768)),
            shape((2, 64, 768)),
            shape((HEADS, 128), F32),
            shape((1, 128), F32),
        ),
        in_specs=[
            ANY,
            fixed(HEADS, 64, 128),
            fixed(HEADS, 2, 96, 128),
            fixed(HEADS, 128),
            fixed(1, 128),
        ],
        out_specs=[ANY]
        + [fixed(2, 64, 768)] * 3
        + [fixed(HEADS, 128), fixed(1, 128)],
        scratch_shapes=[pltpu.VMEM((64, 512, 128), BF16), sems((8,)), sems((8,))],
        compiler_params=pltpu.CompilerParams(vmem_limit_bytes=60 * MIB),
    )(near_pair, near_dq, near_dkv, near_weight, near_gain)
    return grad_queries, grad_keys, grad_values, grad_pair, grad_weight.T, grad_gain.reshape(128)


def solution(mesh):
    tokens = P("samp", "row", None)
    pairs = P("row", "samp", None)
    return jax.shard_map(
        on_device,
        mesh=mesh,
        in_specs=(tokens, tokens, tokens, tokens, pairs, P(), P(), P()),
        out_specs=(tokens, tokens, tokens, pairs, P(), P()),
        check_vma=False,
    )
```

```python
import functools
import math

import jax
import jax.numpy as jnp
from jax import lax
from jax.experimental import pallas as pl
from jax.experimental.pallas import tpu as pltpu
from jax.sharding import PartitionSpec as P

MESH = pl.DeviceIdType.MESH
F32 = jnp.float32
BF16 = jnp.bfloat16
LOG2E = math.log2(math.e)
MASKED = -1e9 * LOG2E
HEADS = 16
SIZE = 48
ANY = pl.BlockSpec(memory_space=pl.ANY)
WHOLE = pl.BlockSpec(memory_space=pltpu.VMEM)
MIB = 1024 * 1024


def shape(dims, dtype=BF16):
    return jax.ShapeDtypeStruct(dims, dtype)


def place():
    samp, row = lax.axis_index("samp"), lax.axis_index("row")
    return samp, row // HEADS, lax.rem(row, HEADS)


def remote(src, dst, send, recv, samp, half, head):
    return pltpu.make_async_remote_copy(
        src_ref=src,
        dst_ref=dst,
        send_sem=send,
        recv_sem=recv,
        device_id=(samp, half * HEADS + head),
        device_id_type=MESH,
    )


def dot(left, right):
    return jnp.dot(left, right, preferred_element_type=F32)


def untangle(first, second):
    first, second = first.astype(F32), second.astype(F32)
    low = lax.broadcasted_iota(jnp.int32, first.shape, 1) < 64
    return (
        jnp.where(low, first, pltpu.roll(second, 64, 1)),
        jnp.where(low, pltpu.roll(first, 64, 1), second),
    )


def steps(count, body, start=0, unroll=1):
    def wrapped(index, _):
        body(index)
        return 0

    lax.fori_loop(start, count, wrapped, 0, unroll=unroll)


def kernel(
    q_ref, o_ref, k_ref, v_ref, pair_ref, gain_ref, weight_ref, mask_ref,
    grad_pair, own_dq, own_dkv, weight_out, gain_out, spilled,
    packed, qo, kv, kv_near, all_bias, bias, pairs, inverse_wide, inverse_ref,
    raised_ref, along_ref, bias_t, qo_rows, kv_t, kv_rows, kept_ref, vals_ref,
    low_ref, tops, stats, dq_parts, dkv_parts, own_bias, weights, turned_ref, wide_ref, mixed_ref,
    centre_ref, mean_ref, keep_ref, dq_sum, dkv_sum, mine_ref, plane_parts, group_parts,
    load_sem, store_sem, own_sem, plane_out, plane_in, bias_out, bias_in, group_out, group_in,
    stat_out, stat_in, dq_out, dq_in, part_out, part_in, back_out, back_in, last_out, last_in, share_out, share_in,
):
    samp, half, head = place()
    core, high = lax.rem(samp, 2), samp // 2
    kin = (samp, high * 2 + 1 - core, (1 - high) * 2 + core, (1 - high) * 2 + 1 - core)
    inv_root = 1.0 / math.sqrt(SIZE)

    barrier = pltpu.get_barrier_semaphore()

    def hello(step):
        peer = lax.rem(head + step, HEADS)
        pl.semaphore_signal(barrier, inc=1, device_id=(samp, half * HEADS + peer), device_id_type=MESH)

    steps(HEADS, hello, 1)
    for apart in range(1, 8):
        side = half if apart < 4 else 1 - half
        pl.semaphore_signal(
            barrier, inc=1, device_id=(lax.rem(samp + apart, 4), side * HEADS + head), device_id_type=MESH
        )

    def load(block):
        return pltpu.make_async_copy(
            pair_ref.at[pl.ds(block * 16, 16)], pairs.at[min(block, 2)], load_sem.at[block]
        )

    spill = pltpu.make_async_copy(pairs.at[2], spilled, store_sem.at[0])
    reload = pltpu.make_async_copy(spilled, pairs.at[0], store_sem.at[1])

    for block in range(3):
        load(block).start()
    for part, ref in enumerate((k_ref, v_ref, q_ref, o_ref)):
        turned = ref[...].T
        for each in range(HEADS):
            packed[each, part * SIZE : (part + 1) * SIZE, :] = turned[each * SIZE : (each + 1) * SIZE]
    pl.semaphore_wait(barrier, 22)

    def copy_pack(step, which):
        peer = lax.rem(head + step, HEADS)
        land = qo.at[samp] if which else kv_near
        return remote(
            packed.at[peer, pl.ds(which * 96, 96)], land.at[head],
            plane_out.at[which, step], plane_in.at[which, step], samp, half, peer,
        )

    for which in range(2):
        steps(HEADS, lambda step: copy_pack(step, which).start(), 1)
    own_kv = pltpu.make_async_copy(packed.at[head, pl.ds(0, 96)], kv_near.at[head], own_sem.at[0])
    own_qo = pltpu.make_async_copy(packed.at[head, pl.ds(96, 96)], qo.at[samp, head], own_sem.at[1])
    own_kv.start()
    own_qo.start()

    row = lax.broadcasted_iota(jnp.int32, (256, 256), 0)
    lane = lax.broadcasted_iota(jnp.int32, (256, 256), 1)
    averager = jnp.where(row // 128 == lane // 128, 1.0 / 128, 0.0)
    mean_ref[...] = averager.astype(BF16)
    centre_ref[...] = (jnp.where(row == lane, 1.0, 0.0) - averager).astype(BF16)
    gain_row = gain_ref[...]
    gain = jnp.concatenate([gain_row, gain_row], 1)
    weight = weight_ref[...].astype(F32)
    chooser = (
        lax.broadcasted_iota(jnp.int32, (HEADS, 256), 1) // 16 == lax.broadcasted_iota(jnp.int32, (HEADS, 256), 0)
    ).astype(F32).astype(BF16)
    wider = dot(weight.T.astype(BF16), chooser)
    lane_in = lax.rem(lax.broadcasted_iota(jnp.int32, (128, 256), 1), 16)
    for each in range(16):
        weights[each * 128 : (each + 1) * 128, :] = jnp.where(lane_in == each, wider, 0.0).astype(BF16)
    for part in range(4):
        at = pl.ds(pl.multiple_of(samp * 512 + part * 128, 128), 128)
        kept = (mask_ref[0:1, at] > 0).astype(F32)
        keep_ref[part * 128 : (part + 1) * 128, :] = jnp.broadcast_to(kept, (128, 128)).T

    narrow = lax.broadcasted_iota(jnp.int32, (128, 128), 1)

    def norm_block(block):
        slot = min(block, 2)
        load(block).wait()

        def couple(index):
            lanes = pl.ds(pl.multiple_of(index * 256, 256), 256)
            for part in range(4):
                rows = pl.ds(part * 128, 128)
                both = jnp.concatenate(
                    [pairs[slot, 2 * index, rows, :], pairs[slot, 2 * index + 1, rows, :]], 1
                )
                centred = dot(both, centre_ref[...])
                variance = dot((centred * centred).astype(BF16), mean_ref[...])
                inverse = lax.rsqrt(variance + 1e-05)
                standard = centred * inverse
                low = standard.astype(BF16)
                pairs[slot, 2 * index, rows, :] = low[:, :128]
                pairs[slot, 2 * index + 1, rows, :] = low[:, 128:]
                low_ref[rows, lanes] = (standard * gain).astype(BF16)
                old = jnp.where(narrow == 2 * index, inverse[:, :128], inverse_wide[rows, :])
                inverse_wide[rows, :] = jnp.where(narrow == 2 * index + 1, inverse[:, 128:], old)

        steps(8, couple, unroll=4)
        if block == 2:
            spill.start()
        rows = pl.ds(block * 16, 16)
        bias[:, rows, :] = dot(low_ref[...], weights[...]).T.reshape(HEADS, 16, 512).astype(BF16)
        inverse_ref[rows, :] = inverse_wide[...].T[:16]

    def bias_rows(block):
        return pl.ds(pl.multiple_of(block // 2 * 512 + head * 32 + block % 2 * 16, 16), 16)

    def copy_bias(block, step):
        return remote(
            bias.at[lax.rem(head + step, HEADS), pl.ds(block * 16, 16)], all_bias.at[bias_rows(block)],
            bias_out.at[block, step], bias_in.at[block, step], samp, half, lax.rem(head + step, HEADS),
        )

    def keep_bias(block):
        return pltpu.make_async_copy(
            bias.at[head, pl.ds(block * 16, 16)], all_bias.at[bias_rows(block)], own_sem.at[2 + block]
        )

    def start_bias(block):
        steps(HEADS, lambda step: copy_bias(block, step).start(), 1)
        keep_bias(block).start()

    def send_kv(part, across):
        return remote(
            kv_near.at[pl.ds(part * 8, 8)], kv.at[samp],
            group_out.at[4 + part * 2 + across], group_in.at[4 + samp],
            2 * half + part, 1 - half if across else half, head,
        )

    def keep_kv(part):
        return pltpu.make_async_copy(kv_near.at[pl.ds(part * 8, 8)], kv.at[samp], own_sem.at[6])

    def wait_kv(owner):
        here = jnp.logical_and(owner == samp, high == half)

        @pl.when(here)
        def _():
            pltpu.make_async_copy(kv_near.at[pl.ds(0, 8)], kv.at[owner], own_sem.at[6]).wait()

        @pl.when(jnp.logical_not(here))
        def _():
            pltpu.make_async_remote_copy(
                src_ref=kv_near.at[pl.ds(0, 8)],
                dst_ref=kv.at[owner],
                send_sem=group_out.at[4],
                recv_sem=group_in.at[4 + owner],
                device_id=(owner, high * HEADS + head),
                device_id_type=MESH,
            ).wait_recv()

    def send_qo(which):
        slot = kin[2] if which == 3 else samp
        to = kin[1] if which == 3 else kin[which]
        return remote(qo.at[slot], qo.at[slot], group_out.at[which], group_in.at[which], to, half, head)

    def wait_qo(which):
        slot = kin[which]
        remote(
            qo.at[slot], qo.at[slot], group_out.at[which], group_in.at[which],
            kin[1] if which == 3 else kin[which], half, head,
        ).wait_recv()

    norm_block(0)
    start_bias(0)
    steps(HEADS, lambda step: copy_pack(step, 0).wait(), 1)
    own_kv.wait()
    for part in range(2):
        send_kv(part, 1).start()
        mine = samp == 2 * half + part

        @pl.when(mine)
        def _():
            keep_kv(part).start()

        @pl.when(jnp.logical_not(mine))
        def _():
            send_kv(part, 0).start()

    norm_block(1)
    start_bias(1)
    steps(HEADS, lambda step: copy_pack(step, 1).wait(), 1)
    own_qo.wait()
    send_qo(2).start()
    send_qo(1).start()
    norm_block(2)
    start_bias(2)
    spill.wait()
    load(3).start()

    filler = jnp.zeros((32, 128), F32)

    def unpack_qo(owner):
        def body(peer):
            filled = jnp.concatenate([qo[owner, peer].astype(F32), filler], 0).T.astype(BF16)
            for which in range(2):
                for part in range(2):
                    at = pl.ds(pl.multiple_of(part * 512 + peer * 32, 32), 32)
                    start = which * 64 + part * 32
                    qo_rows[2 * owner + which, at, :] = filled[start : start + 32]

        steps(HEADS, body, unroll=2)

    def unpack_kv(owner):
        def body(pair):
            at = pl.ds(pl.multiple_of(pair * 128, 128), 128)
            both = untangle(kv[owner, 2 * pair], kv[owner, 2 * pair + 1])
            for which in range(2):
                filled = jnp.concatenate([both[which], filler], 0)
                kv_t[2 * owner + which, :, at] = filled.astype(BF16)
                kv_rows[2 * owner + which, at, :] = filled.T.astype(BF16)

        steps(4, body, unroll=2)

    unpack_qo(samp)
    norm_block(3)
    start_bias(3)
    wait_qo(2)
    send_qo(3).start()
    wait_kv(samp)
    unpack_kv(samp)

    def turn_bias(part):
        for block in (2 * part, 2 * part + 1):
            keep_bias(block).wait()
            steps(HEADS, lambda step: copy_bias(block, step).wait(), 1)

        def body(block):
            at = pl.ds(pl.multiple_of(part * 512 + block * 128, 128), 128)
            turned = all_bias[at, :].astype(F32).T * LOG2E
            bias_t[:, at] = jnp.where(keep_ref[...] > 0, turned, MASKED)

        steps(4, body)

    def stat_copy(sample, apart):
        return remote(
            stats.at[samp, sample], stats.at[samp, sample],
            stat_out.at[sample, apart], stat_in.at[sample, apart],
            lax.rem(samp + apart, 4), half, head,
        )

    wide = lax.broadcasted_iota(jnp.int32, (512, 128), 1)

    def first_pass(sample, block):
        both = kv_rows[sample]
        kept_ref[...] = jnp.where((wide < SIZE) & (keep_ref[...] > 0), both, 0).astype(BF16)
        vals_ref[...] = jnp.where(wide >= SIZE, both, 0).astype(BF16)
        at = pl.ds(pl.multiple_of(block * 512, 512), 512)
        right = qo_rows[sample, at, :].T
        partial = []
        for part in range(4):
            rows = pl.ds(part * 128, 128)
            score = dot(kept_ref[rows, :], right)
            along = dot(vals_ref[rows, :], right)
            score = score * (inv_root * LOG2E) + bias_t[rows, at]
            top = jnp.max(score, 0, keepdims=True)
            raised = jnp.exp2(score - top)
            raised_ref[sample, rows, at] = raised
            along_ref[sample, rows, at] = along
            tops[sample, part : part + 1, at] = top
            partial.append((top, jnp.sum(raised, 0, keepdims=True), jnp.sum(raised * along, 0, keepdims=True)))
        peak = functools.reduce(jnp.maximum, [p[0] for p in partial])
        scale = [jnp.exp2(p[0] - peak) for p in partial]
        stats[samp, sample, 0:1, at] = peak
        stats[samp, sample, 1:2, at] = sum(p[1] * w for p, w in zip(partial, scale))
        stats[samp, sample, 2:3, at] = sum(p[2] * w for p, w in zip(partial, scale))

    stats[samp] = jnp.zeros((8, 8, 1024), F32)
    def send_stats(owner):
        for index in range(2):
            for apart in range(1, 4):
                stat_copy(2 * owner + index, apart).start()

    turn_bias(0)
    steps(2, lambda index: first_pass(2 * samp + index, 0))
    wait_qo(1)
    wait_kv(kin[1])
    unpack_qo(kin[1])
    unpack_kv(kin[1])
    steps(2, lambda index: first_pass(2 * kin[1] + index, 0))
    turn_bias(1)
    steps(2, lambda index: first_pass(2 * samp + index, 1))
    send_stats(samp)
    steps(2, lambda index: first_pass(2 * kin[1] + index, 1))
    send_stats(kin[1])
    for which in range(2, 4):
        if which == 3:
            wait_qo(3)
        wait_kv(kin[which])
        unpack_qo(kin[which])
        unpack_kv(kin[which])
        steps(4, lambda index: first_pass(2 * kin[which] + index // 2, lax.rem(index, 2)))
        send_stats(kin[which])

    for which in range(1, 4):
        send_qo(which).wait_send()
    bias_t[...] = jnp.zeros((512, 1024), F32)

    def kin_of(which):
        across, over = lax.rem(which, 2), which // 2
        return (high + over - 2 * high * over) * 2 + core + across - 2 * core * across

    def second_pass(owner, block):
        both = [None, None]
        for piece in range(2):
            start = block * 512 + piece * 256
            at = slice(start, start + 256)
            scales = []
            for index in range(2):
                sample = 2 * owner + index
                peaks = [stats[other, sample, 0:1, at] for other in range(4)]
                peak = functools.reduce(jnp.maximum, peaks)
                scale = [jnp.exp2(p - peak) for p in peaks]
                total = sum(stats[other, sample, 1:2, at] * scale[other] for other in range(4))
                blend = sum(stats[other, sample, 2:3, at] * scale[other] for other in range(4))
                share = 1.0 / total
                scales.append((peak, share, blend * share))
            for part in range(4):
                rows = pl.ds(part * 128, 128)
                grads = []
                for index in range(2):
                    sample = 2 * owner + index
                    peak, share, mean = scales[index]
                    factor = jnp.exp2(tops[sample, part : part + 1, at] - peak) * share
                    probs = raised_ref[sample, rows, at] * factor
                    grad = probs * (along_ref[sample, rows, at] - mean)
                    grads.append(grad)
                    spot = index * 1024 + piece * 256
                    low_ref[rows, spot : spot + 256] = probs.astype(BF16)
                    low_ref[rows, spot + 512 : spot + 768] = grad.astype(BF16)
                bias_t[rows, at] += grads[0] + grads[1]
            for index in range(2):
                sample = 2 * owner + index
                spot = index * 1024 + piece * 256
                right = qo_rows[sample, at, :]
                dv = dot(low_ref[:, spot : spot + 256], right)
                dk = dot(low_ref[:, spot + 512 : spot + 768], right)
                here = jnp.where(wide < SIZE, dk * inv_root, dv)
                both[index] = here if piece == 0 else both[index] + here
                dq = (dot(kv_t[sample, :SIZE, :], low_ref[:, spot + 512 : spot + 768]) * inv_root).astype(BF16)
                for side in range(2):
                    qo[owner, 2 * (block * 4 + piece * 2 + side) + index, :SIZE, :] = dq[
                        :, side * 128 : side * 128 + 128
                    ]
        for index in range(2):
            sample = 2 * owner + index
            if block == 0:
                raised_ref[sample, :, 0:128] = both[index]
            else:
                turned = (both[index] + raised_ref[sample, :, 0:128]).T
                for piece in range(4):
                    packed[2 * sample + piece // 2, piece % 2 * 96 : piece % 2 * 96 + 96, :] = turned[
                        :96, piece * 128 : piece * 128 + 128
                    ].astype(BF16)

    def send_dq(which, part):
        some = pl.ds(part * 8, 8)
        return remote(
            qo.at[kin_of(which), some, pl.ds(0, SIZE)], dq_parts.at[which - 1, some],
            dq_out.at[part, which], dq_in.at[part, which], kin_of(which), half, head,
        )

    def send_dkv(which):
        return remote(
            packed.at[pl.ds(4 * kin_of(which), 4)], dkv_parts.at[core, half],
            part_out.at[4 + which], part_in.at[4 + 2 * core + half], kin_of(which), high, head,
        )

    keep_dkv = pltpu.make_async_copy(packed.at[pl.ds(4 * samp, 4)], dkv_parts.at[core, half], own_sem.at[7])

    def send_back(peer, part):
        at = pl.ds(pl.multiple_of(part * 512 + peer * 32, 32), 32)
        return remote(
            all_bias.at[at], own_bias.at[head, pl.ds(part * 32, 32)],
            back_out.at[part, peer], back_in.at[part, head], samp, half, peer,
        )

    def keep_back(part):
        at = pl.ds(pl.multiple_of(part * 512 + head * 32, 32), 32)
        return pltpu.make_async_copy(
            all_bias.at[at], own_bias.at[head, pl.ds(part * 32, 32)], own_sem.at[8 + part]
        )

    def turn_back(part):
        def body(step):
            block = lax.rem(head // 4 + step, 4)
            at = pl.ds(pl.multiple_of(part * 512 + block * 128, 128), 128)
            all_bias[at, :] = bias_t[:, at].T.astype(BF16)

            def send(index):
                peer = 4 * block + lax.rem(head + index, 4)

                @pl.when(peer == head)
                def _():
                    keep_back(part).start()

                @pl.when(peer != head)
                def _():
                    send_back(peer, part).start()

            steps(4, send)

        steps(4, body)

    def wait_back(part):
        keep_back(part).wait()

        def body(step):
            other = lax.rem(head + step, HEADS)
            at = pl.ds(pl.multiple_of(part * 512 + other * 32, 32), 32)
            remote(
                all_bias.at[at], own_bias.at[other, pl.ds(part * 32, 32)],
                back_out.at[part, other], back_in.at[part, other], samp, half, other,
            ).wait()

        steps(HEADS, body, 1)

    for part in range(2):
        def pair_body(step):
            which = lax.rem(step + 1, 4) if part == 0 else 3 - step
            owner = kin_of(which)
            if part == 0:
                for index in range(2):
                    for apart in range(1, 4):
                        stat_copy(2 * owner + index, apart).wait_recv()
            second_pass(owner, part)

            @pl.when(which > 0)
            def _():
                if part == 1:
                    send_dkv(which).start()
                send_dq(which, part).start()

        steps(4, pair_body)
        turn_back(part)

    @pl.when(high == half)
    def _():
        keep_dkv.start()

    @pl.when(high != half)
    def _():
        send_dkv(0).start()

    scaled_weight = weight * gain_row
    scaled_weight = scaled_weight - jnp.mean(scaled_weight, -1, keepdims=True)
    picker = (
        lax.broadcasted_iota(jnp.int32, (256, HEADS), 0) // 16 == lax.broadcasted_iota(jnp.int32, (256, HEADS), 1)
    ).astype(F32).astype(BF16)
    taller = dot(picker, scaled_weight.astype(BF16))
    taller = jnp.concatenate([taller, taller], 1)
    for each in range(8):
        weights[each * 256 : (each + 1) * 256, :] = jnp.where(
            lax.rem(row, 16) == 2 * each + lane // 128, taller, 0.0
        ).astype(BF16)
    mixed_ref[...] = jnp.zeros((32, 256), F32)

    def unload(block):
        slot = 0 if block == 2 else min(block, 2)
        return pltpu.make_async_copy(
            pairs.at[slot], grad_pair.at[pl.ds(block * 16, 16)], load_sem.at[block]
        )

    def pair_block(block):
        slot = 0 if block == 2 else min(block, 2)
        ours = pl.ds(block * 16, 16)
        dbias = own_bias[:, ours, :].reshape(256, 512).astype(F32)
        for part in range(4):
            wide_ref[part] = dbias[:, part * 128 : (part + 1) * 128]
        shrunk = dbias.reshape(HEADS, 16, 512) * inverse_ref[ours, :][None]
        turned_ref[...] = shrunk.reshape(256, 512).T.astype(BF16)

        def couple(index):
            left = jnp.concatenate(
                [
                    jnp.concatenate(
                        [wide_ref[part, pl.ds(2 * index + which, 16, stride=16), :] for part in range(4)], 1
                    )
                    for which in range(2)
                ],
                0,
            ).astype(BF16)
            mixed = mixed_ref[...]
            spread = weights[pl.ds(pl.multiple_of(index * 256, 256), 256), :]
            for part in range(4):
                rows = pl.ds(part * 128, 128)
                low = jnp.concatenate(
                    [pairs[slot, 2 * index, rows, :], pairs[slot, 2 * index + 1, rows, :]], 1
                )
                standard = low.astype(F32)
                scaled = dot(turned_ref[rows, :], spread)
                for which in range(2):
                    lanes = slice(which * 128, which * 128 + 128)
                    mine = standard[:, lanes]
                    along = jnp.sum(scaled[:, lanes] * mine, -1, keepdims=True) * (1.0 / 128)
                    pairs[slot, 2 * index + which, rows, :] = (scaled[:, lanes] - mine * along).astype(BF16)
                mixed = mixed + dot(left[:, part * 128 : (part + 1) * 128], low)
            mixed_ref[...] = mixed

        steps(8, couple, unroll=2)
        unload(block).start()

    def last_dq(part, step):
        peer = lax.rem(head + step, HEADS)
        some = pl.ds(part * 32, 32)
        return remote(
            dq_sum.at[peer, some], own_dq.at[head, some],
            last_out.at[part, step], last_in.at[part, step], samp, half, peer,
        )

    def keep_dq(part):
        some = pl.ds(part * 32, 32)
        return pltpu.make_async_copy(dq_sum.at[head, some], own_dq.at[head, some], own_sem.at[10 + part])

    def sum_dq(part):
        for which in range(1, 4):
            send_dq(which, part).wait()
        for block in range(4):
            pieces = []
            for which in range(2):
                spot = part * 8 + 2 * block + which
                total = qo[samp, spot, :SIZE, :].astype(F32)
                for other in range(3):
                    total = total + dq_parts[other, spot].astype(F32)
                pieces.append(total)
            turned = jnp.concatenate(pieces + [filler], 0).T.astype(BF16)
            for each in range(4):
                dq_sum[block * 4 + each, part * 32 : part * 32 + 32, :] = turned[each * 32 : each * 32 + 32]
        steps(HEADS, lambda step: last_dq(part, step).start(), 1)
        keep_dq(part).start()

    wait_back(0)
    pair_block(0)
    sum_dq(0)
    pair_block(1)
    unload(0).wait()
    reload.start()
    wait_back(1)
    pair_block(3)
    reload.wait()
    pair_block(2)

    mine_ref[...] = mixed_ref[:16, :128] + mixed_ref[16:, 128:]

    def share(step):
        return remote(
            mine_ref, plane_parts.at[head], last_out.at[3, step], last_in.at[3, step],
            samp, half, lax.rem(head + step, HEADS),
        )

    steps(HEADS, lambda step: share(step).start(), 1)
    plane_parts[head] = mine_ref[...]

    @pl.when(high == half)
    def _():
        keep_dkv.wait()

    @pl.when(high != half)
    def _():
        send_dkv(0).wait_send()

    for which in range(1, 4):
        send_dkv(which).wait_send()
    for piece in range(2):
        for side in range(2):
            source = 2 * half + piece

            @pl.when(jnp.logical_not((source == samp) & (half == side)))
            def _():
                pltpu.make_async_remote_copy(
                    src_ref=packed.at[pl.ds(0, 4)],
                    dst_ref=dkv_parts.at[piece, side],
                    send_sem=part_out.at[4],
                    recv_sem=part_in.at[4 + 2 * piece + side],
                    device_id=(source, side * HEADS + head),
                    device_id_type=MESH,
                ).wait_recv()

    for piece in range(2):
        for which in range(2):
            for block in range(4):
                spot = (2 * which + block // 2, slice(block % 2 * 96, block % 2 * 96 + 96))
                total = dkv_parts[piece, 0, spot[0], spot[1], :].astype(F32)
                total = total + dkv_parts[piece, 1, spot[0], spot[1], :].astype(F32)
                dkv_sum[piece * 4 + block, which] = total.astype(BF16)

    def last_dkv(step):
        peer = lax.rem(head + step, HEADS)
        return remote(
            dkv_sum.at[peer // 2], own_dkv.at[head], last_out.at[2, step], last_in.at[2, step], samp, half, peer
        )

    steps(HEADS, lambda step: last_dkv(step).start(), 1)
    keep_last = pltpu.make_async_copy(dkv_sum.at[head // 2], own_dkv.at[head], own_sem.at[12])
    keep_last.start()
    sum_dq(1)

    steps(HEADS, lambda step: share(step).wait(), 1)
    spot = samp * 2 + half
    group_parts[spot] = sum(plane_parts[other] for other in range(HEADS))

    def share_group(apart):
        return remote(
            group_parts.at[spot], group_parts.at[spot], share_out.at[apart], share_in.at[apart],
            lax.rem(samp + apart % 4, 4), half if apart < 4 else 1 - half, head,
        )

    for apart in range(1, 8):
        share_group(apart).start()

    for apart in range(1, 8):
        share_group(apart).wait()
    total = sum(group_parts[other] for other in range(8))
    gain_out[...] = jnp.sum(total * weight, 0, keepdims=True)
    weight_out[...] = total * gain_row
    keep_last.wait()
    for part in range(2):
        keep_dq(part).wait()
        steps(HEADS, lambda step: last_dq(part, step).wait(), 1)
    steps(HEADS, lambda step: last_dkv(step).wait(), 1)
    for part in range(2):
        send_kv(part, 1).wait_send()

        @pl.when(samp != 2 * half + part)
        def _():
            send_kv(part, 0).wait_send()

    def sent(sample):
        for apart in range(1, 4):
            stat_copy(sample, apart).wait_send()

    steps(8, sent)
    for block in (1, 2, 3):
        unload(block).wait()


def deliver_kernel(
    pair_ref, dq_ref, dkv_ref, weight_ref, gain_ref, pair_out, q_out, k_out, v_out, weight_out, gain_out,
    held, load_sem, store_sem,
):
    def load(block):
        at = pl.ds(block * 8, 8)
        return pltpu.make_async_copy(pair_ref.at[at], held.at[at], load_sem.at[block])

    def store(block):
        at = pl.ds(block * 8, 8)
        return pltpu.make_async_copy(held.at[at], pair_out.at[at], store_sem.at[block])

    for block in range(8):
        load(block).start()
    weight_out[...] = weight_ref[...]
    gain_out[...] = gain_ref[...]
    odd = lax.rem(lax.axis_index("row"), 2) == 1
    for block in range(8):
        load(block).wait()
        store(block).start()
        which = block % 2
        if block // 2 == 0:
            pieces = [dq_ref[each, :, which * SIZE : which * SIZE + SIZE].astype(F32) for each in range(HEADS)]
            q_out[which] = jnp.concatenate(pieces, 1).astype(BF16)
        elif block // 2 < 3:
            out, rows = ((k_out, slice(0, SIZE)), (v_out, slice(SIZE, 2 * SIZE)))[block // 2 - 1]
            turned = dkv_ref[:, which, rows].reshape(HEADS * SIZE, 128).astype(F32).T
            out[which] = jnp.where(odd, turned[64:], turned[:64]).astype(BF16)
    for block in range(8):
        store(block).wait()


def on_device(queries, keys, values, out_grad, pair_repr, norm_gain, bias_weight, token_mask):
    flat = [array.reshape(128, 768) for array in (queries, out_grad, keys, values)]
    sems = pltpu.SemaphoreType.DMA
    outs = pl.pallas_call(
        kernel,
        out_shape=(
            shape((64, 512, 128)),
            shape((HEADS, 64, 128)),
            shape((HEADS, 2, 96, 128)),
            shape((HEADS, 128), F32),
            shape((1, 128), F32),
            shape((16, 512, 128)),
        ),
        in_specs=[WHOLE] * 4 + [ANY] + [WHOLE] * 3,
        out_specs=[ANY] * 3 + [WHOLE] * 2 + [ANY],
        scratch_shapes=[
            pltpu.VMEM((HEADS, 4 * SIZE, 128), BF16),
            pltpu.VMEM((4, HEADS, 96, 128), BF16),
            pltpu.VMEM((4, 8, 96, 128), BF16),
            pltpu.VMEM((HEADS, 96, 128), BF16),
            pltpu.VMEM((1024, 512), BF16),
            pltpu.VMEM((HEADS, 64, 512), BF16),
            pltpu.VMEM((3, 16, 512, 128), BF16),
            pltpu.VMEM((512, 128), F32),
            pltpu.VMEM((64, 512), F32),
            pltpu.VMEM((8, 512, 1024), F32),
            pltpu.VMEM((8, 512, 1024), F32),
            pltpu.VMEM((512, 1024), F32),
            pltpu.VMEM((8, 1024, 128), BF16),
            pltpu.VMEM((8, 128, 512), BF16),
            pltpu.VMEM((8, 512, 128), BF16),
            pltpu.VMEM((512, 128), BF16),
            pltpu.VMEM((512, 128), BF16),
            pltpu.VMEM((512, 2048), BF16),
            pltpu.VMEM((8, 8, 1024), F32),
            pltpu.VMEM((4, 8, 8, 1024), F32),
            pltpu.VMEM((3, HEADS, SIZE, 128), BF16),
            pltpu.VMEM((2, 2, 4, 192, 128), BF16),
            pltpu.VMEM((HEADS, 64, 512), BF16),
            pltpu.VMEM((2048, 256), BF16),
            pltpu.VMEM((512, 256), BF16),
            pltpu.VMEM((4, 256, 128), F32),
            pltpu.VMEM((32, 256), F32),
            pltpu.VMEM((256, 256), BF16),
            pltpu.VMEM((256, 256), BF16),
            pltpu.VMEM((512, 128), F32),
            pltpu.VMEM((HEADS, 64, 128), BF16),
            pltpu.VMEM((8, 2, 96, 128), BF16),
            pltpu.VMEM((HEADS, 128), F32),
            pltpu.VMEM((HEADS, HEADS, 128), F32),
            pltpu.VMEM((8, HEADS, 128), F32),
            sems((4,)),
            sems((2,)),
            sems((13,)),
            sems((2, 16)),
            sems((2, 16)),
            sems((4, 16)),
            sems((4, 16)),
            sems((8,)),
            sems((8,)),
            sems((8, 4)),
            sems((8, 4)),
            sems((2, 4)),
            sems((2, 4)),
            sems((8,)),
            sems((8,)),
            sems((2, 16)),
            sems((2, 16)),
            sems((4, 16)),
            sems((4, 16)),
            sems((8,)),
            sems((8,)),
        ],
        compiler_params=pltpu.CompilerParams(
            collective_id=0, has_side_effects=True, vmem_limit_bytes=63 * MIB
        ),
    )(*flat, pair_repr, norm_gain.reshape(1, 128), bias_weight.T, token_mask.reshape(1, 2048))
    near_pair, near_dq, near_dkv, near_weight, near_gain, _ = outs
    fixed = lambda *dims: pl.BlockSpec(dims, lambda i: (0,) * len(dims))
    grad_pair, grad_queries, grad_keys, grad_values, grad_weight, grad_gain = pl.pallas_call(
        deliver_kernel,
        grid=(1,),
        out_shape=(
            shape((64, 512, 128)),
            shape((2, 64, 768)),
            shape((2, 64, 768)),
            shape((2, 64, 768)),
            shape((HEADS, 128), F32),
            shape((1, 128), F32),
        ),
        in_specs=[
            ANY,
            fixed(HEADS, 64, 128),
            fixed(HEADS, 2, 96, 128),
            fixed(HEADS, 128),
            fixed(1, 128),
        ],
        out_specs=[ANY]
        + [fixed(2, 64, 768)] * 3
        + [fixed(HEADS, 128), fixed(1, 128)],
        scratch_shapes=[pltpu.VMEM((64, 512, 128), BF16), sems((8,)), sems((8,))],
        compiler_params=pltpu.CompilerParams(vmem_limit_bytes=60 * MIB),
    )(near_pair, near_dq, near_dkv, near_weight, near_gain)
    return grad_queries, grad_keys, grad_values, grad_pair, grad_weight.T, grad_gain.reshape(128)


def solution(mesh):
    tokens = P("samp", "row", None)
    pairs = P("row", "samp", None)
    return jax.shard_map(
        on_device,
        mesh=mesh,
        in_specs=(tokens, tokens, tokens, tokens, pairs, P(), P(), P()),
        out_specs=(tokens, tokens, tokens, pairs, P(), P()),
        check_vma=False,
    )
```

```python
import functools
import math

import jax
import jax.numpy as jnp
from jax import lax
from jax.experimental import pallas as pl
from jax.experimental.pallas import tpu as pltpu
from jax.sharding import PartitionSpec as P

MESH = pl.DeviceIdType.MESH
F32 = jnp.float32
BF16 = jnp.bfloat16
LOG2E = math.log2(math.e)
MASKED = -1e9 * LOG2E
HEADS = 16
SIZE = 48
ANY = pl.BlockSpec(memory_space=pl.ANY)
WHOLE = pl.BlockSpec(memory_space=pltpu.VMEM)
MIB = 1024 * 1024


def shape(dims, dtype=BF16):
    return jax.ShapeDtypeStruct(dims, dtype)


def place():
    samp, row = lax.axis_index("samp"), lax.axis_index("row")
    return samp, row // HEADS, lax.rem(row, HEADS)


def remote(src, dst, send, recv, samp, half, head):
    return pltpu.make_async_remote_copy(
        src_ref=src,
        dst_ref=dst,
        send_sem=send,
        recv_sem=recv,
        device_id=(samp, half * HEADS + head),
        device_id_type=MESH,
    )


def dot(left, right):
    return jnp.dot(left, right, preferred_element_type=F32)


def untangle(first, second):
    first, second = first.astype(F32), second.astype(F32)
    low = lax.broadcasted_iota(jnp.int32, first.shape, 1) < 64
    return (
        jnp.where(low, first, pltpu.roll(second, 64, 1)),
        jnp.where(low, pltpu.roll(first, 64, 1), second),
    )


def steps(count, body, start=0, unroll=1):
    def wrapped(index, _):
        body(index)
        return 0

    lax.fori_loop(start, count, wrapped, 0, unroll=unroll)


def kernel(
    q_ref, o_ref, k_ref, v_ref, pair_ref, gain_ref, weight_ref, mask_ref,
    grad_pair, own_dq, own_dkv, weight_out, gain_out, spilled,
    packed, qo, kv, kv_near, all_bias, bias, pairs, inverse_wide, inverse_ref,
    raised_ref, along_ref, bias_t, qo_rows, kv_t, kv_rows, kept_ref, vals_ref,
    low_ref, tops, stats, dq_parts, dkv_parts, own_bias, weights, turned_ref, wide_ref, mixed_ref,
    centre_ref, mean_ref, keep_ref, dq_sum, dkv_sum, mine_ref, plane_parts, group_parts,
    load_sem, store_sem, own_sem, plane_out, plane_in, bias_out, bias_in, group_out, group_in,
    stat_out, stat_in, dq_out, dq_in, part_out, part_in, back_out, back_in, last_out, last_in, share_out, share_in,
):
    samp, half, head = place()
    core, high = lax.rem(samp, 2), samp // 2
    kin = (samp, high * 2 + 1 - core, (1 - high) * 2 + core, (1 - high) * 2 + 1 - core)
    inv_root = 1.0 / math.sqrt(SIZE)

    barrier = pltpu.get_barrier_semaphore()

    def hello(step):
        peer = lax.rem(head + step, HEADS)
        pl.semaphore_signal(barrier, inc=1, device_id=(samp, half * HEADS + peer), device_id_type=MESH)

    steps(HEADS, hello, 1)
    for apart in range(1, 8):
        side = half if apart < 4 else 1 - half
        pl.semaphore_signal(
            barrier, inc=1, device_id=(lax.rem(samp + apart, 4), side * HEADS + head), device_id_type=MESH
        )

    def load(block):
        return pltpu.make_async_copy(
            pair_ref.at[pl.ds(block * 16, 16)], pairs.at[min(block, 2)], load_sem.at[block]
        )

    spill = pltpu.make_async_copy(pairs.at[2], spilled, store_sem.at[0])
    reload = pltpu.make_async_copy(spilled, pairs.at[0], store_sem.at[1])

    for block in range(3):
        load(block).start()
    for part, ref in enumerate((k_ref, v_ref, q_ref, o_ref)):
        turned = ref[...].T
        for each in range(HEADS):
            packed[each, part * SIZE : (part + 1) * SIZE, :] = turned[each * SIZE : (each + 1) * SIZE]
    pl.semaphore_wait(barrier, 22)

    def copy_pack(step, which):
        peer = lax.rem(head + step, HEADS)
        land = qo.at[samp] if which else kv_near
        return remote(
            packed.at[peer, pl.ds(which * 96, 96)], land.at[head],
            plane_out.at[which, step], plane_in.at[which, step], samp, half, peer,
        )

    for which in range(2):
        steps(HEADS, lambda step: copy_pack(step, which).start(), 1)
    own_kv = pltpu.make_async_copy(packed.at[head, pl.ds(0, 96)], kv_near.at[head], own_sem.at[0])
    own_qo = pltpu.make_async_copy(packed.at[head, pl.ds(96, 96)], qo.at[samp, head], own_sem.at[1])
    own_kv.start()
    own_qo.start()

    row = lax.broadcasted_iota(jnp.int32, (256, 256), 0)
    lane = lax.broadcasted_iota(jnp.int32, (256, 256), 1)
    averager = jnp.where(row // 128 == lane // 128, 1.0 / 128, 0.0)
    mean_ref[...] = averager.astype(BF16)
    centre_ref[...] = (jnp.where(row == lane, 1.0, 0.0) - averager).astype(BF16)
    gain_row = gain_ref[...]
    gain = jnp.concatenate([gain_row, gain_row], 1)
    weight = weight_ref[...].astype(F32)
    chooser = (
        lax.broadcasted_iota(jnp.int32, (HEADS, 256), 1) // 16 == lax.broadcasted_iota(jnp.int32, (HEADS, 256), 0)
    ).astype(F32).astype(BF16)
    wider = dot(weight.T.astype(BF16), chooser)
    lane_in = lax.rem(lax.broadcasted_iota(jnp.int32, (128, 256), 1), 16)
    for each in range(16):
        weights[each * 128 : (each + 1) * 128, :] = jnp.where(lane_in == each, wider, 0.0).astype(BF16)
    for part in range(4):
        at = pl.ds(pl.multiple_of(samp * 512 + part * 128, 128), 128)
        kept = (mask_ref[0:1, at] > 0).astype(F32)
        keep_ref[part * 128 : (part + 1) * 128, :] = jnp.broadcast_to(kept, (128, 128)).T

    narrow = lax.broadcasted_iota(jnp.int32, (128, 128), 1)

    def norm_block(block):
        slot = min(block, 2)
        load(block).wait()

        def couple(index):
            lanes = pl.ds(pl.multiple_of(index * 256, 256), 256)
            for part in range(4):
                rows = pl.ds(part * 128, 128)
                both = jnp.concatenate(
                    [pairs[slot, 2 * index, rows, :], pairs[slot, 2 * index + 1, rows, :]], 1
                )
                centred = dot(both, centre_ref[...])
                variance = dot((centred * centred).astype(BF16), mean_ref[...])
                inverse = lax.rsqrt(variance + 1e-05)
                standard = centred * inverse
                low = standard.astype(BF16)
                pairs[slot, 2 * index, rows, :] = low[:, :128]
                pairs[slot, 2 * index + 1, rows, :] = low[:, 128:]
                low_ref[rows, lanes] = (standard * gain).astype(BF16)
                old = jnp.where(narrow == 2 * index, inverse[:, :128], inverse_wide[rows, :])
                inverse_wide[rows, :] = jnp.where(narrow == 2 * index + 1, inverse[:, 128:], old)

        steps(8, couple, unroll=4)
        if block == 2:
            spill.start()
        rows = pl.ds(block * 16, 16)
        bias[:, rows, :] = dot(low_ref[...], weights[...]).T.reshape(HEADS, 16, 512).astype(BF16)
        inverse_ref[rows, :] = inverse_wide[...].T[:16]

    def bias_rows(part):
        return pl.ds(pl.multiple_of(part * 512 + head * 32, 32), 32)

    def copy_bias(part, step):
        return remote(
            bias.at[lax.rem(head + step, HEADS), pl.ds(part * 32, 32)], all_bias.at[bias_rows(part)],
            bias_out.at[part, step], bias_in.at[part, step], samp, half, lax.rem(head + step, HEADS),
        )

    def keep_bias(part):
        return pltpu.make_async_copy(
            bias.at[head, pl.ds(part * 32, 32)], all_bias.at[bias_rows(part)], own_sem.at[2 + part]
        )

    def start_bias(part):
        steps(HEADS, lambda step: copy_bias(part, step).start(), 1)
        keep_bias(part).start()

    def send_kv(part, across):
        return remote(
            kv_near.at[pl.ds(part * 8, 8)], kv.at[samp],
            group_out.at[4 + part * 2 + across], group_in.at[4 + samp],
            2 * half + part, 1 - half if across else half, head,
        )

    def keep_kv(part):
        return pltpu.make_async_copy(kv_near.at[pl.ds(part * 8, 8)], kv.at[samp], own_sem.at[6])

    def wait_kv(owner):
        here = jnp.logical_and(owner == samp, high == half)

        @pl.when(here)
        def _():
            pltpu.make_async_copy(kv_near.at[pl.ds(0, 8)], kv.at[owner], own_sem.at[6]).wait()

        @pl.when(jnp.logical_not(here))
        def _():
            pltpu.make_async_remote_copy(
                src_ref=kv_near.at[pl.ds(0, 8)],
                dst_ref=kv.at[owner],
                send_sem=group_out.at[4],
                recv_sem=group_in.at[4 + owner],
                device_id=(owner, high * HEADS + head),
                device_id_type=MESH,
            ).wait_recv()

    def send_qo(which):
        slot = kin[2] if which == 3 else samp
        to = kin[1] if which == 3 else kin[which]
        return remote(qo.at[slot], qo.at[slot], group_out.at[which], group_in.at[which], to, half, head)

    def wait_qo(which):
        slot = kin[which]
        remote(
            qo.at[slot], qo.at[slot], group_out.at[which], group_in.at[which],
            kin[1] if which == 3 else kin[which], half, head,
        ).wait_recv()

    norm_block(0)
    steps(HEADS, lambda step: copy_pack(step, 0).wait(), 1)
    own_kv.wait()
    for part in range(2):
        send_kv(part, 1).start()
        mine = samp == 2 * half + part

        @pl.when(mine)
        def _():
            keep_kv(part).start()

        @pl.when(jnp.logical_not(mine))
        def _():
            send_kv(part, 0).start()

    norm_block(1)
    start_bias(0)
    steps(HEADS, lambda step: copy_pack(step, 1).wait(), 1)
    own_qo.wait()
    send_qo(2).start()
    send_qo(1).start()
    norm_block(2)
    spill.wait()
    load(3).start()

    filler = jnp.zeros((32, 128), F32)

    def unpack_qo(owner):
        def body(peer):
            filled = jnp.concatenate([qo[owner, peer].astype(F32), filler], 0).T.astype(BF16)
            for which in range(2):
                for part in range(2):
                    at = pl.ds(pl.multiple_of(part * 512 + peer * 32, 32), 32)
                    start = which * 64 + part * 32
                    qo_rows[2 * owner + which, at, :] = filled[start : start + 32]

        steps(HEADS, body, unroll=8)

    def unpack_kv(owner):
        def body(pair):
            at = pl.ds(pl.multiple_of(pair * 128, 128), 128)
            both = untangle(kv[owner, 2 * pair], kv[owner, 2 * pair + 1])
            for which in range(2):
                filled = jnp.concatenate([both[which], filler], 0)
                kv_t[2 * owner + which, :, at] = filled.astype(BF16)
                kv_rows[2 * owner + which, at, :] = filled.T.astype(BF16)

        steps(4, body, unroll=4)

    unpack_qo(samp)
    norm_block(3)
    start_bias(1)
    wait_qo(2)
    send_qo(3).start()
    wait_kv(samp)
    unpack_kv(samp)

    def turn_bias(part):
        keep_bias(part).wait()
        steps(HEADS, lambda step: copy_bias(part, step).wait(), 1)

        def body(block):
            at = pl.ds(pl.multiple_of(part * 512 + block * 128, 128), 128)
            turned = all_bias[at, :].astype(F32).T * LOG2E
            bias_t[:, at] = jnp.where(keep_ref[...] > 0, turned, MASKED)

        steps(4, body, unroll=4)

    def stat_copy(sample, apart):
        return remote(
            stats.at[samp, sample], stats.at[samp, sample],
            stat_out.at[sample, apart], stat_in.at[sample, apart],
            lax.rem(samp + apart, 4), half, head,
        )

    wide = lax.broadcasted_iota(jnp.int32, (512, 128), 1)

    def first_pass(sample, block):
        both = kv_rows[sample]
        kept_ref[...] = jnp.where((wide < SIZE) & (keep_ref[...] > 0), both, 0).astype(BF16)
        vals_ref[...] = jnp.where(wide >= SIZE, both, 0).astype(BF16)
        at = pl.ds(pl.multiple_of(block * 512, 512), 512)
        right = qo_rows[sample, at, :].T
        partial = []
        for part in range(4):
            rows = pl.ds(part * 128, 128)
            score = dot(kept_ref[rows, :], right)
            along = dot(vals_ref[rows, :], right)
            score = score * (inv_root * LOG2E) + bias_t[rows, at]
            top = jnp.max(score, 0, keepdims=True)
            raised = jnp.exp2(score - top)
            raised_ref[sample, rows, at] = raised
            along_ref[sample, rows, at] = along
            tops[sample, part : part + 1, at] = top
            partial.append((top, jnp.sum(raised, 0, keepdims=True), jnp.sum(raised * along, 0, keepdims=True)))
        peak = functools.reduce(jnp.maximum, [p[0] for p in partial])
        scale = [jnp.exp2(p[0] - peak) for p in partial]
        stats[samp, sample, 0:1, at] = peak
        stats[samp, sample, 1:2, at] = sum(p[1] * w for p, w in zip(partial, scale))
        stats[samp, sample, 2:3, at] = sum(p[2] * w for p, w in zip(partial, scale))

    stats[samp] = jnp.zeros((8, 8, 1024), F32)
    def send_stats(owner):
        for index in range(2):
            for apart in range(1, 4):
                stat_copy(2 * owner + index, apart).start()

    turn_bias(0)
    steps(2, lambda index: first_pass(2 * samp + index, 0))
    wait_qo(1)
    wait_kv(kin[1])
    unpack_qo(kin[1])
    unpack_kv(kin[1])
    steps(2, lambda index: first_pass(2 * kin[1] + index, 0))
    turn_bias(1)
    steps(2, lambda index: first_pass(2 * samp + index, 1))
    send_stats(samp)
    steps(2, lambda index: first_pass(2 * kin[1] + index, 1))
    send_stats(kin[1])
    for which in range(2, 4):
        if which == 3:
            wait_qo(3)
        wait_kv(kin[which])
        unpack_qo(kin[which])
        unpack_kv(kin[which])
        steps(4, lambda index: first_pass(2 * kin[which] + index // 2, lax.rem(index, 2)))
        send_stats(kin[which])

    for which in range(1, 4):
        send_qo(which).wait_send()
    bias_t[...] = jnp.zeros((512, 1024), F32)

    def kin_of(which):
        across, over = lax.rem(which, 2), which // 2
        return (high + over - 2 * high * over) * 2 + core + across - 2 * core * across

    def second_pass(owner, block):
        both = [None, None]
        for piece in range(2):
            start = block * 512 + piece * 256
            at = slice(start, start + 256)
            scales = []
            for index in range(2):
                sample = 2 * owner + index
                peaks = [stats[other, sample, 0:1, at] for other in range(4)]
                peak = functools.reduce(jnp.maximum, peaks)
                scale = [jnp.exp2(p - peak) for p in peaks]
                total = sum(stats[other, sample, 1:2, at] * scale[other] for other in range(4))
                blend = sum(stats[other, sample, 2:3, at] * scale[other] for other in range(4))
                share = 1.0 / total
                scales.append((peak, share, blend * share))
            for part in range(4):
                rows = pl.ds(part * 128, 128)
                grads = []
                for index in range(2):
                    sample = 2 * owner + index
                    peak, share, mean = scales[index]
                    factor = jnp.exp2(tops[sample, part : part + 1, at] - peak) * share
                    probs = raised_ref[sample, rows, at] * factor
                    grad = probs * (along_ref[sample, rows, at] - mean)
                    grads.append(grad)
                    spot = index * 1024 + piece * 256
                    low_ref[rows, spot : spot + 256] = probs.astype(BF16)
                    low_ref[rows, spot + 512 : spot + 768] = grad.astype(BF16)
                bias_t[rows, at] += grads[0] + grads[1]
            for index in range(2):
                sample = 2 * owner + index
                spot = index * 1024 + piece * 256
                right = qo_rows[sample, at, :]
                dv = dot(low_ref[:, spot : spot + 256], right)
                dk = dot(low_ref[:, spot + 512 : spot + 768], right)
                here = jnp.where(wide < SIZE, dk * inv_root, dv)
                both[index] = here if piece == 0 else both[index] + here
                dq = (dot(kv_t[sample, :SIZE, :], low_ref[:, spot + 512 : spot + 768]) * inv_root).astype(BF16)
                for side in range(2):
                    qo[owner, 2 * (block * 4 + piece * 2 + side) + index, :SIZE, :] = dq[
                        :, side * 128 : side * 128 + 128
                    ]
        for index in range(2):
            sample = 2 * owner + index
            if block == 0:
                raised_ref[sample, :, 0:128] = both[index]
            else:
                turned = (both[index] + raised_ref[sample, :, 0:128]).T
                for piece in range(4):
                    packed[2 * sample + piece // 2, piece % 2 * 96 : piece % 2 * 96 + 96, :] = turned[
                        :96, piece * 128 : piece * 128 + 128
                    ].astype(BF16)

    def send_dq(which, part):
        some = pl.ds(part * 8, 8)
        return remote(
            qo.at[kin[which], some, pl.ds(0, SIZE)], dq_parts.at[which - 1, some],
            dq_out.at[part, which], dq_in.at[part, which], kin[2 if which == 2 else 1], half, head,
        )

    def merge_dq(part):
        send_dq(3, part).wait_recv()
        for spot in range(part * 8, part * 8 + 8):
            total = qo[kin[2], spot, :SIZE, :].astype(F32) + dq_parts[2, spot].astype(F32)
            qo[kin[2], spot, :SIZE, :] = total.astype(BF16)
        send_dq(2, part).start()

    def send_dkv(which):
        return remote(
            packed.at[pl.ds(4 * kin_of(which), 4)], dkv_parts.at[core, half],
            part_out.at[4 + which], part_in.at[4 + 2 * core + half], kin_of(which), high, head,
        )

    keep_dkv = pltpu.make_async_copy(packed.at[pl.ds(4 * samp, 4)], dkv_parts.at[core, half], own_sem.at[7])

    def send_back(peer, part):
        at = pl.ds(pl.multiple_of(part * 512 + peer * 32, 32), 32)
        return remote(
            all_bias.at[at], own_bias.at[head, pl.ds(part * 32, 32)],
            back_out.at[part, peer], back_in.at[part, head], samp, half, peer,
        )

    def keep_back(part):
        at = pl.ds(pl.multiple_of(part * 512 + head * 32, 32), 32)
        return pltpu.make_async_copy(
            all_bias.at[at], own_bias.at[head, pl.ds(part * 32, 32)], own_sem.at[8 + part]
        )

    def turn_back(part):
        def body(step):
            block = lax.rem(head // 4 + step, 4)
            at = pl.ds(pl.multiple_of(part * 512 + block * 128, 128), 128)
            all_bias[at, :] = bias_t[:, at].T.astype(BF16)

            def send(index):
                peer = 4 * block + lax.rem(head + index, 4)

                @pl.when(peer == head)
                def _():
                    keep_back(part).start()

                @pl.when(peer != head)
                def _():
                    send_back(peer, part).start()

            steps(4, send)

        steps(4, body)

    def wait_back(part):
        keep_back(part).wait()

        def body(step):
            other = lax.rem(head + step, HEADS)
            at = pl.ds(pl.multiple_of(part * 512 + other * 32, 32), 32)
            remote(
                all_bias.at[at], own_bias.at[other, pl.ds(part * 32, 32)],
                back_out.at[part, other], back_in.at[part, other], samp, half, other,
            ).wait()

        steps(HEADS, body, 1)

    for part in range(2):
        def pair_body(step):
            which = lax.rem(step + 1, 4) if part == 0 else 3 - step
            owner = kin_of(which)
            if part == 0:
                for index in range(2):
                    for apart in range(1, 4):
                        stat_copy(2 * owner + index, apart).wait_recv()
            second_pass(owner, part)

            for side in (1, 3):
                @pl.when(which == side)
                def _():
                    send_dq(side, part).start()

            if part == 1:
                @pl.when(which > 0)
                def _():
                    send_dkv(which).start()

            @pl.when(step == 3 - part)
            def _():
                merge_dq(part)

        steps(4, pair_body)
        turn_back(part)

    @pl.when(high == half)
    def _():
        keep_dkv.start()

    @pl.when(high != half)
    def _():
        send_dkv(0).start()

    scaled_weight = weight * gain_row
    scaled_weight = scaled_weight - jnp.mean(scaled_weight, -1, keepdims=True)
    picker = (
        lax.broadcasted_iota(jnp.int32, (256, HEADS), 0) // 16 == lax.broadcasted_iota(jnp.int32, (256, HEADS), 1)
    ).astype(F32).astype(BF16)
    taller = dot(picker, scaled_weight.astype(BF16))
    taller = jnp.concatenate([taller, taller], 1)
    for each in range(8):
        weights[each * 256 : (each + 1) * 256, :] = jnp.where(
            lax.rem(row, 16) == 2 * each + lane // 128, taller, 0.0
        ).astype(BF16)
    mixed_ref[...] = jnp.zeros((32, 256), F32)

    def unload(block):
        slot = 0 if block == 2 else min(block, 2)
        return pltpu.make_async_copy(
            pairs.at[slot], grad_pair.at[pl.ds(block * 16, 16)], load_sem.at[block]
        )

    def pair_block(block):
        slot = 0 if block == 2 else min(block, 2)
        ours = pl.ds(block * 16, 16)
        dbias = own_bias[:, ours, :].reshape(256, 512).astype(F32)
        for part in range(4):
            wide_ref[part] = dbias[:, part * 128 : (part + 1) * 128]
        shrunk = dbias.reshape(HEADS, 16, 512) * inverse_ref[ours, :][None]
        turned_ref[...] = shrunk.reshape(256, 512).T.astype(BF16)

        def couple(index):
            left = jnp.concatenate(
                [
                    jnp.concatenate(
                        [wide_ref[part, pl.ds(2 * index + which, 16, stride=16), :] for part in range(4)], 1
                    )
                    for which in range(2)
                ],
                0,
            ).astype(BF16)
            mixed = mixed_ref[...]
            spread = weights[pl.ds(pl.multiple_of(index * 256, 256), 256), :]
            for part in range(4):
                rows = pl.ds(part * 128, 128)
                low = jnp.concatenate(
                    [pairs[slot, 2 * index, rows, :], pairs[slot, 2 * index + 1, rows, :]], 1
                )
                standard = low.astype(F32)
                scaled = dot(turned_ref[rows, :], spread)
                for which in range(2):
                    lanes = slice(which * 128, which * 128 + 128)
                    mine = standard[:, lanes]
                    along = jnp.sum(scaled[:, lanes] * mine, -1, keepdims=True) * (1.0 / 128)
                    pairs[slot, 2 * index + which, rows, :] = (scaled[:, lanes] - mine * along).astype(BF16)
                mixed = mixed + dot(left[:, part * 128 : (part + 1) * 128], low)
            mixed_ref[...] = mixed

        steps(8, couple, unroll=2)
        unload(block).start()

    def last_dq(part, step):
        peer = lax.rem(head + step, HEADS)
        some = pl.ds(part * 32, 32)
        return remote(
            dq_sum.at[peer, some], own_dq.at[head, some],
            last_out.at[part, step], last_in.at[part, step], samp, half, peer,
        )

    def keep_dq(part):
        some = pl.ds(part * 32, 32)
        return pltpu.make_async_copy(dq_sum.at[head, some], own_dq.at[head, some], own_sem.at[10 + part])

    def sum_dq(part):
        for which in range(1, 3):
            send_dq(which, part).wait()
        send_dq(3, part).wait_send()
        for block in range(4):
            pieces = []
            for which in range(2):
                spot = part * 8 + 2 * block + which
                total = qo[samp, spot, :SIZE, :].astype(F32)
                for other in range(2):
                    total = total + dq_parts[other, spot].astype(F32)
                pieces.append(total)
            turned = jnp.concatenate(pieces + [filler], 0).T.astype(BF16)
            for each in range(4):
                dq_sum[block * 4 + each, part * 32 : part * 32 + 32, :] = turned[each * 32 : each * 32 + 32]
        steps(HEADS, lambda step: last_dq(part, step).start(), 1)
        keep_dq(part).start()

    wait_back(0)
    pair_block(0)
    sum_dq(0)
    pair_block(1)
    unload(0).wait()
    reload.start()
    wait_back(1)
    pair_block(3)
    reload.wait()
    pair_block(2)

    mine_ref[...] = mixed_ref[:16, :128] + mixed_ref[16:, 128:]

    def share(step):
        return remote(
            mine_ref, plane_parts.at[head], last_out.at[3, step], last_in.at[3, step],
            samp, half, lax.rem(head + step, HEADS),
        )

    steps(HEADS, lambda step: share(step).start(), 1)
    plane_parts[head] = mine_ref[...]

    @pl.when(high == half)
    def _():
        keep_dkv.wait()

    @pl.when(high != half)
    def _():
        send_dkv(0).wait_send()

    for which in range(1, 4):
        send_dkv(which).wait_send()
    for piece in range(2):
        for side in range(2):
            source = 2 * half + piece

            @pl.when(jnp.logical_not((source == samp) & (half == side)))
            def _():
                pltpu.make_async_remote_copy(
                    src_ref=packed.at[pl.ds(0, 4)],
                    dst_ref=dkv_parts.at[piece, side],
                    send_sem=part_out.at[4],
                    recv_sem=part_in.at[4 + 2 * piece + side],
                    device_id=(source, side * HEADS + head),
                    device_id_type=MESH,
                ).wait_recv()

    for piece in range(2):
        for which in range(2):
            for block in range(4):
                spot = (2 * which + block // 2, slice(block % 2 * 96, block % 2 * 96 + 96))
                total = dkv_parts[piece, 0, spot[0], spot[1], :].astype(F32)
                total = total + dkv_parts[piece, 1, spot[0], spot[1], :].astype(F32)
                dkv_sum[piece * 4 + block, which] = total.astype(BF16)

    def last_dkv(step):
        peer = lax.rem(head + step, HEADS)
        return remote(
            dkv_sum.at[peer // 2], own_dkv.at[head], last_out.at[2, step], last_in.at[2, step], samp, half, peer
        )

    steps(HEADS, lambda step: last_dkv(step).start(), 1)
    keep_last = pltpu.make_async_copy(dkv_sum.at[head // 2], own_dkv.at[head], own_sem.at[12])
    keep_last.start()
    sum_dq(1)

    steps(HEADS, lambda step: share(step).wait(), 1)
    spot = samp * 2 + half
    group_parts[spot] = sum(plane_parts[other] for other in range(HEADS))

    def share_group(apart):
        return remote(
            group_parts.at[spot], group_parts.at[spot], share_out.at[apart], share_in.at[apart],
            lax.rem(samp + apart % 4, 4), half if apart < 4 else 1 - half, head,
        )

    for apart in range(1, 8):
        share_group(apart).start()

    for apart in range(1, 8):
        share_group(apart).wait()
    total = sum(group_parts[other] for other in range(8))
    gain_out[...] = jnp.sum(total * weight, 0, keepdims=True)
    weight_out[...] = total * gain_row
    keep_last.wait()
    for part in range(2):
        keep_dq(part).wait()
        steps(HEADS, lambda step: last_dq(part, step).wait(), 1)
    steps(HEADS, lambda step: last_dkv(step).wait(), 1)
    for part in range(2):
        send_kv(part, 1).wait_send()

        @pl.when(samp != 2 * half + part)
        def _():
            send_kv(part, 0).wait_send()

    def sent(sample):
        for apart in range(1, 4):
            stat_copy(sample, apart).wait_send()

    steps(8, sent)
    for block in (1, 2, 3):
        unload(block).wait()


def deliver_kernel(
    pair_ref, near_dq, near_dkv, weight_ref, gain_ref, pair_out, q_out, k_out, v_out, weight_out, gain_out,
    held, dq_ref, dkv_ref, load_sem, store_sem, token_sem,
):
    def load(block):
        at = pl.ds(block * 8, 8)
        return pltpu.make_async_copy(pair_ref.at[at], held.at[at], load_sem.at[block])

    def store(block):
        at = pl.ds(block * 8, 8)
        return pltpu.make_async_copy(held.at[at], pair_out.at[at], store_sem.at[block])

    load_dq = pltpu.make_async_copy(near_dq, dq_ref, token_sem.at[0])
    load_dkv = pltpu.make_async_copy(near_dkv, dkv_ref, token_sem.at[1])
    load(0).start()
    load_dq.start()
    load_dkv.start()
    for block in range(1, 8):
        load(block).start()
    weight_out[...] = weight_ref[...]
    gain_out[...] = gain_ref[...]
    odd = lax.rem(lax.axis_index("row"), 2) == 1
    for block in range(8):
        load(block).wait()
        store(block).start()
        which = block % 2
        if block == 0:
            load_dq.wait()
        if block == 2:
            load_dkv.wait()
        if block // 2 == 0:
            pieces = [dq_ref[each, :, which * SIZE : which * SIZE + SIZE].astype(F32) for each in range(HEADS)]
            q_out[which] = jnp.concatenate(pieces, 1).astype(BF16)
        elif block // 2 < 3:
            out, rows = ((k_out, slice(0, SIZE)), (v_out, slice(SIZE, 2 * SIZE)))[block // 2 - 1]
            turned = dkv_ref[:, which, rows].reshape(HEADS * SIZE, 128).astype(F32).T
            out[which] = jnp.where(odd, turned[64:], turned[:64]).astype(BF16)
    for block in range(8):
        store(block).wait()


def on_device(queries, keys, values, out_grad, pair_repr, norm_gain, bias_weight, token_mask):
    flat = [array.reshape(128, 768) for array in (queries, out_grad, keys, values)]
    sems = pltpu.SemaphoreType.DMA
    outs = pl.pallas_call(
        kernel,
        out_shape=(
            shape((64, 512, 128)),
            shape((HEADS, 64, 128)),
            shape((HEADS, 2, 96, 128)),
            shape((HEADS, 128), F32),
            shape((1, 128), F32),
            shape((16, 512, 128)),
        ),
        in_specs=[WHOLE] * 4 + [ANY] + [WHOLE] * 3,
        out_specs=[ANY] * 3 + [WHOLE] * 2 + [ANY],
        scratch_shapes=[
            pltpu.VMEM((HEADS, 4 * SIZE, 128), BF16),
            pltpu.VMEM((4, HEADS, 96, 128), BF16),
            pltpu.VMEM((4, 8, 96, 128), BF16),
            pltpu.VMEM((HEADS, 96, 128), BF16),
            pltpu.VMEM((1024, 512), BF16),
            pltpu.VMEM((HEADS, 64, 512), BF16),
            pltpu.VMEM((3, 16, 512, 128), BF16),
            pltpu.VMEM((512, 128), F32),
            pltpu.VMEM((64, 512), F32),
            pltpu.VMEM((8, 512, 1024), F32),
            pltpu.VMEM((8, 512, 1024), F32),
            pltpu.VMEM((512, 1024), F32),
            pltpu.VMEM((8, 1024, 128), BF16),
            pltpu.VMEM((8, 128, 512), BF16),
            pltpu.VMEM((8, 512, 128), BF16),
            pltpu.VMEM((512, 128), BF16),
            pltpu.VMEM((512, 128), BF16),
            pltpu.VMEM((512, 2048), BF16),
            pltpu.VMEM((8, 8, 1024), F32),
            pltpu.VMEM((4, 8, 8, 1024), F32),
            pltpu.VMEM((3, HEADS, SIZE, 128), BF16),
            pltpu.VMEM((2, 2, 4, 192, 128), BF16),
            pltpu.VMEM((HEADS, 64, 512), BF16),
            pltpu.VMEM((2048, 256), BF16),
            pltpu.VMEM((512, 256), BF16),
            pltpu.VMEM((4, 256, 128), F32),
            pltpu.VMEM((32, 256), F32),
            pltpu.VMEM((256, 256), BF16),
            pltpu.VMEM((256, 256), BF16),
            pltpu.VMEM((512, 128), F32),
            pltpu.VMEM((HEADS, 64, 128), BF16),
            pltpu.VMEM((8, 2, 96, 128), BF16),
            pltpu.VMEM((HEADS, 128), F32),
            pltpu.VMEM((HEADS, HEADS, 128), F32),
            pltpu.VMEM((8, HEADS, 128), F32),
            sems((4,)),
            sems((2,)),
            sems((13,)),
            sems((2, 16)),
            sems((2, 16)),
            sems((2, 16)),
            sems((2, 16)),
            sems((8,)),
            sems((8,)),
            sems((8, 4)),
            sems((8, 4)),
            sems((2, 4)),
            sems((2, 4)),
            sems((8,)),
            sems((8,)),
            sems((2, 16)),
            sems((2, 16)),
            sems((4, 16)),
            sems((4, 16)),
            sems((8,)),
            sems((8,)),
        ],
        compiler_params=pltpu.CompilerParams(
            collective_id=0, has_side_effects=True, vmem_limit_bytes=63 * MIB
        ),
    )(*flat, pair_repr, norm_gain.reshape(1, 128), bias_weight.T, token_mask.reshape(1, 2048))
    near_pair, near_dq, near_dkv, near_weight, near_gain, _ = outs
    fixed = lambda *dims: pl.BlockSpec(dims, lambda i: (0,) * len(dims))
    grad_pair, grad_queries, grad_keys, grad_values, grad_weight, grad_gain = pl.pallas_call(
        deliver_kernel,
        grid=(1,),
        out_shape=(
            shape((64, 512, 128)),
            shape((2, 64, 768)),
            shape((2, 64, 768)),
            shape((2, 64, 768)),
            shape((HEADS, 128), F32),
            shape((1, 128), F32),
        ),
        in_specs=[
            ANY,
            ANY,
            ANY,
            fixed(HEADS, 128),
            fixed(1, 128),
        ],
        out_specs=[ANY]
        + [fixed(2, 64, 768)] * 3
        + [fixed(HEADS, 128), fixed(1, 128)],
        scratch_shapes=[
            pltpu.VMEM((64, 512, 128), BF16),
            pltpu.VMEM((HEADS, 64, 128), BF16),
            pltpu.VMEM((HEADS, 2, 96, 128), BF16),
            sems((8,)),
            sems((8,)),
            sems((2,)),
        ],
        compiler_params=pltpu.CompilerParams(vmem_limit_bytes=60 * MIB),
    )(near_pair, near_dq, near_dkv, near_weight, near_gain)
    return grad_queries, grad_keys, grad_values, grad_pair, grad_weight.T, grad_gain.reshape(128)


def solution(mesh):
    tokens = P("samp", "row", None)
    pairs = P("row", "samp", None)
    return jax.shard_map(
        on_device,
        mesh=mesh,
        in_specs=(tokens, tokens, tokens, tokens, pairs, P(), P(), P()),
        out_specs=(tokens, tokens, tokens, pairs, P(), P()),
        check_vma=False,
    )
```
